32 devices in a mesh: dp: 2 (over y), ctx: 16 (over z, x, core).
Axes of the slice: x: 2, y: 2, z: 4, core: 2. Of those that a mesh axis runs over, the one named last changes fastest.
Arguments:
- events: bfloat16 [2, 4096, 1024], P('dp', 'ctx'), may hold values from -6 to 6
- w_query: bfloat16 [1024, 512], replicated, may hold values from -0.1875 to 0.1875
- w_key: bfloat16 [1024, 512], replicated, may hold values from -0.1875 to 0.1875
- values: bfloat16 [2, 4096, 512], P('dp', 'ctx'), may hold values from -6 to 6
- grad_out: bfloat16 [2, 4096, 512], P('dp', 'ctx'), may hold values from -6 to 6
- lengths: int32 [2, 8], P('dp'), may hold values from 1 to 768, 4096 in all within a row
- stream_shift: int32 [2], P('dp'), may hold values from 0 to 4095
- block_keep: int32 [2, 32], P('dp'), may hold values 0 or 1
Outputs:
- attended: bfloat16 [2, 4096, 512], P('dp', 'ctx')
- grad_values: bfloat16 [2, 4096, 512], P('dp', 'ctx')
- grad_wq: bfloat16 [1024, 512], P('ctx')
- grad_wk: bfloat16 [1024, 512], P('ctx')
The draws below stay inside these ranges and needn't reach their ends.
Inputs may be any that keep to these rules, and one draw needn't show every extreme that they name: The lengths of a stream sum to 4096; the longest is exactly 768.
All inputs are finite; a program needn't handle non-finite values. No bound on the sum of `block_keep` on one device may be relied on, other than what follows from the above.
Results may differ from the reference program's by a relative error of at most 0.011.
Values may be sent and summed in bfloat16 or wider, within the bound.
No kernel may reach another device: no remote copies, remote signals or barrier semaphores. Data moves between devices by JAX's collectives and lax.ppermute only.
A program may use at most 64 MiB of HBM per device.

```python
import math
import jax
import jax.numpy as jnp
import numpy as np
from jax import lax

D = 1024
HEADS = 4
HD = 128
ROWS_DEV = 256
SPAN = 3
BLOCK = 128
STREAMS = 2
L = 4096
USERS = 8
MAXLEN = 768
NBLK = 32


def touch_ends(result, key, low, high):
    extent = result.shape
    index_at = [jax.random.randint(jax.random.fold_in(key, axis), (), 0, extent[axis]) for axis in range(len(extent))]
    result = result.at[tuple(index_at)].set(low)
    longest = extent.index(max(extent))
    index_at[longest] = (index_at[longest] + 1) % extent[longest]
    return result.at[tuple(index_at)].set(high)


def levels(key, extent, cuts, smallest, top_value):
    def one(dim, blocks):
        draws = jax.random.uniform(jax.random.fold_in(jax.random.fold_in(key, 6), dim), (blocks,), jnp.float32, smallest / len(cuts), top_value / len(cuts))
        return jnp.repeat(jnp.exp(draws), extent[dim] // blocks).reshape((-1,) + (1,) * (len(extent) - dim - 1))

    level = one(*cuts[0])
    for cut in cuts[1:]:
        level = level * one(*cut)
    return level


def split_up(amount, total, most, slope):
    weights = [(1 << 20) // math.isqrt(standing ** slope) + 1 for standing in range(2, amount + 1)]
    surplus, counts = total - most - (amount - 1), [1] * (amount - 1)
    while surplus > 0:
        free = [i for i in range(amount - 1) if counts[i] < most]
        pool, left = sum([weights[i] for i in free]), surplus
        for i in free:
            more = min(most - counts[i], max(1, left * weights[i] // pool), surplus)
            counts[i] = counts[i] + more
            surplus = surplus - more
    return np.array([most] + counts)


def uneven_parts(key, amount, total, limit, lean):
    if amount == 2:
        one = jax.random.randint(key, (), max(1, total - limit), min(limit, total - 1) + 1)
        return jnp.stack([one, total - one])
    sizes = jnp.asarray(split_up(amount, total, limit, lean), jnp.int32)
    twos = (amount - 1) // 2
    giver, taker = sizes[1:1 + 2 * twos:2], sizes[2:2 + 2 * twos:2]
    room = jnp.minimum(giver - 1, limit - taker)
    moved = jax.random.randint(jax.random.fold_in(key, 1), (twos,), 0, 1 << 20) % (room + 1)
    sizes = sizes.at[1:1 + 2 * twos:2].set(giver - moved).at[2:2 + 2 * twos:2].set(taker + moved)
    return sizes[jax.random.permutation(jax.random.fold_in(key, 2), amount)]


def bell_draw(own_key, dims, deviation, most, pieces=(), held_as=jnp.bfloat16):
    result = jax.random.normal(own_key, dims, jnp.float32) * deviation
    if len(pieces) > 0:
        result = levels(own_key, dims, pieces, -0.22, 0.18) * result
    return jnp.clip(result, min=-most, max=most).astype(held_as)


def setup_inputs(seed: int = 0) -> dict:
    keys = jax.random.split(jax.random.key(seed), 9)
    events = bell_draw(keys[0], (STREAMS, L, D), 1.0, 6.0, ((0, 2), (1, 16)))
    w_query = bell_draw(keys[1], (D, HEADS * HD), D ** -0.5, 0.1875)
    w_key = bell_draw(keys[2], (D, HEADS * HD), D ** -0.5, 0.1875)
    values = bell_draw(keys[3], (STREAMS, L, HEADS * HD), 1.0, 6.0, ((0, 2), (1, 16)))
    grad_out = bell_draw(keys[4], (STREAMS, L, HEADS * HD), 1.0, 6.0, ((0, 2), (1, 16)))
    lengths = jax.vmap(lambda own: uneven_parts(own, USERS, L, MAXLEN, 1))(jax.random.split(keys[5], STREAMS)).reshape((STREAMS, USERS)).astype(jnp.int32)
    stream_shift = jax.random.randint(keys[6], (STREAMS,), 0, L).astype(jnp.int32)
    block_keep = touch_ends((jax.random.randint(keys[7], (STREAMS, NBLK), 0, 4) < 3).astype(jnp.int32), jax.random.fold_in(keys[7], 1), 0, 1)
    return {"events": events, "w_query": w_query, "w_key": w_key, "values": values, "grad_out": grad_out, "lengths": lengths, "stream_shift": stream_shift, "block_keep": block_keep}


def tile_terms(query, grad, key, value, valid, scale, alpha):
    q32 = query.astype(jnp.float32)
    k32 = key.astype(jnp.float32)
    v32 = value.astype(jnp.float32)
    g32 = grad.astype(jnp.float32)
    z = jnp.einsum("bqhd,bkhd->bhqk", q32, k32) * alpha
    sig = jax.nn.sigmoid(z)
    weight = valid[:, None, :, :].astype(jnp.float32) * scale
    att = (z * sig * weight).astype(jnp.bfloat16)
    a32 = att.astype(jnp.float32)
    out = jnp.einsum("bhqk,bkhd->bqhd", a32, v32)
    dprod = jnp.einsum("bqhd,bkhd->bhqk", g32, v32)
    dsc = (dprod * sig * (1.0 + z * (1.0 - sig)) * weight * alpha).astype(jnp.bfloat16)
    d32 = dsc.astype(jnp.float32)
    dquery = jnp.einsum("bhqk,bkhd->bqhd", d32, k32)
    dkey = jnp.einsum("bhqk,bqhd->bkhd", d32, q32)
    dvalue = jnp.einsum("bhqk,bqhd->bkhd", a32, g32)
    return out, dquery, dkey, dvalue


def reference(events, w_query, w_key, values, grad_out, lengths, stream_shift, block_keep):
    alpha = 1.0 / (HD ** 0.5)
    scale = 1.0 / (MAXLEN ** 0.5)

    def one_stream(packed):
        x, vals, grads, lens, shift, keep = packed
        total = x.shape[0]
        nblocks = total // ROWS_DEV
        query = jnp.dot(x, w_query, preferred_element_type=jnp.float32).astype(jnp.bfloat16)
        key = jnp.dot(x, w_key, preferred_element_type=jnp.float32).astype(jnp.bfloat16)
        q4 = query.reshape(nblocks, ROWS_DEV, HEADS, HD)
        k4 = key.reshape(nblocks, ROWS_DEV, HEADS, HD)
        v4 = vals.reshape(nblocks, ROWS_DEV, HEADS, HD)
        g4 = grads.reshape(nblocks, ROWS_DEV, HEADS, HD)
        stored = jnp.arange(total, dtype=jnp.int32)
        pos = jnp.remainder(stored - shift, total).astype(jnp.int32)
        ends = jnp.cumsum(lens).astype(jnp.int32)
        user = jnp.sum((pos[:, None] >= ends[None, :]).astype(jnp.int32), axis=1).astype(jnp.int32)
        kept = keep[(pos // BLOCK).astype(jnp.int32)] > 0
        pos = pos.reshape(nblocks, ROWS_DEV)
        user = user.reshape(nblocks, ROWS_DEV)
        kept = kept.reshape(nblocks, ROWS_DEV)
        out = jnp.zeros((nblocks, ROWS_DEV, HEADS, HD), jnp.float32)
        dq = jnp.zeros_like(out)
        dk = jnp.zeros_like(out)
        dv = jnp.zeros_like(out)
        for step in range(SPAN + 1):
            kr = jnp.roll(k4, step, axis=0)
            vr = jnp.roll(v4, step, axis=0)
            posk = jnp.roll(pos, step, axis=0)
            userk = jnp.roll(user, step, axis=0)
            keptk = jnp.roll(kept, step, axis=0)
            valid = (user[:, :, None] == userk[:, None, :]) & (posk[:, None, :] <= pos[:, :, None]) & keptk[:, None, :]
            o, a, b, c = tile_terms(q4, g4, kr, vr, valid, scale, alpha)
            out = out + o
            dq = dq + a
            dk = dk + jnp.roll(b, -step, axis=0)
            dv = dv + jnp.roll(c, -step, axis=0)
        dq_b = dq.reshape(total, HEADS * HD).astype(jnp.bfloat16)
        dk_b = dk.reshape(total, HEADS * HD).astype(jnp.bfloat16)
        gq = jnp.dot(x.T, dq_b, preferred_element_type=jnp.float32)
        gk = jnp.dot(x.T, dk_b, preferred_element_type=jnp.float32)
        return (out.reshape(total, HEADS * HD).astype(jnp.bfloat16),
                dv.reshape(total, HEADS * HD).astype(jnp.bfloat16), gq, gk)

    attended, grad_values, gq, gk = lax.map(one_stream, (events, values, grad_out, lengths, stream_shift, block_keep))
    grad_wq = jnp.sum(gq, axis=0).astype(jnp.bfloat16)
    grad_wk = jnp.sum(gk, axis=0).astype(jnp.bfloat16)
    return (attended, grad_values, grad_wq, grad_wk)
```

```python
import functools

import jax
import jax.numpy as jnp
from jax import lax
from jax.experimental import pallas as pl
from jax.experimental.pallas import tpu as pltpu
from jax.sharding import PartitionSpec as P

HD = 128
BLOCK = 128
MAXLEN = 768
GROUP = 4
FAR = 1 << 30
ALPHA = 1.0 / HD**0.5
SCALE = 1.0 / MAXLEN**0.5
VMEM = pl.BlockSpec(memory_space=pltpu.VMEM)
SMEM = pl.BlockSpec(memory_space=pltpu.SMEM)


def call(kernel, outs, args, specs=None, flops=0, scratch=()):
    moved = sum(a.size * a.dtype.itemsize for a in list(outs) + list(args))
    return pl.pallas_call(
        kernel,
        out_shape=tuple(outs),
        in_specs=specs or [VMEM] * len(args),
        out_specs=tuple([VMEM] * len(outs)),
        scratch_shapes=scratch,
        compiler_params=pltpu.CompilerParams(vmem_limit_bytes=24 * 1024 * 1024),
        cost_estimate=pl.CostEstimate(flops=flops, bytes_accessed=moved, transcendentals=0),
    )(*args)


def like(rows, cols, dtype=jnp.bfloat16):
    return jax.ShapeDtypeStruct((rows, cols), dtype)


def partner(value, steps):
    count = lax.axis_size("ctx")
    return lax.ppermute(value, "ctx", [(i, i ^ steps) for i in range(count)])


def around(value, steps):
    count = lax.axis_size("ctx")
    return lax.ppermute(value, "ctx", [(i, (i + steps) % count) for i in range(count)])


def place():
    return lax.rem(lax.axis_index("ctx"), GROUP)


def head_cols(h):
    return pl.ds(pl.multiple_of(h * HD, HD), HD)


def nt(a, b):
    return lax.dot_general(a, b, (((1,), (1,)), ((), ())), preferred_element_type=jnp.float32)


def nn(a, b):
    return jnp.dot(a, b, preferred_element_type=jnp.float32)


def split_kernel(a_ref, b_ref, *outs):
    me = place()
    for k in range(GROUP):
        cols = head_cols(me ^ k)
        outs[k][:, :HD] = a_ref[:, cols]
        outs[k][:, HD:] = b_ref[:, cols]


def project_kernel(x_ref, wk_ref, wq_ref, o0, o1, o2, o3, keys, queries):
    keys[...] = nn(x_ref[...], wk_ref[...]).astype(jnp.bfloat16)
    queries[...] = nn(x_ref[...], wq_ref[...]).astype(jnp.bfloat16)
    split_kernel(keys, queries, o0, o1, o2, o3)


def arrange_kernel(i0, i1, i2, i3, first, second, up, down):
    rows = i0.shape[0]
    span = up.shape[0] // rows
    me = place()
    for k, ref in enumerate((i0, i1, i2, i3)):
        j = me ^ k
        at = pl.ds(pl.multiple_of(j * rows, rows), rows)
        first[at, :] = ref[:, :HD]
        second[at, :] = ref[:, HD:]

        @pl.when(j >= GROUP - span)
        def _():
            up[pl.ds(pl.multiple_of((j - (GROUP - span)) * rows, rows), rows), :] = ref[:, :HD]

        @pl.when(j < span)
        def _():
            down[at, :] = ref[:, HD:]


def offset_of(row, shift, total):
    return lax.rem(row - shift + 2 * total, total)


def key_place(row, rows, shift, keep_ref, total):
    base = offset_of(row, shift, total)
    nblk = keep_ref.shape[1]
    raw = base + lax.broadcasted_iota(jnp.int32, (rows, HD), 0)
    b0 = base // BLOCK
    kept = jnp.full((rows, HD), keep_ref[0, b0], jnp.int32)
    for more in range(1, rows // BLOCK + 1):
        flag = keep_ref[0, lax.rem(b0 + more, nblk)]
        kept = jnp.where(raw >= (b0 + more) * BLOCK, flag, kept)
    where = jnp.where(raw >= total, raw - total, raw)
    return jnp.where(kept > 0, where, FAR)


def query_place(row, rows, shift, len_ref, total):
    base = offset_of(row, shift, total)
    raw = base + lax.broadcasted_iota(jnp.int32, (1, rows), 1)
    where = jnp.where(raw >= total, raw - total, raw)
    begin = jnp.zeros((1, rows), jnp.int32)
    end = jnp.int32(0)
    for u in range(len_ref.shape[1]):
        length = len_ref[0, u]
        end = end + length
        begin = begin + jnp.where(where >= end, length, 0)
    return where, begin


def tile_terms(k, v, q, o, kpos, qpos, qbegin):
    y = nt(k, q) * (0.5 * ALPHA)
    t = jnp.tanh(y)
    u = 1.0 + t
    kpos = jnp.concatenate([kpos] * (q.shape[0] // HD), axis=1)
    valid = (kpos >= qbegin) & (kpos <= qpos)
    att = jnp.where(valid, y * u, 0.0).astype(jnp.bfloat16)
    slope = u * (1.0 + y * (1.0 - t))
    ds = jnp.where(valid, nt(v, o) * slope, 0.0).astype(jnp.bfloat16)
    return att, ds


def inner_kernel(len_ref, shift_ref, keep_ref, k_ref, q_ref, v_ref, o_ref, out_t, dq_t, dk, dv):
    rows = k_ref.shape[0] // GROUP
    count = lax.axis_size("ctx")
    total = rows * count
    shift = shift_ref[0]
    base = (lax.axis_index("ctx") // GROUP) * (GROUP * rows)
    out_t[...] = jnp.zeros_like(out_t)
    dq_t[...] = jnp.zeros_like(dq_t)

    def key_step(kt, _):
        at = pl.ds(pl.multiple_of(kt * rows, rows), rows)
        k, v = k_ref[at, :], v_ref[at, :]
        k_t, v_t = k.T, v.T
        kpos = key_place(base + kt * rows, rows, shift, keep_ref, total)
        dk[at, :] = jnp.zeros((rows, HD), jnp.float32)
        dv[at, :] = jnp.zeros((rows, HD), jnp.float32)

        def query_step(qt, _):
            qs = pl.ds(pl.multiple_of(qt * rows, rows), rows)
            q, o = q_ref[qs, :], o_ref[qs, :]
            qpos, qbegin = query_place(base + qt * rows, rows, shift, len_ref, total)
            att, ds = tile_terms(k, v, q, o, kpos, qpos, qbegin)
            out_t[:, qs] += nn(v_t, att)
            dq_t[:, qs] += nn(k_t, ds)
            dv[at, :] += nn(att, o)
            dk[at, :] += nn(ds, q)
            return 0

        return lax.fori_loop(kt, GROUP, query_step, 0)

    lax.fori_loop(0, GROUP, key_step, 0)


def outer_kernel(
    len_ref, shift_ref, keep_ref, k_ref, q_ref, v_ref, o_ref, kp_ref, vp_ref, qn_ref, on_ref,
    out_in, dq_in, dk_in, dv_in, s0, s1, s2, s3, dqk, out_t, dq_t, dk, dv,
):
    rows = k_ref.shape[0] // GROUP
    span = kp_ref.shape[0] // rows
    count = lax.axis_size("ctx")
    total = rows * count
    shift = shift_ref[0]
    base = (lax.axis_index("ctx") // GROUP) * (GROUP * rows)
    me = place()
    out_t[...] = out_in[...]
    dq_t[...] = dq_in[...]
    dk[...] = dk_in[...]
    dv[...] = dv_in[...]

    def before(p, _):
        at = pl.ds(pl.multiple_of(p * rows, rows), rows)
        k, v = kp_ref[at, :], vp_ref[at, :]
        k_t, v_t = k.T, v.T
        kpos = key_place(base + (p - span) * rows, rows, shift, keep_ref, total)

        def query_step(qt, _):
            qs = pl.ds(pl.multiple_of(qt * rows, rows), rows)
            qpos, qbegin = query_place(base + qt * rows, rows, shift, len_ref, total)
            att, ds = tile_terms(k, v, q_ref[qs, :], o_ref[qs, :], kpos, qpos, qbegin)
            out_t[:, qs] += nn(v_t, att)
            dq_t[:, qs] += nn(k_t, ds)
            return 0

        return lax.fori_loop(0, p + 1, query_step, 0)

    lax.fori_loop(0, span, before, 0)

    def after(n, _):
        qs = pl.ds(pl.multiple_of(n * rows, rows), rows)
        q, o = qn_ref[qs, :], on_ref[qs, :]
        qpos, qbegin = query_place(base + (GROUP + n) * rows, rows, shift, len_ref, total)

        def key_step(kt, _):
            at = pl.ds(pl.multiple_of(kt * rows, rows), rows)
            kpos = key_place(base + kt * rows, rows, shift, keep_ref, total)
            att, ds = tile_terms(k_ref[at, :], v_ref[at, :], q, o, kpos, qpos, qbegin)
            dv[at, :] += nn(att, o)
            dk[at, :] += nn(ds, q)
            return 0

        return lax.fori_loop(n + 1, GROUP, key_step, 0)

    lax.fori_loop(0, span, after, 0)

    factor = 0.5 * SCALE * ALPHA
    dqk[:HD, :] = (dq_t[...] * factor).astype(jnp.bfloat16)
    for j in range(GROUP):
        at = slice(j * rows, (j + 1) * rows)
        dqk[HD:, at] = (dk[at, :] * factor).T.astype(jnp.bfloat16)
    for k, ref in enumerate((s0, s1, s2, s3)):
        at = pl.ds(pl.multiple_of((me ^ k) * rows, rows), rows)
        ref[:, :HD] = (out_t[:, at] * SCALE).T.astype(jnp.bfloat16)
        ref[:, HD:] = (dv[at, :] * SCALE).astype(jnp.bfloat16)


def terms_of(dqk, e0, e1, e2, e3):
    rows = e0.shape[0]
    me = place()
    total = None
    for k, ref in enumerate((e0, e1, e2, e3)):
        at = pl.ds(pl.multiple_of((me ^ k) * rows, rows), rows)
        part = nn(dqk[:, at], ref[...])
        total = part if total is None else total + part
    return total


def terms_kernel(dqk, e0, e1, e2, e3, whole):
    whole[...] = terms_of(dqk, e0, e1, e2, e3)


def block_terms_kernel(targets, dqk, e0, e1, e2, e3, *refs):
    outs, hold = refs[:-1], refs[-1]
    hold[...] = terms_of(dqk, e0, e1, e2, e3).astype(jnp.bfloat16)
    planes = lax.axis_size("ctx") // GROUP
    y = lax.axis_index("dp")
    z = lax.axis_index("ctx") // GROUP
    for (dy, dz), ref in zip(targets, outs):
        block = 2 * lax.rem(z + dz, planes) + (y ^ dy)
        width = ref.shape[1]
        ref[...] = hold[:, pl.ds(pl.multiple_of(block * width, width), width)]


def sum_kernel(*refs):
    ins, (near, far, hold) = refs[:-3], refs[-3:]
    total = ins[0][...].astype(jnp.float32)
    for ref in ins[1:]:
        total = total + ref[...].astype(jnp.float32)
    hold[...] = total.T
    share = near.shape[0]
    core = lax.rem(lax.axis_index("ctx"), 2)
    near[...] = hold[pl.ds(pl.multiple_of(core * share, share), share), :].astype(jnp.bfloat16)
    far[...] = hold[pl.ds(pl.multiple_of((1 - core) * share, share), share), :].astype(jnp.bfloat16)


def finish_kernel(r00, r01, r10, r11, gq, gk):
    y = lax.axis_index("dp")
    core = lax.rem(lax.axis_index("ctx"), 2)
    for (a, b), ref in zip(((0, 0), (0, 1), (1, 0), (1, 1)), (r00, r01, r10, r11)):
        cols = head_cols(2 * (y ^ a) + (core ^ b))
        gq[:, cols] = ref[:, :HD]
        gk[:, cols] = ref[:, HD:]


def merge_kernel(i0, i1, i2, i3, first, second):
    me = place()
    for k, ref in enumerate((i0, i1, i2, i3)):
        cols = head_cols(me ^ k)
        first[:, cols] = ref[:, :HD]
        second[:, cols] = ref[:, HD:]


def direct_reduce(dqk, gathered, share):
    streams = lax.axis_size("dp")
    count = lax.axis_size("ctx")
    planes = count // GROUP
    width = gathered[0].shape[1]
    block = width // (streams * planes)
    targets = [(dy, dz) for dz in range(planes) for dy in range(streams)]
    flops = 2 * dqk.shape[0] * dqk.shape[1] * width
    sends = call(
        functools.partial(block_terms_kernel, targets),
        [like(2 * HD, block)] * len(targets),
        (dqk, *gathered),
        flops=flops,
        scratch=[pltpu.VMEM((2 * HD, width), jnp.bfloat16)],
    )
    arrived = []
    for (dy, dz), value in zip(targets, sends):
        if (dy, dz) != (0, 0):
            pairs = []
            for y in range(streams):
                for i in range(count):
                    pairs.append((y * count + i, (y ^ dy) * count + (i + dz * GROUP) % count))
            value = lax.ppermute(value, ("dp", "ctx"), pairs)
        arrived.append(value)
    near, far = call(
        sum_kernel,
        [like(share, 2 * HD)] * 2,
        arrived,
        scratch=[pltpu.VMEM((block, 2 * HD), jnp.float32)],
    )
    received = []
    for a in range(2):
        for b in range(2):
            pairs = []
            for y in range(2):
                for i in range(count):
                    z, x, c = i // 4, (i // 2) % 2, i % 2
                    pairs.append((y * count + i, (x ^ a) * count + 4 * z + 2 * y + (c ^ b)))
            received.append(lax.ppermute((near, far)[b], ("dp", "ctx"), pairs))
    return call(finish_kernel, [like(share, GROUP * HD)] * 2, received)


def general_reduce(dqk, gathered, share):
    count = lax.axis_size("ctx")
    planes = count // GROUP
    width = gathered[0].shape[1]
    flops = 2 * dqk.shape[0] * dqk.shape[1] * width
    (whole,) = call(
        terms_kernel, [like(2 * HD, width, jnp.float32)], (dqk, *gathered), flops=flops
    )
    whole = lax.psum(whole.T, "dp")
    same_head = [[g * GROUP + j for g in range(planes)] for j in range(GROUP)]
    plane = [[g * GROUP + j for j in range(GROUP)] for g in range(planes)]
    part = lax.psum_scatter(
        whole, "ctx", scatter_dimension=0, axis_index_groups=same_head, tiled=True
    ).astype(jnp.bfloat16)
    part = lax.all_to_all(
        part.reshape(GROUP, share, 2 * HD), "ctx", 0, 0, axis_index_groups=plane, tiled=True
    )
    part = jnp.moveaxis(part.reshape(GROUP, share, 2, HD), 0, 2)
    return part[:, 0].reshape(share, GROUP * HD), part[:, 1].reshape(share, GROUP * HD)


def body(events, w_query, w_key, values, grad_out, lengths, stream_shift, block_keep):
    rows, width = events.shape[1:]
    features = w_query.shape[1]
    count = lax.axis_size("ctx")
    local = events[0]
    all_rows = GROUP * rows
    halo = MAXLEN
    pair = like(rows, 2 * HD)
    full = like(all_rows, HD)
    edge = like(halo, HD)

    vo = call(split_kernel, [pair] * GROUP, (values[0], grad_out[0]))
    vo = (vo[0],) + tuple(partner(vo[k], k) for k in range(1, GROUP))
    kq = call(
        project_kernel,
        [pair] * GROUP,
        (local, w_key, w_query),
        flops=4 * rows * width * features,
        scratch=[pltpu.VMEM((rows, features), jnp.bfloat16)] * 2,
    )
    kq = (kq[0],) + tuple(partner(kq[k], k) for k in range(1, GROUP))
    v, o, v_up, o_down = call(arrange_kernel, [full, full, edge, edge], vo)
    v_prev, o_next = around(v_up, GROUP), around(o_down, -GROUP)
    k, q, k_up, q_down = call(arrange_kernel, [full, full, edge, edge], kq)
    k_prev, q_next = around(k_up, GROUP), around(q_down, -GROUP)

    e1 = partner(local, 1)
    late, _ = lax.optimization_barrier((local, kq[2]))
    e2 = partner(late, 2)
    e3 = partner(e2, 1)
    info = (lengths, stream_shift, block_keep)
    wide, tall = like(HD, all_rows, jnp.float32), like(all_rows, HD, jnp.float32)
    sums = call(
        inner_kernel,
        [wide, wide, tall, tall],
        (*info, k, q, v, o),
        specs=[SMEM] * 3 + [VMEM] * 4,
        flops=2 * 6 * 10 * rows * rows * HD,
    )
    *parts, dqk = call(
        outer_kernel,
        [pair] * GROUP + [like(2 * HD, all_rows)],
        (*info, k, q, v, o, k_prev, v_prev, q_next, o_next, *sums),
        specs=[SMEM] * 3 + [VMEM] * 12,
        flops=2 * 8 * 6 * rows * rows * HD,
        scratch=[
            pltpu.VMEM((HD, all_rows), jnp.float32),
            pltpu.VMEM((HD, all_rows), jnp.float32),
            pltpu.VMEM((all_rows, HD), jnp.float32),
            pltpu.VMEM((all_rows, HD), jnp.float32),
        ],
    )
    share = width // count
    reduce = direct_reduce if lax.axis_size("dp") == 2 and count == 16 else general_reduce
    grad_wq, grad_wk = reduce(dqk, (local, e1, e2, e3), share)
    parts = (parts[0],) + tuple(partner(parts[k], k) for k in range(1, GROUP))
    attended, grad_values = call(merge_kernel, [like(rows, features)] * 2, parts)
    return (attended[None], grad_values[None], grad_wq, grad_wk)


def solution(mesh):
    placed = (
        P("dp", "ctx", None),
        P(),
        P(),
        P("dp", "ctx", None),
        P("dp", "ctx", None),
        P("dp", None),
        P("dp"),
        P("dp", None),
    )
    return jax.shard_map(
        body,
        mesh=mesh,
        in_specs=placed,
        out_specs=(P("dp", "ctx", None), P("dp", "ctx", None), P("ctx", None), P("ctx", None)),
        check_vma=False,
    )
```

```python
import functools

import jax
import jax.numpy as jnp
from jax import lax
from jax.experimental import pallas as pl
from jax.experimental.pallas import tpu as pltpu
from jax.sharding import PartitionSpec as P

HD = 128
BLOCK = 128
MAXLEN = 768
GROUP = 4
FAR = 1 << 30
PEAK = 1.15e9
ALPHA = 1.0 / HD**0.5
SCALE = 1.0 / MAXLEN**0.5
VMEM = pl.BlockSpec(memory_space=pltpu.VMEM)
SMEM = pl.BlockSpec(memory_space=pltpu.SMEM)


def call(kernel, outs, args, specs=None, busy=0.5, scratch=()):
    moved = sum(a.size * a.dtype.itemsize for a in list(outs) + list(args))
    return pl.pallas_call(
        kernel,
        out_shape=tuple(outs),
        in_specs=specs or [VMEM] * len(args),
        out_specs=tuple([VMEM] * len(outs)),
        scratch_shapes=scratch,
        compiler_params=pltpu.CompilerParams(vmem_limit_bytes=24 * 1024 * 1024),
        cost_estimate=pl.CostEstimate(
            flops=int(busy * PEAK), bytes_accessed=moved, transcendentals=0
        ),
    )(*args)


def like(rows, cols, dtype=jnp.bfloat16):
    return jax.ShapeDtypeStruct((rows, cols), dtype)


def partner(value, steps):
    count = lax.axis_size("ctx")
    return lax.ppermute(value, "ctx", [(i, i ^ steps) for i in range(count)])


def around(value, low, high):
    count = lax.axis_size("ctx")
    pairs = []
    for i in range(count):
        planes = low if i % GROUP < GROUP // 2 else high
        pairs.append((i, (i + planes * GROUP) % count))
    return lax.ppermute(value, "ctx", pairs)


def after(value, *earlier):
    return lax.optimization_barrier((value, *earlier))[0]


def place():
    return lax.rem(lax.axis_index("ctx"), GROUP)


def head_cols(h):
    return pl.ds(pl.multiple_of(h * HD, HD), HD)


def nt(a, b):
    return lax.dot_general(a, b, (((1,), (1,)), ((), ())), preferred_element_type=jnp.float32)


def nn(a, b):
    return jnp.dot(a, b, preferred_element_type=jnp.float32)


def split_kernel(a_ref, b_ref, *outs):
    me = place()
    for k in range(GROUP):
        cols = head_cols(me ^ k)
        outs[k][:, :HD] = a_ref[:, cols]
        outs[k][:, HD:] = b_ref[:, cols]


def project_kernel(x_ref, wk_ref, wq_ref, o0, o1, o2, o3, keys, queries):
    keys[...] = nn(x_ref[...], wk_ref[...]).astype(jnp.bfloat16)
    queries[...] = nn(x_ref[...], wq_ref[...]).astype(jnp.bfloat16)
    split_kernel(keys, queries, o0, o1, o2, o3)


def upper():
    return lax.div(place(), 2)


def edge_kernel(own, near_kq, near_vo, far_kq, far_vo, big, small):
    rows = near_kq.shape[0]
    core = lax.rem(place(), 2)
    keys_big = upper() == (1 if own else 0)
    for ref_kq, ref_vo, at_core in ((near_kq, near_vo, core), (far_kq, far_vo, 1 - core)):
        at = pl.ds(pl.multiple_of(at_core * rows, rows), rows)

        @pl.when(keys_big)
        def _():
            big[at, :HD] = ref_kq[:, :HD]
            big[at, HD:] = ref_vo[:, :HD]

            @pl.when(at_core == 0)
            def _():
                small[:, :HD] = ref_kq[:, HD:]
                small[:, HD:] = ref_vo[:, HD:]

        @pl.when(jnp.logical_not(keys_big))
        def _():
            big[at, :HD] = ref_kq[:, HD:]
            big[at, HD:] = ref_vo[:, HD:]

            @pl.when(at_core == 1)
            def _():
                small[:, :HD] = ref_kq[:, :HD]
                small[:, HD:] = ref_vo[:, :HD]


def offset_of(row, shift, total):
    return lax.rem(row - shift + 2 * total, total)


def key_place(row, rows, shift, keep_ref, total):
    base = offset_of(row, shift, total)
    nblk = keep_ref.shape[1]
    raw = base + lax.broadcasted_iota(jnp.int32, (rows, HD), 0)
    b0 = base // BLOCK
    kept = jnp.full((rows, HD), keep_ref[0, b0], jnp.int32)
    for more in range(1, rows // BLOCK + 1):
        flag = keep_ref[0, lax.rem(b0 + more, nblk)]
        kept = jnp.where(raw >= (b0 + more) * BLOCK, flag, kept)
    where = jnp.where(raw >= total, raw - total, raw)
    return jnp.where(kept > 0, where, FAR)


def query_place(row, rows, shift, len_ref, total):
    base = offset_of(row, shift, total)
    raw = base + lax.broadcasted_iota(jnp.int32, (1, rows), 1)
    where = jnp.where(raw >= total, raw - total, raw)
    begin = jnp.zeros((1, rows), jnp.int32)
    end = jnp.int32(0)
    for u in range(len_ref.shape[1]):
        length = len_ref[0, u]
        end = end + length
        begin = begin + jnp.where(where >= end, length, 0)
    return where, begin


def tile_terms(k, v, q, o, kpos, qpos, qbegin):
    y = nt(k, q) * (0.5 * ALPHA)
    t = jnp.tanh(y)
    u = 1.0 + t
    kpos = jnp.concatenate([kpos] * (q.shape[0] // HD), axis=1)
    valid = (kpos >= qbegin) & (kpos <= qpos)
    att = jnp.where(valid, y * u, 0.0).astype(jnp.bfloat16)
    slope = u * (1.0 + y * (1.0 - t))
    ds = jnp.where(valid, nt(v, o) * slope, 0.0).astype(jnp.bfloat16)
    return att, ds


def inner_kernel(
    len_ref, shift_ref, keep_ref, a0, a1, a2, a3, b0, b1, b2, b3,
    k_ref, q_ref, v_ref, o_ref, out_t, dq_t, dk, dv,
):
    rows = a0.shape[0]
    count = lax.axis_size("ctx")
    total = rows * count
    shift = shift_ref[0]
    base = (lax.axis_index("ctx") // GROUP) * (GROUP * rows)
    me = place()
    for i, (kq, vo) in enumerate(((a0, b0), (a1, b1), (a2, b2), (a3, b3))):
        at = pl.ds(pl.multiple_of((me ^ i) * rows, rows), rows)
        k_ref[at, :] = kq[:, :HD]
        q_ref[at, :] = kq[:, HD:]
        v_ref[at, :] = vo[:, :HD]
        o_ref[at, :] = vo[:, HD:]
    out_t[...] = jnp.zeros_like(out_t)
    dq_t[...] = jnp.zeros_like(dq_t)

    def key_step(kt, _):
        at = pl.ds(pl.multiple_of(kt * rows, rows), rows)
        k, v = k_ref[at, :], v_ref[at, :]
        k_t, v_t = k.T, v.T
        kpos = key_place(base + kt * rows, rows, shift, keep_ref, total)
        dk[at, :] = jnp.zeros((rows, HD), jnp.float32)
        dv[at, :] = jnp.zeros((rows, HD), jnp.float32)

        def query_step(qt, _):
            qs = pl.ds(pl.multiple_of(qt * rows, rows), rows)
            q, o = q_ref[qs, :], o_ref[qs, :]
            qpos, qbegin = query_place(base + qt * rows, rows, shift, len_ref, total)
            att, ds = tile_terms(k, v, q, o, kpos, qpos, qbegin)
            out_t[:, qs] += nn(v_t, att)
            dq_t[:, qs] += nn(k_t, ds)
            dv[at, :] += nn(att, o)
            dk[at, :] += nn(ds, q)
            return 0

        return lax.fori_loop(kt, GROUP, query_step, 0)

    lax.fori_loop(0, GROUP, key_step, 0)


def halo_kernel(
    own, last, len_ref, shift_ref, keep_ref, k_ref, q_ref, v_ref, o_ref, big, small,
    out_in, dq_in, dk_in, dv_in, *outs,
):
    out_t, dq_t, dk, dv = outs[-4:]
    rows = small.shape[0]
    span = GROUP - 1
    count = lax.axis_size("ctx")
    total = rows * count
    shift = shift_ref[0]
    base = (lax.axis_index("ctx") // GROUP) * (GROUP * rows)
    me = place()
    out_t[...] = out_in[...]
    dq_t[...] = dq_in[...]
    dk[...] = dk_in[...]
    dv[...] = dv_in[...]

    def before(source, first):
        def key_step(p, _):
            at = pl.ds(pl.multiple_of((p - first) * rows, rows), rows)
            k, v = source[at, :HD], source[at, HD:]
            k_t, v_t = k.T, v.T
            kpos = key_place(base + (p - span) * rows, rows, shift, keep_ref, total)

            def query_step(qt, _):
                qs = pl.ds(pl.multiple_of(qt * rows, rows), rows)
                qpos, qbegin = query_place(base + qt * rows, rows, shift, len_ref, total)
                att, ds = tile_terms(k, v, q_ref[qs, :], o_ref[qs, :], kpos, qpos, qbegin)
                out_t[:, qs] += nn(v_t, att)
                dq_t[:, qs] += nn(k_t, ds)
                return 0

            return lax.fori_loop(0, p + 1, query_step, 0)

        return key_step

    def behind(source, first):
        def query_step(n, _):
            qs = pl.ds(pl.multiple_of((n - first) * rows, rows), rows)
            q, o = source[qs, :HD], source[qs, HD:]
            qpos, qbegin = query_place(base + (GROUP + n) * rows, rows, shift, len_ref, total)

            def key_step(kt, _):
                at = pl.ds(pl.multiple_of(kt * rows, rows), rows)
                kpos = key_place(base + kt * rows, rows, shift, keep_ref, total)
                att, ds = tile_terms(k_ref[at, :], v_ref[at, :], q, o, kpos, qpos, qbegin)
                dv[at, :] += nn(att, o)
                dk[at, :] += nn(ds, q)
                return 0

            return lax.fori_loop(n + 1, GROUP, key_step, 0)

        return query_step

    keys_big = upper() == (1 if own else 0)

    @pl.when(keys_big)
    def _():
        lax.fori_loop(1, span, before(big, 1), 0)
        behind(small, span - 1)(jnp.int32(span - 1), 0)

    @pl.when(jnp.logical_not(keys_big))
    def _():
        before(small, 0)(jnp.int32(0), 0)
        lax.fori_loop(0, span - 1, behind(big, 0), 0)

    if not last:
        return
    s0, s1, s2, s3, dqk = outs[:5]
    factor = 0.5 * SCALE * ALPHA
    dqk[:HD, :] = (dq_t[...] * factor).astype(jnp.bfloat16)
    for j in range(GROUP):
        at = slice(j * rows, (j + 1) * rows)
        dqk[HD:, at] = (dk[at, :] * factor).T.astype(jnp.bfloat16)
    for i, ref in enumerate((s0, s1, s2, s3)):
        at = pl.ds(pl.multiple_of((me ^ i) * rows, rows), rows)
        ref[:, :HD] = (out_t[:, at] * SCALE).T.astype(jnp.bfloat16)
        ref[:, HD:] = (dv[at, :] * SCALE).astype(jnp.bfloat16)


def terms_of(dqk, e0, e1, e2, e3):
    rows = e0.shape[0]
    me = place()
    total = None
    for k, ref in enumerate((e0, e1, e2, e3)):
        at = pl.ds(pl.multiple_of((me ^ k) * rows, rows), rows)
        part = nn(dqk[:, at], ref[...])
        total = part if total is None else total + part
    return total


def terms_kernel(dqk, e0, e1, e2, e3, whole):
    whole[...] = terms_of(dqk, e0, e1, e2, e3)


def block_terms_kernel(targets, dqk, e0, e1, e2, e3, *refs):
    outs, hold = refs[:-1], refs[-1]
    hold[...] = terms_of(dqk, e0, e1, e2, e3).astype(jnp.bfloat16)
    planes = lax.axis_size("ctx") // GROUP
    y = lax.axis_index("dp")
    z = lax.axis_index("ctx") // GROUP
    for (dy, dz), ref in zip(targets, outs):
        block = 2 * lax.rem(z + dz, planes) + (y ^ dy)
        width = ref.shape[1]
        ref[...] = hold[:, pl.ds(pl.multiple_of(block * width, width), width)]


def sum_kernel(*refs):
    ins, (near, far, hold) = refs[:-3], refs[-3:]
    total = ins[0][...].astype(jnp.float32)
    for ref in ins[1:]:
        total = total + ref[...].astype(jnp.float32)
    hold[...] = total.T
    share = near.shape[0]
    core = lax.rem(lax.axis_index("ctx"), 2)
    near[...] = hold[pl.ds(pl.multiple_of(core * share, share), share), :].astype(jnp.bfloat16)
    far[...] = hold[pl.ds(pl.multiple_of((1 - core) * share, share), share), :].astype(jnp.bfloat16)


def finish_kernel(r00, r01, r10, r11, gq, gk):
    y = lax.axis_index("dp")
    core = lax.rem(lax.axis_index("ctx"), 2)
    for (a, b), ref in zip(((0, 0), (0, 1), (1, 0), (1, 1)), (r00, r01, r10, r11)):
        cols = head_cols(2 * (y ^ a) + (core ^ b))
        gq[:, cols] = ref[:, :HD]
        gk[:, cols] = ref[:, HD:]


def merge_kernel(i0, i1, i2, i3, first, second):
    me = place()
    for k, ref in enumerate((i0, i1, i2, i3)):
        cols = head_cols(me ^ k)
        first[:, cols] = ref[:, :HD]
        second[:, cols] = ref[:, HD:]


def direct_reduce(dqk, gathered, share):
    streams = lax.axis_size("dp")
    count = lax.axis_size("ctx")
    planes = count // GROUP
    width = gathered[0].shape[1]
    block = width // (streams * planes)
    targets = [(dy, dz) for dz in range(planes) for dy in range(streams)]
    sends = call(
        functools.partial(block_terms_kernel, targets),
        [like(2 * HD, block)] * len(targets),
        (dqk, *gathered),
        busy=2,
        scratch=[pltpu.VMEM((2 * HD, width), jnp.bfloat16)],
    )
    arrived = []
    for (dy, dz), value in zip(targets, sends):
        if (dy, dz) != (0, 0):
            pairs = []
            for y in range(streams):
                for i in range(count):
                    pairs.append((y * count + i, (y ^ dy) * count + (i + dz * GROUP) % count))
            value = lax.ppermute(value, ("dp", "ctx"), pairs)
        arrived.append(value)
    near, far = call(
        sum_kernel,
        [like(share, 2 * HD)] * 2,
        arrived,
        scratch=[pltpu.VMEM((block, 2 * HD), jnp.float32)],
    )
    received = []
    for a in range(2):
        for b in range(2):
            pairs = []
            for y in range(2):
                for i in range(count):
                    z, x, c = i // 4, (i // 2) % 2, i % 2
                    pairs.append((y * count + i, (x ^ a) * count + 4 * z + 2 * y + (c ^ b)))
            received.append(lax.ppermute((near, far)[b], ("dp", "ctx"), pairs))
    return call(finish_kernel, [like(share, GROUP * HD)] * 2, received)


def general_reduce(dqk, gathered, share):
    count = lax.axis_size("ctx")
    planes = count // GROUP
    width = gathered[0].shape[1]
    (whole,) = call(
        terms_kernel, [like(2 * HD, width, jnp.float32)], (dqk, *gathered), busy=2
    )
    whole = lax.psum(whole.T, "dp")
    same_head = [[g * GROUP + j for g in range(planes)] for j in range(GROUP)]
    plane = [[g * GROUP + j for j in range(GROUP)] for g in range(planes)]
    part = lax.psum_scatter(
        whole, "ctx", scatter_dimension=0, axis_index_groups=same_head, tiled=True
    ).astype(jnp.bfloat16)
    part = lax.all_to_all(
        part.reshape(GROUP, share, 2 * HD), "ctx", 0, 0, axis_index_groups=plane, tiled=True
    )
    part = jnp.moveaxis(part.reshape(GROUP, share, 2, HD), 0, 2)
    return part[:, 0].reshape(share, GROUP * HD), part[:, 1].reshape(share, GROUP * HD)


def body(events, w_query, w_key, values, grad_out, lengths, stream_shift, block_keep):
    rows, width = events.shape[1:]
    features = w_query.shape[1]
    count = lax.axis_size("ctx")
    local = events[0]
    all_rows = GROUP * rows
    pair = like(rows, 2 * HD)
    full = like(all_rows, HD)

    vo = call(split_kernel, [pair] * GROUP, (values[0], grad_out[0]))
    vo = (vo[0],) + tuple(partner(vo[k], k) for k in range(1, GROUP))
    kq = call(
        project_kernel,
        [pair] * GROUP,
        (local, w_key, w_query),
        busy=4,
        scratch=[pltpu.VMEM((rows, features), jnp.bfloat16)] * 2,
    )
    kq = (kq[0], partner(kq[1], 1)) + tuple(
        partner(after(kq[k], vo[2], vo[3]), k) for k in range(2, GROUP)
    )
    edges = [like(2 * rows, 2 * HD), pair]
    big, small = call(functools.partial(edge_kernel, True), edges, (kq[0], vo[0], kq[1], vo[1]))
    own = around(big, -1, 1), around(small, 1, -1)
    big, small = call(functools.partial(edge_kernel, False), edges, (kq[2], vo[2], kq[3], vo[3]))
    other = around(big, 1, -1), around(small, -1, 1)

    e1 = partner(local, 1)
    e2 = partner(after(local, kq[2], kq[3]), 2)
    info = (lengths, stream_shift, block_keep)
    wide, tall = like(HD, all_rows, jnp.float32), like(all_rows, HD, jnp.float32)
    sums = [wide, wide, tall, tall]
    k, q, v, o, *held = call(
        inner_kernel,
        [full] * 4 + sums,
        (*info, *kq, *vo),
        specs=[SMEM] * 3 + [VMEM] * 8,
        busy=15,
    )
    held = call(
        functools.partial(halo_kernel, True, False),
        sums,
        (*info, k, q, v, o, *own, *held),
        specs=[SMEM] * 3 + [VMEM] * 10,
        busy=8,
    )
    e3 = partner(after(e2, *held), 1)
    *parts, dqk = call(
        functools.partial(halo_kernel, False, True),
        [pair] * GROUP + [like(2 * HD, all_rows)],
        (*info, k, q, v, o, *other, *held),
        specs=[SMEM] * 3 + [VMEM] * 10,
        busy=8,
        scratch=[
            pltpu.VMEM((HD, all_rows), jnp.float32),
            pltpu.VMEM((HD, all_rows), jnp.float32),
            pltpu.VMEM((all_rows, HD), jnp.float32),
            pltpu.VMEM((all_rows, HD), jnp.float32),
        ],
    )
    share = width // count
    reduce = direct_reduce if lax.axis_size("dp") == 2 and count == 16 else general_reduce
    grad_wq, grad_wk = reduce(dqk, (local, e1, e2, e3), share)
    parts = (parts[0],) + tuple(partner(parts[k], k) for k in range(1, GROUP))
    attended, grad_values = call(merge_kernel, [like(rows, features)] * 2, parts)
    return (attended[None], grad_values[None], grad_wq, grad_wk)


def solution(mesh):
    placed = (
        P("dp", "ctx", None),
        P(),
        P(),
        P("dp", "ctx", None),
        P("dp", "ctx", None),
        P("dp", None),
        P("dp"),
        P("dp", None),
    )
    return jax.shard_map(
        body,
        mesh=mesh,
        in_specs=placed,
        out_specs=(P("dp", "ctx", None), P("dp", "ctx", None), P("ctx", None), P("ctx", None)),
        check_vma=False,
    )
```

```python
import functools

import jax
import jax.numpy as jnp
from jax import lax
from jax.experimental import pallas as pl
from jax.experimental.pallas import tpu as pltpu
from jax.sharding import PartitionSpec as P

HD = 128
BLOCK = 128
MAXLEN = 768
GROUP = 4
FAR = 1 << 30
PEAK = 1.15e9
ALPHA = 1.0 / HD**0.5
SCALE = 1.0 / MAXLEN**0.5
VMEM = pl.BlockSpec(memory_space=pltpu.VMEM)
HBM = pl.BlockSpec(memory_space=pltpu.HBM)
SMEM = pl.BlockSpec(memory_space=pltpu.SMEM)


def call(kernel, outs, args, specs=None, busy=0.5, scratch=(), aliases=None):
    moved = sum(a.size * a.dtype.itemsize for a in list(outs) + list(args))
    return pl.pallas_call(
        kernel,
        out_shape=tuple(outs),
        in_specs=specs or [VMEM] * len(args),
        out_specs=tuple([VMEM] * len(outs)),
        scratch_shapes=scratch,
        input_output_aliases=aliases or {},
        compiler_params=pltpu.CompilerParams(vmem_limit_bytes=24 * 1024 * 1024),
        cost_estimate=pl.CostEstimate(
            flops=int(busy * PEAK), bytes_accessed=moved, transcendentals=0
        ),
    )(*args)


def like(rows, cols, dtype=jnp.bfloat16):
    return jax.ShapeDtypeStruct((rows, cols), dtype)


def partner(value, steps):
    count = lax.axis_size("ctx")
    return lax.ppermute(value, "ctx", [(i, i ^ steps) for i in range(count)])


def around(value, low, high):
    count = lax.axis_size("ctx")
    pairs = []
    for i in range(count):
        planes = low if i % GROUP < GROUP // 2 else high
        pairs.append((i, (i + planes * GROUP) % count))
    return lax.ppermute(value, "ctx", pairs)


def place():
    return lax.rem(lax.axis_index("ctx"), GROUP)


def head_cols(h):
    return pl.ds(pl.multiple_of(h * HD, HD), HD)


def nn(a, b):
    return jnp.dot(a, b, preferred_element_type=jnp.float32)


def fetch_kernel(a_ref, b_ref, wk_ref, wq_ref, *refs):
    outs, weights, sems = refs[:GROUP], refs[GROUP], refs[GROUP + 1]
    me = place()
    copies = []
    for side, ref in enumerate((wk_ref, wq_ref)):
        to = slice(side * HD, (side + 1) * HD)
        copies.append((ref.at[:, head_cols(me)], weights.at[:, to]))
    for k in range(GROUP):
        for side, ref in enumerate((a_ref, b_ref)):
            to = slice(side * HD, (side + 1) * HD)
            copies.append((ref.at[:, head_cols(me ^ k)], outs[k].at[:, to]))
    started = [pltpu.make_async_copy(*pair, sems.at[i]) for i, pair in enumerate(copies)]
    for copy in started:
        copy.start()
    for copy in started:
        copy.wait()


def project_kernel(near, far, weights, near_kq, far_kq):
    near_kq[...] = nn(near[...], weights[...]).astype(jnp.bfloat16)
    far_kq[...] = nn(far[...], weights[...]).astype(jnp.bfloat16)


def upper():
    return lax.div(place(), 2)


def edge_kernel(own, *refs):
    *sources, big, small = refs
    rows = small.shape[0]
    core = lax.rem(place(), 2)
    keys_big = upper() == (1 if own else 0)
    for pair in range(len(sources) // 2):
        to = slice(pair * HD, (pair + 1) * HD)
        for ref, at_core in ((sources[2 * pair], core), (sources[2 * pair + 1], 1 - core)):
            at = pl.ds(pl.multiple_of(at_core * rows, rows), rows)

            @pl.when(keys_big)
            def _():
                big[at, to] = ref[:, :HD]

                @pl.when(at_core == 0)
                def _():
                    small[:, to] = ref[:, HD:]

            @pl.when(jnp.logical_not(keys_big))
            def _():
                big[at, to] = ref[:, HD:]

                @pl.when(at_core == 1)
                def _():
                    small[:, to] = ref[:, :HD]


def offset_of(row, shift, total):
    return lax.rem(row - shift + 2 * total, total)


def key_place(row, rows, shift, keep_ref, total):
    base = offset_of(row, shift, total)
    nblk = keep_ref.shape[1]
    raw = base + lax.broadcasted_iota(jnp.int32, (rows, HD), 0)
    b0 = base // BLOCK
    kept = jnp.full((rows, HD), keep_ref[0, b0], jnp.int32)
    for more in range(1, rows // BLOCK + 1):
        flag = keep_ref[0, lax.rem(b0 + more, nblk)]
        kept = jnp.where(raw >= (b0 + more) * BLOCK, flag, kept)
    where = jnp.where(raw >= total, raw - total, raw)
    return jnp.where(kept > 0, where, FAR)


def query_place(row, rows, shift, len_ref, total):
    base = offset_of(row, shift, total)
    raw = base + lax.broadcasted_iota(jnp.int32, (1, rows), 1)
    where = jnp.where(raw >= total, raw - total, raw)
    begin = jnp.zeros((1, rows), jnp.int32)
    end = jnp.int32(0)
    for u in range(len_ref.shape[1]):
        length = len_ref[0, u]
        end = end + length
        begin = begin + jnp.where(where >= end, length, 0)
    return where, begin


def after(value, *earlier):
    return lax.optimization_barrier((value, *earlier))[0]


def tile_terms(k, v, q_t, o_t, kpos, qpos, qbegin):
    y = nn(k, q_t) * (0.5 * ALPHA)
    t = jnp.tanh(y)
    u = 1.0 + t
    kpos = jnp.concatenate([kpos] * (q_t.shape[1] // HD), axis=1)
    valid = (kpos >= qbegin) & (kpos <= qpos)
    att = jnp.where(valid, y * u, 0.0).astype(jnp.bfloat16)
    slope = u * (1.0 + y * (1.0 - t))
    ds = jnp.where(valid, nn(v, o_t) * slope, 0.0).astype(jnp.bfloat16)
    return att, ds


def cross_pairs(
    own, len_ref, shift_ref, keep_ref, k_ref, q_ref, v_ref, o_ref, big, small,
    out_t, dq_t, dk, dv,
):
    rows = small.shape[0]
    span = GROUP - 1
    total = rows * lax.axis_size("ctx")
    shift = shift_ref[0]
    base = (lax.axis_index("ctx") // GROUP) * (GROUP * rows)

    def shard(j):
        return slice(j * rows, (j + 1) * rows)

    def load(ref, j):
        return ref[shard(j), :HD], ref[shard(j), HD:]

    def before(ref, first, reached):
        q_ts = [q_ref[shard(j), :].T for j in range(max(reached) + 1)]
        o_ts = [o_ref[shard(j), :].T for j in range(max(reached) + 1)]
        for p in reached:
            k, v = load(ref, p - first)
            k_t, v_t = k.T, v.T
            kpos = key_place(base + (p - span) * rows, rows, shift, keep_ref, total)
            for qt in range(p + 1):
                place_q = query_place(base + qt * rows, rows, shift, len_ref, total)
                att, ds = tile_terms(k, v, q_ts[qt], o_ts[qt], kpos, *place_q)
                out_t[:, shard(qt)] += nn(v_t, att)
                dq_t[:, shard(qt)] += nn(k_t, ds)

    def behind(ref, first, reached):
        for n in reached:
            q, o = load(ref, n - first)
            q_t, o_t = q.T, o.T
            place_q = query_place(base + (GROUP + n) * rows, rows, shift, len_ref, total)
            for kt in range(n + 1, GROUP):
                kpos = key_place(base + kt * rows, rows, shift, keep_ref, total)
                att, ds = tile_terms(
                    k_ref[shard(kt), :], v_ref[shard(kt), :], q_t, o_t, kpos, *place_q
                )
                dv[shard(kt), :] += nn(att, o)
                dk[shard(kt), :] += nn(ds, q)

    keys_big = upper() == (1 if own else 0)

    @pl.when(keys_big)
    def _():
        before(big, 1, range(1, span))
        behind(small, span - 1, [span - 1])

    @pl.when(jnp.logical_not(keys_big))
    def _():
        before(small, 0, [0])
        behind(big, 0, range(span - 1))


def inner_kernel(
    len_ref, shift_ref, keep_ref, a0, a1, a2, a3, b0, b1, b2, b3, big, small,
    k_ref, q_ref, v_ref, o_ref, out_t, dq_t, dk, dv,
):
    rows = a0.shape[0]
    total = rows * lax.axis_size("ctx")
    shift = shift_ref[0]
    base = (lax.axis_index("ctx") // GROUP) * (GROUP * rows)
    me = place()
    for i, (kq, vo) in enumerate(((a0, b0), (a1, b1), (a2, b2), (a3, b3))):
        at = pl.ds(pl.multiple_of((me ^ i) * rows, rows), rows)
        k_ref[at, :] = kq[:, :HD]
        q_ref[at, :] = kq[:, HD:]
        v_ref[at, :] = vo[:, :HD]
        o_ref[at, :] = vo[:, HD:]
    shards = [slice(j * rows, (j + 1) * rows) for j in range(GROUP)]
    places = [query_place(base + j * rows, rows, shift, len_ref, total) for j in range(GROUP)]
    q_ts = [q_ref[at, :].T for at in shards]
    o_ts = [o_ref[at, :].T for at in shards]
    for kt, at in enumerate(shards):
        k, v = k_ref[at, :], v_ref[at, :]
        k_t, v_t = k.T, v.T
        kpos = key_place(base + kt * rows, rows, shift, keep_ref, total)
        dk_sum, dv_sum = 0.0, 0.0
        for qt in range(kt, GROUP):
            qs = shards[qt]
            att, ds = tile_terms(k, v, q_ts[qt], o_ts[qt], kpos, *places[qt])
            if kt == 0:
                out_t[:, qs] = nn(v_t, att)
                dq_t[:, qs] = nn(k_t, ds)
            else:
                out_t[:, qs] += nn(v_t, att)
                dq_t[:, qs] += nn(k_t, ds)
            dv_sum = dv_sum + nn(att, o_ref[qs, :])
            dk_sum = dk_sum + nn(ds, q_ref[qs, :])
        dk[at, :] = dk_sum
        dv[at, :] = dv_sum
    cross_pairs(
        True, len_ref, shift_ref, keep_ref, k_ref, q_ref, v_ref, o_ref, big, small,
        out_t, dq_t, dk, dv,
    )


def outer_kernel(
    len_ref, shift_ref, keep_ref, k_ref, q_ref, v_ref, o_ref, big, small, *refs
):
    out_t, dq_t, dk, dv, s0, s1, s2, s3, dqk = refs[4:]
    cross_pairs(
        False, len_ref, shift_ref, keep_ref, k_ref, q_ref, v_ref, o_ref, big, small,
        out_t, dq_t, dk, dv,
    )
    rows = small.shape[0]
    me = place()
    factor = 0.5 * SCALE * ALPHA
    dqk[:HD, :] = (dq_t[...] * factor).astype(jnp.bfloat16)
    for j in range(GROUP):
        dqk[HD:, slice(j * rows, (j + 1) * rows)] = (dk[slice(j * rows, (j + 1) * rows), :] * factor).T.astype(jnp.bfloat16)
    for i, ref in enumerate((s0, s1, s2, s3)):
        at = pl.ds(pl.multiple_of((me ^ i) * rows, rows), rows)
        ref[:, :HD] = (out_t[:, at] * SCALE).T.astype(jnp.bfloat16)
        ref[:, HD:] = (dv[at, :] * SCALE).astype(jnp.bfloat16)


def terms_of(dqk, e0, e1, e2, e3):
    rows = e0.shape[0]
    me = place()
    total = None
    for k, ref in enumerate((e0, e1, e2, e3)):
        at = pl.ds(pl.multiple_of((me ^ k) * rows, rows), rows)
        part = nn(dqk[:, at], ref[...])
        total = part if total is None else total + part
    return total


def terms_kernel(dqk, e0, e1, e2, e3, whole):
    whole[...] = terms_of(dqk, e0, e1, e2, e3)


def half_terms_kernel(same, dqk, e0, e1, e2, e3, out):
    rows = e0.shape[0]
    me = place()
    y = lax.axis_index("dp")
    half = y if same else 1 - y
    width = out.shape[1]
    high = dqk.shape[0]
    count = out.shape[0] // high
    for z in range(0, count, 2):
        cols = [pl.ds(pl.multiple_of((2 * (z + i) + half) * width, width), width) for i in (0, 1)]
        total = 0.0
        for k, ref in enumerate((e0, e1, e2, e3)):
            at = pl.ds(pl.multiple_of((me ^ k) * rows, rows), rows)
            piece = jnp.concatenate([ref[:, cols[0]], ref[:, cols[1]]], axis=1)
            total = total + nn(dqk[:, at], piece)
        out[z * high : (z + 1) * high, :] = total[:, :width].astype(out.dtype)
        out[(z + 1) * high : (z + 2) * high, :] = total[:, width:].astype(out.dtype)


def pair_sum_kernel(mine, other, *outs):
    planes = lax.axis_size("ctx") // GROUP
    z = lax.axis_index("ctx") // GROUP
    high = outs[0].shape[0]
    for dz, ref in enumerate(outs):
        at = pl.ds(pl.multiple_of(lax.rem(z + dz, planes) * high, high), high)
        ref[...] = (mine[at, :] + other[at, :].astype(jnp.float32)).astype(ref.dtype)


def sum_kernel(*refs):
    ins, (near, far, hold) = refs[:-3], refs[-3:]
    total = ins[0][...].astype(jnp.float32)
    for ref in ins[1:]:
        total = total + ref[...].astype(jnp.float32)
    hold[...] = total.T
    share = near.shape[0]
    core = lax.rem(lax.axis_index("ctx"), 2)
    near[...] = hold[pl.ds(pl.multiple_of(core * share, share), share), :].astype(jnp.bfloat16)
    far[...] = hold[pl.ds(pl.multiple_of((1 - core) * share, share), share), :].astype(jnp.bfloat16)


def finish_kernel(r00, r01, r10, r11, gq, gk):
    y = lax.axis_index("dp")
    core = lax.rem(lax.axis_index("ctx"), 2)
    for (a, b), ref in zip(((0, 0), (0, 1), (1, 0), (1, 1)), (r00, r01, r10, r11)):
        cols = head_cols(2 * (y ^ a) + (core ^ b))
        gq[:, cols] = ref[:, :HD]
        gk[:, cols] = ref[:, HD:]


def merge_kernel(i0, i1, i2, i3, first, second):
    me = place()
    for k, ref in enumerate((i0, i1, i2, i3)):
        cols = head_cols(me ^ k)
        first[:, cols] = ref[:, :HD]
        second[:, cols] = ref[:, HD:]


def direct_reduce(dqk, gathered, share, early, late):
    count = lax.axis_size("ctx")
    planes = count // GROUP
    width = gathered[0].shape[1]
    block = width // (2 * planes)
    shape = (2 * HD * planes, block)
    args = (dqk, *gathered)
    (give,) = call(functools.partial(half_terms_kernel, False), [like(*shape)], args, busy=1)
    (keep,) = call(
        functools.partial(half_terms_kernel, True), [like(*shape, jnp.float32)], args, busy=1
    )
    got = lax.ppermute(give, "dp", [(0, 1), (1, 0)])
    sends = call(
        pair_sum_kernel,
        [like(2 * HD, block, jnp.float32)] + [like(2 * HD, block)] * (planes - 1),
        (keep, after(got, *early)),
    )
    arrived = [after(sends[0], *late)] + [around(sends[dz], dz, dz) for dz in range(1, planes)]
    near, far = call(
        sum_kernel,
        [like(share, 2 * HD)] * 2,
        arrived,
        scratch=[pltpu.VMEM((block, 2 * HD), jnp.float32)],
    )
    received = []
    for a in range(2):
        for b in range(2):
            pairs = []
            for y in range(2):
                for i in range(count):
                    z, x, c = i // 4, (i // 2) % 2, i % 2
                    pairs.append((y * count + i, (x ^ a) * count + 4 * z + 2 * y + (c ^ b)))
            received.append(lax.ppermute((near, far)[b], ("dp", "ctx"), pairs))
    return call(finish_kernel, [like(share, GROUP * HD)] * 2, received)


def general_reduce(dqk, gathered, share, early, late):
    count = lax.axis_size("ctx")
    planes = count // GROUP
    width = gathered[0].shape[1]
    (whole,) = call(
        terms_kernel, [like(2 * HD, width, jnp.float32)], (dqk, *gathered), busy=2
    )
    whole = lax.psum(whole.T, "dp")
    same_head = [[g * GROUP + j for g in range(planes)] for j in range(GROUP)]
    plane = [[g * GROUP + j for j in range(GROUP)] for g in range(planes)]
    part = lax.psum_scatter(
        whole, "ctx", scatter_dimension=0, axis_index_groups=same_head, tiled=True
    ).astype(jnp.bfloat16)
    part = lax.all_to_all(
        part.reshape(GROUP, share, 2 * HD), "ctx", 0, 0, axis_index_groups=plane, tiled=True
    )
    part = jnp.moveaxis(part.reshape(GROUP, share, 2, HD), 0, 2)
    return part[:, 0].reshape(share, GROUP * HD), part[:, 1].reshape(share, GROUP * HD)


def body(events, w_query, w_key, values, grad_out, lengths, stream_shift, block_keep):
    rows, width = events.shape[1:]
    features = w_query.shape[1]
    count = lax.axis_size("ctx")
    local = events[0]
    all_rows = GROUP * rows
    pair = like(rows, 2 * HD)
    full = like(all_rows, HD)

    e1 = partner(local, 1)
    e2 = partner(local, 2)
    *vo, weights = call(
        fetch_kernel,
        [pair] * GROUP + [like(width, 2 * HD)],
        [
            pltpu.with_memory_space_constraint(a, pltpu.HBM)
            for a in (values[0], grad_out[0], w_key, w_query)
        ],
        specs=[HBM] * 4,
        scratch=[pltpu.SemaphoreType.DMA((2 * GROUP + 2,))],
    )
    vo = (vo[0],) + tuple(partner(vo[k], k) for k in range(1, GROUP))
    edges = [like(2 * rows, 2 * HD), pair]
    own_edge, other_edge = (functools.partial(edge_kernel, flag) for flag in (True, False))
    kq = call(project_kernel, [pair] * 2, (local, e1, weights), busy=3)
    big, small = call(own_edge, edges, (*kq, *vo[:2]))
    own = around(big, -1, 1), around(small, 1, -1)
    e3 = partner(after(e2, *own, *vo[2:]), 1)
    kq = kq + call(project_kernel, [pair] * 2, (e2, e3, weights), busy=3)
    big, small = call(other_edge, edges, (*kq[2:], *vo[2:]))
    other = around(big, 1, -1), around(small, -1, 1)

    info = (lengths, stream_shift, block_keep)
    wide, tall = like(HD, all_rows, jnp.float32), like(all_rows, HD, jnp.float32)
    sums = [wide, wide, tall, tall]
    k, q, v, o, *held = call(
        inner_kernel,
        [full] * 4 + sums,
        (*info, *kq, *vo, *own),
        specs=[SMEM] * 3 + [VMEM] * 10,
        busy=15,
    )
    *_, p0, p1, p2, p3, dqk = call(
        outer_kernel,
        sums + [pair] * GROUP + [like(2 * HD, all_rows)],
        (*info, k, q, v, o, *other, *held),
        specs=[SMEM] * 3 + [VMEM] * 10,
        aliases={9: 0, 10: 1, 11: 2, 12: 3},
        busy=6,
    )
    parts = (p0, p1, p2, p3)
    parts = (parts[0],) + tuple(partner(parts[k], k) for k in range(1, GROUP))
    merged = call(merge_kernel, [like(rows, features)] * 2, parts)
    share = width // count
    reduce = direct_reduce if lax.axis_size("dp") == 2 and count == 16 else general_reduce
    grad_wq, grad_wk = reduce(dqk, (local, e1, e2, e3), share, parts[1:3], merged)
    attended, grad_values = merged
    return (attended[None], grad_values[None], grad_wq, grad_wk)


def solution(mesh):
    placed = (
        P("dp", "ctx", None),
        P(),
        P(),
        P("dp", "ctx", None),
        P("dp", "ctx", None),
        P("dp", None),
        P("dp"),
        P("dp", None),
    )
    return jax.shard_map(
        body,
        mesh=mesh,
        in_specs=placed,
        out_specs=(P("dp", "ctx", None), P("dp", "ctx", None), P("ctx", None), P("ctx", None)),
        check_vma=False,
    )
```

```python
import functools

import jax
import jax.numpy as jnp
from jax import lax
from jax.experimental import pallas as pl
from jax.experimental.pallas import tpu as pltpu
from jax.sharding import PartitionSpec as P

HD = 128
BLOCK = 128
MAXLEN = 768
GROUP = 4
FAR = 1 << 30
PEAK = 1.15e9
ALPHA = 1.0 / HD**0.5
SCALE = 1.0 / MAXLEN**0.5
VMEM = pl.BlockSpec(memory_space=pltpu.VMEM)
HBM = pl.BlockSpec(memory_space=pltpu.HBM)
SMEM = pl.BlockSpec(memory_space=pltpu.SMEM)


def call(kernel, outs, args, specs=None, busy=0.5, scratch=(), aliases=None):
    return pl.pallas_call(
        kernel,
        out_shape=tuple(outs),
        in_specs=specs or [VMEM] * len(args),
        out_specs=tuple([VMEM] * len(outs)),
        scratch_shapes=scratch,
        input_output_aliases=aliases or {},
        compiler_params=pltpu.CompilerParams(vmem_limit_bytes=24 * 1024 * 1024),
        cost_estimate=pl.CostEstimate(
            flops=int(busy * PEAK), bytes_accessed=0, transcendentals=0
        ),
    )(*args)


def like(rows, cols, dtype=jnp.bfloat16):
    return jax.ShapeDtypeStruct((rows, cols), dtype)


def partner(value, steps):
    count = lax.axis_size("ctx")
    return lax.ppermute(value, "ctx", [(i, i ^ steps) for i in range(count)])


def around(value, low, high):
    count = lax.axis_size("ctx")
    pairs = []
    for i in range(count):
        planes = low if i % GROUP < GROUP // 2 else high
        pairs.append((i, (i + planes * GROUP) % count))
    return lax.ppermute(value, "ctx", pairs)


def place():
    return lax.rem(lax.axis_index("ctx"), GROUP)


def paired():
    return lax.axis_size("dp") == 2 and lax.axis_size("ctx") == 16


def head():
    return place() ^ (2 * lax.axis_index("dp")) if paired() else place()


def head_cols(h):
    return pl.ds(pl.multiple_of(h * HD, HD), HD)


def nn(a, b):
    return jnp.dot(a, b, preferred_element_type=jnp.float32)


def fetch_kernel(a_ref, b_ref, wk_ref, wq_ref, *refs):
    own, near, far, weights, sems = refs
    mine = head()
    copies = []
    for k in range(2):
        for side, ref in enumerate((wk_ref, wq_ref)):
            to = slice((2 * k + side) * HD, (2 * k + side + 1) * HD)
            copies.append((ref.at[:, head_cols(mine ^ k)], weights.at[:, to]))
    for k, (out, at) in enumerate(((own, 0), (near, 0), (far, 0), (far, 2))):
        for side, ref in enumerate((a_ref, b_ref)):
            to = slice((at + side) * HD, (at + side + 1) * HD)
            copies.append((ref.at[:, head_cols(mine ^ k)], out.at[:, to]))
    started = [pltpu.make_async_copy(*pair, sems.at[i]) for i, pair in enumerate(copies)]
    for copy in started:
        copy.start()
    for copy in started:
        copy.wait()


def project_kernel(near, far, weights, near_kq, far_kq):
    own = weights[:, : 2 * HD]
    near_kq[...] = nn(near[...], own).astype(jnp.bfloat16)
    far_kq[...] = nn(far[...], own).astype(jnp.bfloat16)


def project_both_kernel(rows_ref, weights, own_kq, other_kq):
    both = nn(rows_ref[...], weights[...]).astype(jnp.bfloat16)
    own_kq[...] = both[:, : 2 * HD]
    other_kq[...] = both[:, 2 * HD :]


def upper():
    return lax.div(place(), 2)


def edge_kernel(own, *refs):
    *sources, big, small = refs
    rows = small.shape[0]
    core = lax.rem(place(), 2)
    keys_big = upper() == (1 if own else 0)
    for pair in range(len(sources) // 2):
        to = slice(pair * HD, (pair + 1) * HD)
        for i, at_core in ((0, core), (1, 1 - core)):
            ref = sources[2 * pair + i]
            if ref.shape[1] > 2 * HD:
                ref = ref.at[:, 2 * i * HD : 2 * (i + 1) * HD]
            at = pl.ds(pl.multiple_of(at_core * rows, rows), rows)

            @pl.when(keys_big)
            def _():
                big[at, to] = ref[:, :HD]

                @pl.when(at_core == 0)
                def _():
                    small[:, to] = ref[:, HD:]

            @pl.when(jnp.logical_not(keys_big))
            def _():
                big[at, to] = ref[:, HD:]

                @pl.when(at_core == 1)
                def _():
                    small[:, to] = ref[:, :HD]


def offset_of(row, shift, total):
    return lax.rem(row - shift + 2 * total, total)


def key_place(row, rows, shift, keep_ref, total):
    base = offset_of(row, shift, total)
    nblk = keep_ref.shape[1]
    raw = base + lax.broadcasted_iota(jnp.int32, (rows, HD), 0)
    b0 = base // BLOCK
    kept = jnp.full((rows, HD), keep_ref[0, b0], jnp.int32)
    for more in range(1, rows // BLOCK + 1):
        flag = keep_ref[0, lax.rem(b0 + more, nblk)]
        kept = jnp.where(raw >= (b0 + more) * BLOCK, flag, kept)
    where = jnp.where(raw >= total, raw - total, raw)
    return jnp.where(kept > 0, where, FAR)


def query_place(row, rows, shift, len_ref, total):
    base = offset_of(row, shift, total)
    raw = base + lax.broadcasted_iota(jnp.int32, (1, rows), 1)
    where = jnp.where(raw >= total, raw - total, raw)
    begin = jnp.zeros((1, rows), jnp.int32)
    end = jnp.int32(0)
    for u in range(len_ref.shape[1]):
        length = len_ref[0, u]
        end = end + length
        begin = begin + jnp.where(where >= end, length, 0)
    return where, begin


def after(value, *earlier):
    return lax.optimization_barrier((value, *earlier))[0]


def tile_terms(k, v, q_t, o_t, kpos, qpos, qbegin):
    y = nn(k, q_t) * (0.5 * ALPHA)
    t = jnp.tanh(y)
    u = 1.0 + t
    kpos = jnp.concatenate([kpos] * (q_t.shape[1] // HD), axis=1)
    valid = (kpos >= qbegin) & (kpos <= qpos)
    att = jnp.where(valid, y * u, 0.0).astype(jnp.bfloat16)
    slope = u * (1.0 + y * (1.0 - t))
    ds = jnp.where(valid, nn(v, o_t) * slope, 0.0).astype(jnp.bfloat16)
    return att, ds


def cross_pairs(
    own, len_ref, shift_ref, keep_ref, k_ref, q_ref, v_ref, o_ref, big, small,
    out_t, dq_t, dk, dv,
):
    rows = small[0].shape[0]
    span = GROUP - 1
    total = rows * lax.axis_size("ctx")
    shift = shift_ref[0]
    base = plane_base(rows)

    def shard(j):
        return slice(j * rows, (j + 1) * rows)

    def load(refs, j):
        if len(refs) == 1:
            return refs[0][shard(j), :HD], refs[0][shard(j), HD:]
        return refs[0][shard(j), :], refs[1][shard(j), :]

    def before(ref, first, reached):
        q_ts = [q_ref[shard(j), :].T for j in range(max(reached) + 1)]
        o_ts = [o_ref[shard(j), :].T for j in range(max(reached) + 1)]
        for p in reached:
            k, v = load(ref, p - first)
            k_t, v_t = k.T, v.T
            kpos = key_place(base + (p - span) * rows, rows, shift, keep_ref, total)
            for qt in range(p + 1):
                place_q = query_place(base + qt * rows, rows, shift, len_ref, total)
                att, ds = tile_terms(k, v, q_ts[qt], o_ts[qt], kpos, *place_q)
                out_t[:, shard(qt)] += nn(v_t, att)
                dq_t[:, shard(qt)] += nn(k_t, ds)

    def behind(ref, first, reached):
        for n in reached:
            q, o = load(ref, n - first)
            q_t, o_t = q.T, o.T
            place_q = query_place(base + (GROUP + n) * rows, rows, shift, len_ref, total)
            for kt in range(n + 1, GROUP):
                kpos = key_place(base + kt * rows, rows, shift, keep_ref, total)
                att, ds = tile_terms(
                    k_ref[shard(kt), :], v_ref[shard(kt), :], q_t, o_t, kpos, *place_q
                )
                dv[shard(kt), :] += nn(att, o)
                dk[shard(kt), :] += nn(ds, q)

    keys_big = upper() == (1 if own else 0)

    @pl.when(keys_big)
    def _():
        before(big, 1, range(1, span))
        behind(small, span - 1, [span - 1])

    @pl.when(jnp.logical_not(keys_big))
    def _():
        before(small, 0, [0])
        behind(big, 0, range(span - 1))


def square(own_row, shift, total, len_ref, keep_ref, pairs, out_t, dq_t, dk, dv, at):
    rows = pairs[0][0].shape[0]
    q_ts = [q.T for _, q, _, _ in pairs]
    o_ts = [o.T for _, _, _, o in pairs]
    places = [query_place(own_row + i * rows, rows, shift, len_ref, total) for i in (0, 1)]
    for kt, (k, _, v, _) in enumerate(pairs):
        k_t, v_t = k.T, v.T
        kpos = key_place(own_row + kt * rows, rows, shift, keep_ref, total)
        dk_sum, dv_sum = 0.0, 0.0
        for qt in range(kt, 2):
            att, ds = tile_terms(k, v, q_ts[qt], o_ts[qt], kpos, *places[qt])
            if kt == 0:
                out_t[:, at[qt]] = nn(v_t, att)
                dq_t[:, at[qt]] = nn(k_t, ds)
            else:
                out_t[:, at[qt]] += nn(v_t, att)
                dq_t[:, at[qt]] += nn(k_t, ds)
            dv_sum = dv_sum + nn(att, pairs[qt][3])
            dk_sum = dk_sum + nn(ds, pairs[qt][1])
        dk[at[kt], :] = dk_sum
        dv[at[kt], :] = dv_sum


def plane_base(rows):
    return (lax.axis_index("ctx") // GROUP) * (GROUP * rows)


def early_kernel(
    len_ref, shift_ref, keep_ref, a0, a1, b0, b1, out_t, dq_t, dk, dv, kq_ref, vo_ref
):
    rows = a0.shape[0]
    core = lax.rem(place(), 2)
    total = rows * lax.axis_size("ctx")
    for at_core, kq, vo in ((core, a0, b0), (1 - core, a1, b1)):
        at = pl.ds(pl.multiple_of(at_core * rows, rows), rows)
        kq_ref[at, :] = kq[...]
        vo_ref[at, :] = vo[...]
    shards = [slice(0, rows), slice(rows, 2 * rows)]
    pairs = [(kq_ref[i, :HD], kq_ref[i, HD:], vo_ref[i, :HD], vo_ref[i, HD:]) for i in shards]
    own_row = plane_base(rows) + upper() * 2 * rows
    square(
        own_row, shift_ref[0], total, len_ref, keep_ref, pairs, out_t, dq_t, dk, dv, shards
    )


def inner_kernel(
    len_ref, shift_ref, keep_ref, a0, a1, a2, a3, b0, b1, b2, b3, big, small,
    early_out, early_dq, early_dk, early_dv,
    k_ref, q_ref, v_ref, o_ref, out_t, dq_t, dk, dv,
):
    rows = a0.shape[0]
    total = rows * lax.axis_size("ctx")
    shift = shift_ref[0]
    base = plane_base(rows)
    me = place()
    b2, b3 = b2.at[:, : 2 * HD], b3.at[:, 2 * HD :]
    for i, (kq, vo) in enumerate(((a0, b0), (a1, b1), (a2, b2), (a3, b3))):
        at = pl.ds(pl.multiple_of((me ^ i) * rows, rows), rows)
        k_ref[at, :] = kq[:, :HD]
        q_ref[at, :] = kq[:, HD:]
        v_ref[at, :] = vo[:, :HD]
        o_ref[at, :] = vo[:, HD:]
    own = pl.ds(pl.multiple_of(upper() * 2 * rows, 2 * rows), 2 * rows)
    out_t[:, own] = early_out[...]
    dq_t[:, own] = early_dq[...]
    dk[own, :] = early_dk[...]
    dv[own, :] = early_dv[...]
    first = (1 - upper()) * 2 * rows
    others = [pl.ds(pl.multiple_of(first + i * rows, rows), rows) for i in (0, 1)]
    pairs = [(k_ref[at, :], q_ref[at, :], v_ref[at, :], o_ref[at, :]) for at in others]
    square(
        base + first, shift, total, len_ref, keep_ref, pairs, out_t, dq_t, dk, dv, others
    )
    shards = [slice(j * rows, (j + 1) * rows) for j in range(GROUP)]
    half = range(GROUP // 2, GROUP)
    places = {j: query_place(base + j * rows, rows, shift, len_ref, total) for j in half}
    q_ts = {j: q_ref[shards[j], :].T for j in half}
    o_ts = {j: o_ref[shards[j], :].T for j in half}
    for kt in range(GROUP // 2):
        at = shards[kt]
        k, v = k_ref[at, :], v_ref[at, :]
        k_t, v_t = k.T, v.T
        kpos = key_place(base + kt * rows, rows, shift, keep_ref, total)
        dk_sum, dv_sum = 0.0, 0.0
        for qt in half:
            qs = shards[qt]
            att, ds = tile_terms(k, v, q_ts[qt], o_ts[qt], kpos, *places[qt])
            out_t[:, qs] += nn(v_t, att)
            dq_t[:, qs] += nn(k_t, ds)
            dv_sum = dv_sum + nn(att, o_ref[qs, :])
            dk_sum = dk_sum + nn(ds, q_ref[qs, :])
        dk[at, :] += dk_sum
        dv[at, :] += dv_sum
    cross_pairs(
        True, len_ref, shift_ref, keep_ref, k_ref, q_ref, v_ref, o_ref, (big,), (small,),
        out_t, dq_t, dk, dv,
    )


def outer_kernel(
    len_ref, shift_ref, keep_ref, k_ref, q_ref, v_ref, o_ref, big_kq, big_vo, small_kq, small_vo,
    *refs,
):
    out_t, dq_t, dk, dv, s0, s1, s2, s3, dqk = refs[4:]
    cross_pairs(
        False, len_ref, shift_ref, keep_ref, k_ref, q_ref, v_ref, o_ref,
        (big_kq, big_vo), (small_kq, small_vo), out_t, dq_t, dk, dv,
    )
    rows = small_kq.shape[0]
    me = place()
    factor = 0.5 * SCALE * ALPHA
    dqk[:HD, :] = (dq_t[...] * factor).astype(jnp.bfloat16)
    for j in range(GROUP):
        dqk[HD:, slice(j * rows, (j + 1) * rows)] = (dk[slice(j * rows, (j + 1) * rows), :] * factor).T.astype(jnp.bfloat16)
    for i, ref in enumerate((s0, s1, s2, s3)):
        at = pl.ds(pl.multiple_of((me ^ i) * rows, rows), rows)
        ref[:, :HD] = (out_t[:, at] * SCALE).T.astype(jnp.bfloat16)
        ref[:, HD:] = (dv[at, :] * SCALE).astype(jnp.bfloat16)


def terms_of(dqk, e0, e1, e2, e3):
    rows = e0.shape[0]
    me = place()
    total = None
    for k, ref in enumerate((e0, e1, e2, e3)):
        at = pl.ds(pl.multiple_of((me ^ k) * rows, rows), rows)
        part = nn(dqk[:, at], ref[...])
        total = part if total is None else total + part
    return total


def terms_kernel(dqk, e0, e1, e2, e3, whole):
    whole[...] = terms_of(dqk, e0, e1, e2, e3)


def half_terms_kernel(same, dqk, e0, e1, e2, e3, out):
    rows = e0.shape[0]
    me = place()
    half = upper() if same else 1 - upper()
    width = out.shape[1]
    high = dqk.shape[0]
    count = out.shape[0] // high
    for z in range(0, count, 2):
        cols = [pl.ds(pl.multiple_of((2 * (z + i) + half) * width, width), width) for i in (0, 1)]
        total = 0.0
        for k, ref in enumerate((e0, e1, e2, e3)):
            at = pl.ds(pl.multiple_of((me ^ k) * rows, rows), rows)
            piece = jnp.concatenate([ref[:, cols[0]], ref[:, cols[1]]], axis=1)
            total = total + nn(dqk[:, at], piece)
        out[z * high : (z + 1) * high, :] = total[:, :width].astype(out.dtype)
        out[(z + 1) * high : (z + 2) * high, :] = total[:, width:].astype(out.dtype)


def pair_sum_kernel(mine, other, *outs):
    planes = lax.axis_size("ctx") // GROUP
    z = lax.axis_index("ctx") // GROUP
    high = outs[0].shape[0]
    for dz, ref in enumerate(outs):
        at = pl.ds(pl.multiple_of(lax.rem(z + dz, planes) * high, high), high)
        ref[...] = (mine[at, :] + other[at, :].astype(jnp.float32)).astype(ref.dtype)


def sum_kernel(*refs):
    ins, (near, far, hold) = refs[:-3], refs[-3:]
    total = ins[0][...].astype(jnp.float32)
    for ref in ins[1:]:
        total = total + ref[...].astype(jnp.float32)
    hold[...] = total.T
    share = near.shape[0]
    core = lax.rem(lax.axis_index("ctx"), 2)
    near[...] = hold[pl.ds(pl.multiple_of(core * share, share), share), :].astype(jnp.bfloat16)
    far[...] = hold[pl.ds(pl.multiple_of((1 - core) * share, share), share), :].astype(jnp.bfloat16)


def join_kernel(own, other, out):
    core = lax.rem(place(), 2)
    width = own.shape[1]
    out[:, pl.ds(pl.multiple_of(core * width, width), width)] = own[...]
    out[:, pl.ds(pl.multiple_of((1 - core) * width, width), width)] = other[...]


def finish_kernel(own, other, gq, gk):
    first = upper() ^ lax.axis_index("dp")
    for pair, ref in ((first, own), (1 - first, other)):
        for core in range(2):
            cols = head_cols(2 * pair + core)
            gq[:, cols] = ref[:, 2 * core * HD : (2 * core + 1) * HD]
            gk[:, cols] = ref[:, (2 * core + 1) * HD : (2 * core + 2) * HD]


def merge_kernel(i0, i1, i2, i3, first, second):
    mine = head()
    for k, ref in enumerate((i0, i1, i2, i3)):
        cols = head_cols(mine ^ k)
        first[:, cols] = ref[:, :HD]
        second[:, cols] = ref[:, HD:]


def direct_reduce(dqk, gathered, share):
    count = lax.axis_size("ctx")
    planes = count // GROUP
    width = gathered[0].shape[1]
    block = width // (2 * planes)
    shape = (2 * HD * planes, block)
    args = (dqk, *gathered)
    (give,) = call(functools.partial(half_terms_kernel, False), [like(*shape)], args, busy=1)
    (keep,) = call(
        functools.partial(half_terms_kernel, True), [like(*shape, jnp.float32)], args, busy=1
    )
    across = [(y * count + i, (1 - y) * count + (i ^ 2)) for y in range(2) for i in range(count)]
    got = lax.ppermute(give, ("dp", "ctx"), across)
    sends = call(
        pair_sum_kernel,
        [like(2 * HD, block, jnp.float32)] + [like(2 * HD, block)] * (planes - 1),
        (keep, got),
    )
    arrived = [sends[0]] + [around(sends[dz], dz, dz) for dz in range(1, planes)]
    near, far = call(
        sum_kernel,
        [like(share, 2 * HD)] * 2,
        arrived,
        scratch=[pltpu.VMEM((block, 2 * HD), jnp.float32)],
    )
    (both,) = call(join_kernel, [like(share, 4 * HD)], (near, partner(far, 1)), busy=0.1)
    other = lax.ppermute(both, "dp", [(0, 1), (1, 0)])
    return got, call(finish_kernel, [like(share, GROUP * HD)] * 2, (both, other))


def general_reduce(dqk, gathered, share):
    count = lax.axis_size("ctx")
    planes = count // GROUP
    width = gathered[0].shape[1]
    (whole,) = call(
        terms_kernel, [like(2 * HD, width, jnp.float32)], (dqk, *gathered), busy=2
    )
    whole = lax.psum(whole.T, "dp")
    same_head = [[g * GROUP + j for g in range(planes)] for j in range(GROUP)]
    plane = [[g * GROUP + j for j in range(GROUP)] for g in range(planes)]
    part = lax.psum_scatter(
        whole, "ctx", scatter_dimension=0, axis_index_groups=same_head, tiled=True
    ).astype(jnp.bfloat16)
    part = lax.all_to_all(
        part.reshape(GROUP, share, 2 * HD), "ctx", 0, 0, axis_index_groups=plane, tiled=True
    )
    part = jnp.moveaxis(part.reshape(GROUP, share, 2, HD), 0, 2)
    grads = part[:, 0].reshape(share, GROUP * HD), part[:, 1].reshape(share, GROUP * HD)
    return dqk, grads


def body(events, w_query, w_key, values, grad_out, lengths, stream_shift, block_keep):
    rows, width = events.shape[1:]
    features = w_query.shape[1]
    count = lax.axis_size("ctx")
    local = events[0]
    all_rows = GROUP * rows
    pair = like(rows, 2 * HD)
    full = like(all_rows, HD)

    e1 = partner(local, 1)
    e2 = partner(local, 2)
    vo0, vo1, far, weights = call(
        fetch_kernel,
        [pair] * 2 + [like(rows, 4 * HD), like(width, 4 * HD)],
        [
            pltpu.with_memory_space_constraint(a, pltpu.HBM)
            for a in (values[0], grad_out[0], w_key, w_query)
        ],
        specs=[HBM] * 4,
        busy=0.1,
        scratch=[pltpu.SemaphoreType.DMA((12,))],
    )
    vo1 = partner(vo1, 1)
    info = (lengths, stream_shift, block_keep)
    wide, tall = like(HD, all_rows, jnp.float32), like(all_rows, HD, jnp.float32)
    sums = [wide, wide, tall, tall]
    wide, tall = like(HD, 2 * rows, jnp.float32), like(2 * rows, HD, jnp.float32)
    own_edge, other_edge = (functools.partial(edge_kernel, flag) for flag in (True, False))
    kq0, kq1 = call(project_kernel, [pair] * 2, (local, e1, weights), busy=0.1)
    big, small = call(own_edge, [like(2 * rows, 2 * HD), pair], (kq0, kq1, vo0, vo1), busy=0.1)
    own = around(big, -1, 1), around(small, 1, -1)
    early = call(
        early_kernel,
        [wide, wide, tall, tall],
        (*info, after(kq0, small), kq1, vo0, vo1),
        specs=[SMEM] * 3 + [VMEM] * 4,
        busy=0.1,
        scratch=[pltpu.VMEM((2 * rows, 2 * HD), jnp.bfloat16)] * 2,
    )
    vo2 = partner(after(far, *early), 2)
    edges = [like(2 * rows, HD), like(rows, HD)]
    kq2, give = call(project_both_kernel, [pair] * 2, (after(e2, own[1], *early), weights), busy=0.1)
    kq3 = partner(give, 1)
    big, small = call(other_edge, edges, (kq2, kq3), busy=0.1)
    other_kq = around(big, 1, -1), around(small, -1, 1)
    vo3 = partner(after(vo2, own[0], big), 1)
    big, small = call(other_edge, edges, (vo2, vo3), busy=0.1)
    other_vo = around(big, 1, -1), around(small, -1, 1)
    k, q, v, o, *held = call(
        inner_kernel,
        [full] * 4 + sums,
        (*info, kq0, kq1, kq2, kq3, vo0, vo1, vo2, vo3, *own, *early),
        specs=[SMEM] * 3 + [VMEM] * 14,
        busy=15,
    )
    *_, p0, p1, p2, p3, dqk = call(
        outer_kernel,
        sums + [pair] * GROUP + [like(2 * HD, all_rows)],
        (*info, k, q, v, o, other_kq[0], other_vo[0], other_kq[1], other_vo[1], *held),
        specs=[SMEM] * 3 + [VMEM] * 12,
        aliases={11: 0, 12: 1, 13: 2, 14: 3},
        busy=6,
    )
    e3 = partner(after(e2, *held), 1)
    share = width // count
    reduce = direct_reduce if paired() else general_reduce
    reached, (grad_wq, grad_wk) = reduce(dqk, (local, e1, e2, e3), share)
    parts = [partner(after(p, reached), k) for k, p in ((1, p1), (2, p2), (3, p3))]
    attended, grad_values = call(merge_kernel, [like(rows, features)] * 2, (p0, *parts))
    return (attended[None], grad_values[None], grad_wq, grad_wk)


def solution(mesh):
    placed = (
        P("dp", "ctx", None),
        P(),
        P(),
        P("dp", "ctx", None),
        P("dp", "ctx", None),
        P("dp", None),
        P("dp"),
        P("dp", None),
    )
    return jax.shard_map(
        body,
        mesh=mesh,
        in_specs=placed,
        out_specs=(P("dp", "ctx", None), P("dp", "ctx", None), P("ctx", None), P("ctx", None)),
        check_vma=False,
    )
```

```python
import functools

import jax
import jax.numpy as jnp
from jax import lax
from jax.experimental import pallas as pl
from jax.experimental.pallas import tpu as pltpu
from jax.sharding import PartitionSpec as P

HD = 128
BLOCK = 128
MAXLEN = 768
GROUP = 4
FAR = 1 << 30
PEAK = 1.15e9
ALPHA = 1.0 / HD**0.5
SCALE = 1.0 / MAXLEN**0.5
VMEM = pl.BlockSpec(memory_space=pltpu.VMEM)
HBM = pl.BlockSpec(memory_space=pltpu.HBM)
SMEM = pl.BlockSpec(memory_space=pltpu.SMEM)


def call(kernel, outs, args, specs=None, busy=0.5, scratch=(), aliases=None):
    return pl.pallas_call(
        kernel,
        out_shape=tuple(outs),
        in_specs=specs or [VMEM] * len(args),
        out_specs=tuple([VMEM] * len(outs)),
        scratch_shapes=scratch,
        input_output_aliases=aliases or {},
        compiler_params=pltpu.CompilerParams(vmem_limit_bytes=24 * 1024 * 1024),
        cost_estimate=pl.CostEstimate(
            flops=int(busy * PEAK), bytes_accessed=0, transcendentals=0
        ),
    )(*args)


def like(rows, cols, dtype=jnp.bfloat16):
    return jax.ShapeDtypeStruct((rows, cols), dtype)


def partner(value, steps):
    count = lax.axis_size("ctx")
    return lax.ppermute(value, "ctx", [(i, i ^ steps) for i in range(count)])


def around(value, low, high):
    count = lax.axis_size("ctx")
    pairs = []
    for i in range(count):
        planes = low if i % GROUP < GROUP // 2 else high
        pairs.append((i, (i + planes * GROUP) % count))
    return lax.ppermute(value, "ctx", pairs)


def place():
    return lax.rem(lax.axis_index("ctx"), GROUP)


def paired():
    return lax.axis_size("dp") == 2 and lax.axis_size("ctx") == 16


def head():
    return place() ^ (2 * lax.axis_index("dp")) if paired() else place()


def head_cols(h):
    return pl.ds(pl.multiple_of(h * HD, HD), HD)


def nn(a, b):
    return jnp.dot(a, b, preferred_element_type=jnp.float32)


def fetch_kernel(a_ref, b_ref, wk_ref, wq_ref, *refs):
    own, near, far, weights, sems = refs
    mine = head()
    copies = []
    for k in range(2):
        for side, ref in enumerate((wk_ref, wq_ref)):
            to = slice((2 * k + side) * HD, (2 * k + side + 1) * HD)
            copies.append((ref.at[:, head_cols(mine ^ k)], weights.at[:, to]))
    for k, (out, at) in enumerate(((own, 0), (near, 0), (far, 0), (far, 2))):
        for side, ref in enumerate((a_ref, b_ref)):
            to = slice((at + side) * HD, (at + side + 1) * HD)
            copies.append((ref.at[:, head_cols(mine ^ k)], out.at[:, to]))
    started = [pltpu.make_async_copy(*pair, sems.at[i]) for i, pair in enumerate(copies)]
    for copy in started:
        copy.start()
    for copy in started:
        copy.wait()


def project_kernel(near, far, weights, near_kq, far_kq):
    own = weights[:, : 2 * HD]
    near_kq[...] = nn(near[...], own).astype(jnp.bfloat16)
    far_kq[...] = nn(far[...], own).astype(jnp.bfloat16)


def project_both_kernel(rows_ref, weights, own_kq, other_kq):
    both = nn(rows_ref[...], weights[...]).astype(jnp.bfloat16)
    own_kq[...] = both[:, : 2 * HD]
    other_kq[...] = both[:, 2 * HD :]


def upper():
    return lax.div(place(), 2)


def edge_kernel(own, skip, *refs):
    *sources, big, small = refs
    rows = small.shape[0]
    core = lax.rem(place(), 2)
    keys_big = upper() == (1 if own else 0)
    for pair in range(len(sources) // 2):
        to = slice(pair * HD, (pair + 1) * HD)
        to_big = slice((pair - skip) * HD, (pair - skip + 1) * HD)
        for i, at_core in ((0, core), (1, 1 - core)):
            ref = sources[2 * pair + i]
            if ref.shape[1] > 2 * HD:
                ref = ref.at[:, 2 * i * HD : 2 * (i + 1) * HD]
            at = pl.ds(pl.multiple_of(at_core * rows, rows), rows)

            @pl.when(keys_big)
            def _():
                if pair >= skip:
                    big[at, to_big] = ref[:, :HD]

                @pl.when(at_core == 0)
                def _():
                    small[:, to] = ref[:, HD:]

            @pl.when(jnp.logical_not(keys_big))
            def _():
                if pair >= skip:
                    big[at, to_big] = ref[:, HD:]

                @pl.when(at_core == 1)
                def _():
                    small[:, to] = ref[:, :HD]


def offset_of(row, shift, total):
    return lax.rem(row - shift + 2 * total, total)


def key_place(row, rows, shift, keep_ref, total):
    base = offset_of(row, shift, total)
    nblk = keep_ref.shape[1]
    raw = base + lax.broadcasted_iota(jnp.int32, (rows, HD), 0)
    b0 = base // BLOCK
    kept = jnp.full((rows, HD), keep_ref[0, b0], jnp.int32)
    for more in range(1, rows // BLOCK + 1):
        flag = keep_ref[0, lax.rem(b0 + more, nblk)]
        kept = jnp.where(raw >= (b0 + more) * BLOCK, flag, kept)
    where = jnp.where(raw >= total, raw - total, raw)
    return jnp.where(kept > 0, where, FAR)


def query_place(row, rows, shift, len_ref, total):
    base = offset_of(row, shift, total)
    raw = base + lax.broadcasted_iota(jnp.int32, (1, rows), 1)
    where = jnp.where(raw >= total, raw - total, raw)
    begin = jnp.zeros((1, rows), jnp.int32)
    end = jnp.int32(0)
    for u in range(len_ref.shape[1]):
        length = len_ref[0, u]
        end = end + length
        begin = begin + jnp.where(where >= end, length, 0)
    return where, begin


def after(value, *earlier):
    return lax.optimization_barrier((value, *earlier))[0]


def tile_terms(k, v, q_t, o_t, kpos, qpos, qbegin):
    y = nn(k, q_t) * (0.5 * ALPHA)
    t = jnp.tanh(y)
    u = 1.0 + t
    kpos = jnp.concatenate([kpos] * (q_t.shape[1] // HD), axis=1)
    valid = (kpos >= qbegin) & (kpos <= qpos)
    att = jnp.where(valid, y * u, 0.0).astype(jnp.bfloat16)
    slope = u * (1.0 + y * (1.0 - t))
    ds = jnp.where(valid, nn(v, o_t) * slope, 0.0).astype(jnp.bfloat16)
    return att, ds


def cross_pairs(
    own, len_ref, shift_ref, keep_ref, k_ref, q_ref, v_ref, o_ref, big, small,
    out_t, dq_t, dk, dv,
):
    rows = small[0].shape[0]
    span = GROUP - 1
    total = rows * lax.axis_size("ctx")
    shift = shift_ref[0]
    base = plane_base(rows)

    def shard(j):
        return slice(j * rows, (j + 1) * rows)

    def load(refs, j):
        if len(refs) == 1:
            return refs[0][shard(j), :HD], refs[0][shard(j), HD:]
        return refs[0][shard(j), :], refs[1][shard(j), :]

    def before(ref, first, reached):
        q_ts = [q_ref[shard(j), :].T for j in range(max(reached) + 1)]
        o_ts = [o_ref[shard(j), :].T for j in range(max(reached) + 1)]
        for p in reached:
            k, v = load(ref, p - first)
            k_t, v_t = k.T, v.T
            kpos = key_place(base + (p - span) * rows, rows, shift, keep_ref, total)
            for qt in range(p + 1):
                place_q = query_place(base + qt * rows, rows, shift, len_ref, total)
                att, ds = tile_terms(k, v, q_ts[qt], o_ts[qt], kpos, *place_q)
                out_t[:, shard(qt)] += nn(v_t, att)
                dq_t[:, shard(qt)] += nn(k_t, ds)

    def behind(ref, first, reached):
        for n in reached:
            q, o = load(ref, n - first)
            q_t, o_t = q.T, o.T
            place_q = query_place(base + (GROUP + n) * rows, rows, shift, len_ref, total)
            for kt in range(n + 1, GROUP):
                kpos = key_place(base + kt * rows, rows, shift, keep_ref, total)
                att, ds = tile_terms(
                    k_ref[shard(kt), :], v_ref[shard(kt), :], q_t, o_t, kpos, *place_q
                )
                dv[shard(kt), :] += nn(att, o)
                dk[shard(kt), :] += nn(ds, q)

    keys_big = upper() == (1 if own else 0)

    @pl.when(keys_big)
    def _():
        before(big, 1, range(1, span))
        behind(small, span - 1, [span - 1])

    @pl.when(jnp.logical_not(keys_big))
    def _():
        before(small, 0, [0])
        behind(big, 0, range(span - 1))


def square(own_row, shift, total, len_ref, keep_ref, pairs, out_t, dq_t, dk, dv, at):
    rows = pairs[0][0].shape[0]
    q_ts = [q.T for _, q, _, _ in pairs]
    o_ts = [o.T for _, _, _, o in pairs]
    places = [query_place(own_row + i * rows, rows, shift, len_ref, total) for i in (0, 1)]
    for kt, (k, _, v, _) in enumerate(pairs):
        k_t, v_t = k.T, v.T
        kpos = key_place(own_row + kt * rows, rows, shift, keep_ref, total)
        dk_sum, dv_sum = 0.0, 0.0
        for qt in range(kt, 2):
            att, ds = tile_terms(k, v, q_ts[qt], o_ts[qt], kpos, *places[qt])
            if kt == 0:
                out_t[:, at[qt]] = nn(v_t, att)
                dq_t[:, at[qt]] = nn(k_t, ds)
            else:
                out_t[:, at[qt]] += nn(v_t, att)
                dq_t[:, at[qt]] += nn(k_t, ds)
            dv_sum = dv_sum + nn(att, pairs[qt][3])
            dk_sum = dk_sum + nn(ds, pairs[qt][1])
        dk[at[kt], :] = dk_sum
        dv[at[kt], :] = dv_sum


def plane_base(rows):
    return (lax.axis_index("ctx") // GROUP) * (GROUP * rows)


def early_kernel(
    len_ref, shift_ref, keep_ref, a0, a1, b0, b1, out_t, dq_t, dk, dv, kq_ref, vo_ref
):
    rows = a0.shape[0]
    core = lax.rem(place(), 2)
    total = rows * lax.axis_size("ctx")
    for at_core, kq, vo in ((core, a0, b0), (1 - core, a1, b1)):
        at = pl.ds(pl.multiple_of(at_core * rows, rows), rows)
        kq_ref[at, :] = kq[...]
        vo_ref[at, :] = vo[...]
    shards = [slice(0, rows), slice(rows, 2 * rows)]
    pairs = [(kq_ref[i, :HD], kq_ref[i, HD:], vo_ref[i, :HD], vo_ref[i, HD:]) for i in shards]
    own_row = plane_base(rows) + upper() * 2 * rows
    square(
        own_row, shift_ref[0], total, len_ref, keep_ref, pairs, out_t, dq_t, dk, dv, shards
    )


def inner_kernel(
    len_ref, shift_ref, keep_ref, a0, a1, a2, a3, b0, b1, b2, b3, big, small,
    early_out, early_dq, early_dk, early_dv,
    k_ref, q_ref, v_ref, o_ref, out_t, dq_t, dk, dv,
):
    rows = a0.shape[0]
    total = rows * lax.axis_size("ctx")
    shift = shift_ref[0]
    base = plane_base(rows)
    me = place()
    b2, b3 = b2.at[:, : 2 * HD], b3.at[:, 2 * HD :]
    for i, (kq, vo) in enumerate(((a0, b0), (a1, b1), (a2, b2), (a3, b3))):
        at = pl.ds(pl.multiple_of((me ^ i) * rows, rows), rows)
        k_ref[at, :] = kq[:, :HD]
        q_ref[at, :] = kq[:, HD:]
        v_ref[at, :] = vo[:, :HD]
        o_ref[at, :] = vo[:, HD:]
    own = pl.ds(pl.multiple_of(upper() * 2 * rows, 2 * rows), 2 * rows)
    out_t[:, own] = early_out[...]
    dq_t[:, own] = early_dq[...]
    dk[own, :] = early_dk[...]
    dv[own, :] = early_dv[...]
    first = (1 - upper()) * 2 * rows
    others = [pl.ds(pl.multiple_of(first + i * rows, rows), rows) for i in (0, 1)]
    pairs = [(k_ref[at, :], q_ref[at, :], v_ref[at, :], o_ref[at, :]) for at in others]
    square(
        base + first, shift, total, len_ref, keep_ref, pairs, out_t, dq_t, dk, dv, others
    )
    shards = [slice(j * rows, (j + 1) * rows) for j in range(GROUP)]
    half = range(GROUP // 2, GROUP)
    places = {j: query_place(base + j * rows, rows, shift, len_ref, total) for j in half}
    q_ts = {j: q_ref[shards[j], :].T for j in half}
    o_ts = {j: o_ref[shards[j], :].T for j in half}
    for kt in range(GROUP // 2):
        at = shards[kt]
        k, v = k_ref[at, :], v_ref[at, :]
        k_t, v_t = k.T, v.T
        kpos = key_place(base + kt * rows, rows, shift, keep_ref, total)
        dk_sum, dv_sum = 0.0, 0.0
        for qt in half:
            qs = shards[qt]
            att, ds = tile_terms(k, v, q_ts[qt], o_ts[qt], kpos, *places[qt])
            out_t[:, qs] += nn(v_t, att)
            dq_t[:, qs] += nn(k_t, ds)
            dv_sum = dv_sum + nn(att, o_ref[qs, :])
            dk_sum = dk_sum + nn(ds, q_ref[qs, :])
        dk[at, :] += dk_sum
        dv[at, :] += dv_sum
    cross_pairs(
        True, len_ref, shift_ref, keep_ref, k_ref, q_ref, v_ref, o_ref, (big,), (small,),
        out_t, dq_t, dk, dv,
    )


def outer_kernel(
    len_ref, shift_ref, keep_ref, k_ref, q_ref, v_ref, o_ref, big_kq, big_vo, small,
    *refs,
):
    out_t, dq_t, dk, dv, s0, s1, s2, s3, dqk = refs[4:]
    cross_pairs(
        False, len_ref, shift_ref, keep_ref, k_ref, q_ref, v_ref, o_ref,
        (big_kq, big_vo), (small,), out_t, dq_t, dk, dv,
    )
    rows = small.shape[0]
    me = place()
    factor = 0.5 * SCALE * ALPHA
    dqk[:HD, :] = (dq_t[...] * factor).astype(jnp.bfloat16)
    for j in range(GROUP):
        dqk[HD:, slice(j * rows, (j + 1) * rows)] = (dk[slice(j * rows, (j + 1) * rows), :] * factor).T.astype(jnp.bfloat16)
    for i, ref in enumerate((s0, s1, s2, s3)):
        at = pl.ds(pl.multiple_of((me ^ i) * rows, rows), rows)
        ref[:, :HD] = (out_t[:, at] * SCALE).T.astype(jnp.bfloat16)
        ref[:, HD:] = (dv[at, :] * SCALE).astype(jnp.bfloat16)


def terms_of(dqk, e0, e1, e2, e3):
    rows = e0.shape[0]
    me = place()
    total = None
    for k, ref in enumerate((e0, e1, e2, e3)):
        at = pl.ds(pl.multiple_of((me ^ k) * rows, rows), rows)
        part = nn(dqk[:, at], ref[...])
        total = part if total is None else total + part
    return total


def terms_kernel(dqk, e0, e1, e2, e3, whole):
    whole[...] = terms_of(dqk, e0, e1, e2, e3)


def half_terms_kernel(same, dqk, e0, e1, e2, e3, out):
    rows = e0.shape[0]
    me = place()
    half = upper() if same else 1 - upper()
    width = out.shape[1]
    high = dqk.shape[0]
    count = out.shape[0] // high
    for z in range(0, count, 2):
        cols = [pl.ds(pl.multiple_of((2 * (z + i) + half) * width, width), width) for i in (0, 1)]
        total = 0.0
        for k, ref in enumerate((e0, e1, e2, e3)):
            at = pl.ds(pl.multiple_of((me ^ k) * rows, rows), rows)
            piece = jnp.concatenate([ref[:, cols[0]], ref[:, cols[1]]], axis=1)
            total = total + nn(dqk[:, at], piece)
        out[z * high : (z + 1) * high, :] = total[:, :width].astype(out.dtype)
        out[(z + 1) * high : (z + 2) * high, :] = total[:, width:].astype(out.dtype)


def pair_sum_kernel(mine, other, *outs):
    planes = lax.axis_size("ctx") // GROUP
    z = lax.axis_index("ctx") // GROUP
    high = outs[0].shape[0]
    for dz, ref in enumerate(outs):
        at = pl.ds(pl.multiple_of(lax.rem(z + dz, planes) * high, high), high)
        ref[...] = (mine[at, :] + other[at, :].astype(jnp.float32)).astype(ref.dtype)


def sum_kernel(*refs):
    ins, (near, far, hold) = refs[:-3], refs[-3:]
    total = ins[0][...].astype(jnp.float32)
    for ref in ins[1:]:
        total = total + ref[...].astype(jnp.float32)
    hold[...] = total.T
    share = near.shape[0]
    core = lax.rem(lax.axis_index("ctx"), 2)
    near[...] = hold[pl.ds(pl.multiple_of(core * share, share), share), :].astype(jnp.bfloat16)
    far[...] = hold[pl.ds(pl.multiple_of((1 - core) * share, share), share), :].astype(jnp.bfloat16)


def join_kernel(own, other, out):
    core = lax.rem(place(), 2)
    width = own.shape[1]
    out[:, pl.ds(pl.multiple_of(core * width, width), width)] = own[...]
    out[:, pl.ds(pl.multiple_of((1 - core) * width, width), width)] = other[...]


def finish_kernel(own, other, gq, gk):
    first = upper() ^ lax.axis_index("dp")
    for pair, ref in ((first, own), (1 - first, other)):
        for core in range(2):
            cols = head_cols(2 * pair + core)
            gq[:, cols] = ref[:, 2 * core * HD : (2 * core + 1) * HD]
            gk[:, cols] = ref[:, (2 * core + 1) * HD : (2 * core + 2) * HD]


def merge_kernel(i0, i1, i2, i3, first, second):
    mine = head()
    for k, ref in enumerate((i0, i1, i2, i3)):
        cols = head_cols(mine ^ k)
        first[:, cols] = ref[:, :HD]
        second[:, cols] = ref[:, HD:]


def direct_reduce(dqk, gathered, share):
    count = lax.axis_size("ctx")
    planes = count // GROUP
    width = gathered[0].shape[1]
    block = width // (2 * planes)
    shape = (2 * HD * planes, block)
    args = (dqk, *gathered)
    (give,) = call(functools.partial(half_terms_kernel, False), [like(*shape)], args, busy=1)
    (keep,) = call(
        functools.partial(half_terms_kernel, True), [like(*shape, jnp.float32)], args, busy=1
    )
    across = [(y * count + i, (1 - y) * count + (i ^ 2)) for y in range(2) for i in range(count)]
    got = lax.ppermute(give, ("dp", "ctx"), across)
    sends = call(
        pair_sum_kernel,
        [like(2 * HD, block, jnp.float32)] + [like(2 * HD, block)] * (planes - 1),
        (keep, got),
    )
    arrived = [sends[0]] + [around(sends[dz], dz, dz) for dz in range(1, planes)]
    near, far = call(
        sum_kernel,
        [like(share, 2 * HD)] * 2,
        arrived,
        scratch=[pltpu.VMEM((block, 2 * HD), jnp.float32)],
    )
    (both,) = call(join_kernel, [like(share, 4 * HD)], (near, partner(far, 1)), busy=0.1)
    other = lax.ppermute(both, "dp", [(0, 1), (1, 0)])
    return got, call(finish_kernel, [like(share, GROUP * HD)] * 2, (both, other))


def general_reduce(dqk, gathered, share):
    count = lax.axis_size("ctx")
    planes = count // GROUP
    width = gathered[0].shape[1]
    (whole,) = call(
        terms_kernel, [like(2 * HD, width, jnp.float32)], (dqk, *gathered), busy=2
    )
    whole = lax.psum(whole.T, "dp")
    same_head = [[g * GROUP + j for g in range(planes)] for j in range(GROUP)]
    plane = [[g * GROUP + j for j in range(GROUP)] for g in range(planes)]
    part = lax.psum_scatter(
        whole, "ctx", scatter_dimension=0, axis_index_groups=same_head, tiled=True
    ).astype(jnp.bfloat16)
    part = lax.all_to_all(
        part.reshape(GROUP, share, 2 * HD), "ctx", 0, 0, axis_index_groups=plane, tiled=True
    )
    part = jnp.moveaxis(part.reshape(GROUP, share, 2, HD), 0, 2)
    grads = part[:, 0].reshape(share, GROUP * HD), part[:, 1].reshape(share, GROUP * HD)
    return dqk, grads


def body(events, w_query, w_key, values, grad_out, lengths, stream_shift, block_keep):
    rows, width = events.shape[1:]
    features = w_query.shape[1]
    count = lax.axis_size("ctx")
    local = events[0]
    all_rows = GROUP * rows
    pair = like(rows, 2 * HD)
    full = like(all_rows, HD)

    e1 = partner(local, 1)
    e2 = partner(local, 2)
    vo0, vo1, far, weights = call(
        fetch_kernel,
        [pair] * 2 + [like(rows, 4 * HD), like(width, 4 * HD)],
        [
            pltpu.with_memory_space_constraint(a, pltpu.HBM)
            for a in (values[0], grad_out[0], w_key, w_query)
        ],
        specs=[HBM] * 4,
        busy=0.1,
        scratch=[pltpu.SemaphoreType.DMA((12,))],
    )
    vo1 = partner(vo1, 1)
    info = (lengths, stream_shift, block_keep)
    wide, tall = like(HD, all_rows, jnp.float32), like(all_rows, HD, jnp.float32)
    sums = [wide, wide, tall, tall]
    wide, tall = like(HD, 2 * rows, jnp.float32), like(2 * rows, HD, jnp.float32)
    kq0, kq1 = call(project_kernel, [pair] * 2, (local, e1, weights), busy=0.1)
    big, small = call(
        functools.partial(edge_kernel, True, 0),
        [like(2 * rows, 2 * HD), pair],
        (kq0, kq1, vo0, vo1),
        busy=0.1,
    )
    own = around(big, -1, 1), around(small, 1, -1)
    early = call(
        early_kernel,
        [wide, wide, tall, tall],
        (*info, after(kq0, small), kq1, vo0, vo1),
        specs=[SMEM] * 3 + [VMEM] * 4,
        busy=0.1,
        scratch=[pltpu.VMEM((2 * rows, 2 * HD), jnp.bfloat16)] * 2,
    )
    vo2 = partner(after(far, *early), 2)
    kq2, give = call(project_both_kernel, [pair] * 2, (after(e2, own[1], *early), weights), busy=0.1)
    kq3 = partner(give, 1)
    big_kq, _ = call(
        functools.partial(edge_kernel, False, 0),
        [like(2 * rows, HD), like(rows, HD)],
        (kq2, kq3),
        busy=0.1,
    )
    vo3 = partner(after(vo2, own[0], big_kq), 1)
    big_vo, small = call(
        functools.partial(edge_kernel, False, 1),
        [like(2 * rows, HD), pair],
        (kq2, kq3, vo2, vo3),
        busy=0.1,
    )
    other = around(big_kq, 1, -1), around(big_vo, 1, -1), around(small, -1, 1)
    k, q, v, o, *held = call(
        inner_kernel,
        [full] * 4 + sums,
        (*info, kq0, kq1, kq2, kq3, vo0, vo1, vo2, vo3, *own, *early),
        specs=[SMEM] * 3 + [VMEM] * 14,
        busy=15,
    )
    *_, p0, p1, p2, p3, dqk = call(
        outer_kernel,
        sums + [pair] * GROUP + [like(2 * HD, all_rows)],
        (*info, k, q, v, o, *other, *held),
        specs=[SMEM] * 3 + [VMEM] * 11,
        aliases={10: 0, 11: 1, 12: 2, 13: 3},
        busy=6,
    )
    e3 = partner(after(e2, *held), 1)
    share = width // count
    reduce = direct_reduce if paired() else general_reduce
    reached, (grad_wq, grad_wk) = reduce(dqk, (local, e1, e2, e3), share)
    parts = [partner(after(p, reached), k) for k, p in ((1, p1), (2, p2), (3, p3))]
    attended, grad_values = call(merge_kernel, [like(rows, features)] * 2, (p0, *parts))
    return (attended[None], grad_values[None], grad_wq, grad_wk)


def solution(mesh):
    placed = (
        P("dp", "ctx", None),
        P(),
        P(),
        P("dp", "ctx", None),
        P("dp", "ctx", None),
        P("dp", None),
        P("dp"),
        P("dp", None),
    )
    return jax.shard_map(
        body,
        mesh=mesh,
        in_specs=placed,
        out_specs=(P("dp", "ctx", None), P("dp", "ctx", None), P("ctx", None), P("ctx", None)),
        check_vma=False,
    )
```

```python
import functools

import jax
import jax.numpy as jnp
from jax import lax
from jax.experimental import pallas as pl
from jax.experimental.pallas import tpu as pltpu
from jax.sharding import PartitionSpec as P

HD = 128
BLOCK = 128
MAXLEN = 768
GROUP = 4
FAR = 1 << 30
PEAK = 1.15e9
ALPHA = 1.0 / HD**0.5
SCALE = 1.0 / MAXLEN**0.5
VMEM = pl.BlockSpec(memory_space=pltpu.VMEM)
HBM = pl.BlockSpec(memory_space=pltpu.HBM)
SMEM = pl.BlockSpec(memory_space=pltpu.SMEM)


def call(kernel, outs, args, specs=None, busy=0.5, scratch=(), aliases=None):
    return pl.pallas_call(
        kernel,
        out_shape=tuple(outs),
        in_specs=specs or [VMEM] * len(args),
        out_specs=tuple([VMEM] * len(outs)),
        scratch_shapes=scratch,
        input_output_aliases=aliases or {},
        compiler_params=pltpu.CompilerParams(vmem_limit_bytes=24 * 1024 * 1024),
        cost_estimate=pl.CostEstimate(
            flops=int(busy * PEAK), bytes_accessed=0, transcendentals=0
        ),
    )(*args)


def like(rows, cols, dtype=jnp.bfloat16):
    return jax.ShapeDtypeStruct((rows, cols), dtype)


def partner(value, steps):
    count = lax.axis_size("ctx")
    return lax.ppermute(value, "ctx", [(i, i ^ steps) for i in range(count)])


def around(value, low, high):
    count = lax.axis_size("ctx")
    pairs = []
    for i in range(count):
        planes = low if i % GROUP < GROUP // 2 else high
        pairs.append((i, (i + planes * GROUP) % count))
    return lax.ppermute(value, "ctx", pairs)


def place():
    return lax.rem(lax.axis_index("ctx"), GROUP)


def paired():
    return lax.axis_size("dp") == 2 and lax.axis_size("ctx") == 16


def head():
    return place() ^ (2 * lax.axis_index("dp")) if paired() else place()


def head_cols(h):
    return pl.ds(pl.multiple_of(h * HD, HD), HD)


def nn(a, b):
    return jnp.dot(a, b, preferred_element_type=jnp.float32)


def fetch_kernel(a_ref, b_ref, wk_ref, wq_ref, *refs):
    own, near, far, weights, sems = refs
    mine = head()
    copies = []
    for k in range(2):
        for side, ref in enumerate((wk_ref, wq_ref)):
            to = slice((2 * k + side) * HD, (2 * k + side + 1) * HD)
            copies.append((ref.at[:, head_cols(mine ^ k)], weights.at[:, to]))
    for k, (out, at) in enumerate(((own, 0), (near, 0), (far, 0), (far, 2))):
        for side, ref in enumerate((a_ref, b_ref)):
            to = slice((at + side) * HD, (at + side + 1) * HD)
            copies.append((ref.at[:, head_cols(mine ^ k)], out.at[:, to]))
    started = [pltpu.make_async_copy(*pair, sems.at[i]) for i, pair in enumerate(copies)]
    for copy in started:
        copy.start()
    for copy in started:
        copy.wait()


def project_kernel(near, far, weights, near_kq, far_kq):
    own = weights[:, : 2 * HD]
    near_kq[...] = nn(near[...], own).astype(jnp.bfloat16)
    far_kq[...] = nn(far[...], own).astype(jnp.bfloat16)


def project_both_kernel(rows_ref, weights, own_kq, other_kq):
    both = nn(rows_ref[...], weights[...]).astype(jnp.bfloat16)
    own_kq[...] = both[:, : 2 * HD]
    other_kq[...] = both[:, 2 * HD :]


def upper():
    return lax.div(place(), 2)


def edge_kernel(own, skip, *refs):
    *sources, big, small = refs
    rows = small.shape[0]
    if big.shape[0] > 2 * rows:
        big[2 * rows :, :] = jnp.zeros((big.shape[0] - 2 * rows, big.shape[1]), big.dtype)
    core = lax.rem(place(), 2)
    keys_big = upper() == (1 if own else 0)
    for pair in range(len(sources) // 2):
        to = slice(pair * HD, (pair + 1) * HD)
        to_big = slice((pair - skip) * HD, (pair - skip + 1) * HD)
        for i, at_core in ((0, core), (1, 1 - core)):
            ref = sources[2 * pair + i]
            if ref.shape[1] > 2 * HD:
                ref = ref.at[:, : 2 * HD]
            at = pl.ds(pl.multiple_of(at_core * rows, rows), rows)

            @pl.when(keys_big)
            def _():
                if pair >= skip:
                    big[at, to_big] = ref[:, :HD]

                @pl.when(at_core == 0)
                def _():
                    small[:, to] = ref[:, HD:]

            @pl.when(jnp.logical_not(keys_big))
            def _():
                if pair >= skip:
                    big[at, to_big] = ref[:, HD:]

                @pl.when(at_core == 1)
                def _():
                    small[:, to] = ref[:, :HD]


def second_half_kernel(ref, out):
    out[...] = ref[:, out.shape[1] :]


def offset_of(row, shift, total):
    return lax.rem(row - shift + 2 * total, total)


def key_place(row, rows, shift, keep_ref, total):
    base = offset_of(row, shift, total)
    nblk = keep_ref.shape[1]
    raw = base + lax.broadcasted_iota(jnp.int32, (rows, HD), 0)
    b0 = base // BLOCK
    kept = jnp.full((rows, HD), keep_ref[0, b0], jnp.int32)
    for more in range(1, rows // BLOCK + 1):
        flag = keep_ref[0, lax.rem(b0 + more, nblk)]
        kept = jnp.where(raw >= (b0 + more) * BLOCK, flag, kept)
    where = jnp.where(raw >= total, raw - total, raw)
    return jnp.where(kept > 0, where, FAR)


def query_place(row, rows, shift, len_ref, total):
    base = offset_of(row, shift, total)
    raw = base + lax.broadcasted_iota(jnp.int32, (1, rows), 1)
    where = jnp.where(raw >= total, raw - total, raw)
    begin = jnp.zeros((1, rows), jnp.int32)
    end = jnp.int32(0)
    for u in range(len_ref.shape[1]):
        length = len_ref[0, u]
        end = end + length
        begin = begin + jnp.where(where >= end, length, 0)
    return where, begin


def after(value, *earlier):
    return lax.optimization_barrier((value, *earlier))[0]


def tile_terms(k, v, q_t, o_t, kpos, qpos, qbegin):
    y = nn(k, q_t) * (0.5 * ALPHA)
    t = jnp.tanh(y)
    u = 1.0 + t
    kpos = jnp.concatenate([kpos] * (q_t.shape[1] // HD), axis=1)
    valid = (kpos >= qbegin) & (kpos <= qpos)
    att = jnp.where(valid, y * u, 0.0).astype(jnp.bfloat16)
    slope = u * (1.0 + y * (1.0 - t))
    ds = jnp.where(valid, nn(v, o_t) * slope, 0.0).astype(jnp.bfloat16)
    return att, ds


def cross_pairs(
    own, len_ref, shift_ref, keep_ref, k_ref, q_ref, v_ref, o_ref, big, small,
    out_t, dq_t, dk, dv,
):
    rows = small[0].shape[0]
    span = GROUP - 1
    total = rows * lax.axis_size("ctx")
    shift = shift_ref[0]
    base = plane_base(rows)

    def shard(j):
        return slice(j * rows, (j + 1) * rows)

    def load(refs, j):
        if len(refs) == 1:
            return refs[0][shard(j), :HD], refs[0][shard(j), HD:]
        return refs[0][shard(j), :], refs[1][shard(j), :]

    def before(ref, first, reached):
        q_ts = [q_ref[shard(j), :].T for j in range(max(reached) + 1)]
        o_ts = [o_ref[shard(j), :].T for j in range(max(reached) + 1)]
        for p in reached:
            k, v = load(ref, p - first)
            k_t, v_t = k.T, v.T
            kpos = key_place(base + (p - span) * rows, rows, shift, keep_ref, total)
            for qt in range(p + 1):
                place_q = query_place(base + qt * rows, rows, shift, len_ref, total)
                att, ds = tile_terms(k, v, q_ts[qt], o_ts[qt], kpos, *place_q)
                out_t[:, shard(qt)] += nn(v_t, att)
                dq_t[:, shard(qt)] += nn(k_t, ds)

    def behind(ref, first, reached):
        for n in reached:
            q, o = load(ref, n - first)
            q_t, o_t = q.T, o.T
            place_q = query_place(base + (GROUP + n) * rows, rows, shift, len_ref, total)
            for kt in range(n + 1, GROUP):
                kpos = key_place(base + kt * rows, rows, shift, keep_ref, total)
                att, ds = tile_terms(
                    k_ref[shard(kt), :], v_ref[shard(kt), :], q_t, o_t, kpos, *place_q
                )
                dv[shard(kt), :] += nn(att, o)
                dk[shard(kt), :] += nn(ds, q)

    keys_big = upper() == (1 if own else 0)

    @pl.when(keys_big)
    def _():
        before(big, 1, range(1, span))
        behind(small, span - 1, [span - 1])

    @pl.when(jnp.logical_not(keys_big))
    def _():
        before(small, 0, [0])
        behind(big, 0, range(span - 1))


def square(own_row, shift, total, len_ref, keep_ref, pairs, out_t, dq_t, dk, dv, at):
    rows = pairs[0][0].shape[0]
    q_ts = [q.T for _, q, _, _ in pairs]
    o_ts = [o.T for _, _, _, o in pairs]
    places = [query_place(own_row + i * rows, rows, shift, len_ref, total) for i in (0, 1)]
    for kt, (k, _, v, _) in enumerate(pairs):
        k_t, v_t = k.T, v.T
        kpos = key_place(own_row + kt * rows, rows, shift, keep_ref, total)
        dk_sum, dv_sum = 0.0, 0.0
        for qt in range(kt, 2):
            att, ds = tile_terms(k, v, q_ts[qt], o_ts[qt], kpos, *places[qt])
            if kt == 0:
                out_t[:, at[qt]] = nn(v_t, att)
                dq_t[:, at[qt]] = nn(k_t, ds)
            else:
                out_t[:, at[qt]] += nn(v_t, att)
                dq_t[:, at[qt]] += nn(k_t, ds)
            dv_sum = dv_sum + nn(att, pairs[qt][3])
            dk_sum = dk_sum + nn(ds, pairs[qt][1])
        dk[at[kt], :] = dk_sum
        dv[at[kt], :] = dv_sum


def plane_base(rows):
    return (lax.axis_index("ctx") // GROUP) * (GROUP * rows)


def early_kernel(
    len_ref, shift_ref, keep_ref, a0, a1, b0, b1, out_t, dq_t, dk, dv, kq_ref, vo_ref
):
    rows = a0.shape[0]
    core = lax.rem(place(), 2)
    total = rows * lax.axis_size("ctx")
    for at_core, kq, vo in ((core, a0, b0), (1 - core, a1, b1)):
        at = pl.ds(pl.multiple_of(at_core * rows, rows), rows)
        kq_ref[at, :] = kq[...]
        vo_ref[at, :] = vo[...]
    shards = [slice(0, rows), slice(rows, 2 * rows)]
    pairs = [(kq_ref[i, :HD], kq_ref[i, HD:], vo_ref[i, :HD], vo_ref[i, HD:]) for i in shards]
    own_row = plane_base(rows) + upper() * 2 * rows
    square(
        own_row, shift_ref[0], total, len_ref, keep_ref, pairs, out_t, dq_t, dk, dv, shards
    )


def inner_kernel(
    len_ref, shift_ref, keep_ref, a0, a1, a2, a3, b0, b1, b2, b3, big, small,
    early_out, early_dq, early_dk, early_dv,
    k_ref, q_ref, v_ref, o_ref, out_t, dq_t, dk, dv,
):
    rows = a0.shape[0]
    total = rows * lax.axis_size("ctx")
    shift = shift_ref[0]
    base = plane_base(rows)
    me = place()
    b2 = b2.at[:, : 2 * HD]
    for i, (kq, vo) in enumerate(((a0, b0), (a1, b1), (a2, b2), (a3, b3))):
        at = pl.ds(pl.multiple_of((me ^ i) * rows, rows), rows)
        k_ref[at, :] = kq[:, :HD]
        q_ref[at, :] = kq[:, HD:]
        v_ref[at, :] = vo[:, :HD]
        o_ref[at, :] = vo[:, HD:]
    own = pl.ds(pl.multiple_of(upper() * 2 * rows, 2 * rows), 2 * rows)
    out_t[:, own] = early_out[...]
    dq_t[:, own] = early_dq[...]
    dk[own, :] = early_dk[...]
    dv[own, :] = early_dv[...]
    first = (1 - upper()) * 2 * rows
    others = [pl.ds(pl.multiple_of(first + i * rows, rows), rows) for i in (0, 1)]
    pairs = [(k_ref[at, :], q_ref[at, :], v_ref[at, :], o_ref[at, :]) for at in others]
    square(
        base + first, shift, total, len_ref, keep_ref, pairs, out_t, dq_t, dk, dv, others
    )
    shards = [slice(j * rows, (j + 1) * rows) for j in range(GROUP)]
    half = range(GROUP // 2, GROUP)
    places = {j: query_place(base + j * rows, rows, shift, len_ref, total) for j in half}
    q_ts = {j: q_ref[shards[j], :].T for j in half}
    o_ts = {j: o_ref[shards[j], :].T for j in half}
    for kt in range(GROUP // 2):
        at = shards[kt]
        k, v = k_ref[at, :], v_ref[at, :]
        k_t, v_t = k.T, v.T
        kpos = key_place(base + kt * rows, rows, shift, keep_ref, total)
        dk_sum, dv_sum = 0.0, 0.0
        for qt in half:
            qs = shards[qt]
            att, ds = tile_terms(k, v, q_ts[qt], o_ts[qt], kpos, *places[qt])
            out_t[:, qs] += nn(v_t, att)
            dq_t[:, qs] += nn(k_t, ds)
            dv_sum = dv_sum + nn(att, o_ref[qs, :])
            dk_sum = dk_sum + nn(ds, q_ref[qs, :])
        dk[at, :] += dk_sum
        dv[at, :] += dv_sum
    cross_pairs(
        True, len_ref, shift_ref, keep_ref, k_ref, q_ref, v_ref, o_ref, (big,), (small,),
        out_t, dq_t, dk, dv,
    )


def outer_kernel(
    len_ref, shift_ref, keep_ref, k_ref, q_ref, v_ref, o_ref, big_kq, big_vo, small,
    *refs,
):
    out_t, dq_t, dk, dv, s0, s1, s2, s3, dqk = refs[4:]
    cross_pairs(
        False, len_ref, shift_ref, keep_ref, k_ref, q_ref, v_ref, o_ref,
        (big_kq, big_vo), (small,), out_t, dq_t, dk, dv,
    )
    rows = small.shape[0]
    me = place()
    factor = 0.5 * SCALE * ALPHA
    dqk[:HD, :] = (dq_t[...] * factor).astype(jnp.bfloat16)
    for j in range(GROUP):
        dqk[HD:, slice(j * rows, (j + 1) * rows)] = (dk[slice(j * rows, (j + 1) * rows), :] * factor).T.astype(jnp.bfloat16)
    for i, ref in enumerate((s0, s1, s2, s3)):
        at = pl.ds(pl.multiple_of((me ^ i) * rows, rows), rows)
        ref[:, :HD] = (out_t[:, at] * SCALE).T.astype(jnp.bfloat16)
        ref[:, HD:] = (dv[at, :] * SCALE).astype(jnp.bfloat16)


def terms_of(dqk, e0, e1, e2, e3):
    rows = e0.shape[0]
    me = place()
    total = None
    for k, ref in enumerate((e0, e1, e2, e3)):
        at = pl.ds(pl.multiple_of((me ^ k) * rows, rows), rows)
        part = nn(dqk[:, at], ref[...])
        total = part if total is None else total + part
    return total


def terms_kernel(dqk, e0, e1, e2, e3, whole):
    whole[...] = terms_of(dqk, e0, e1, e2, e3)


def half_terms_kernel(same, dqk, e0, e1, e2, e3, out):
    rows = e0.shape[0]
    me = place()
    half = upper() if same else 1 - upper()
    width = out.shape[1]
    high = dqk.shape[0]
    count = out.shape[0] // high
    for z in range(0, count, 2):
        cols = [pl.ds(pl.multiple_of((2 * (z + i) + half) * width, width), width) for i in (0, 1)]
        total = 0.0
        for k, ref in enumerate((e0, e1, e2, e3)):
            at = pl.ds(pl.multiple_of((me ^ k) * rows, rows), rows)
            piece = jnp.concatenate([ref[:, cols[0]], ref[:, cols[1]]], axis=1)
            total = total + nn(dqk[:, at], piece)
        out[z * high : (z + 1) * high, :] = total[:, :width].astype(out.dtype)
        out[(z + 1) * high : (z + 2) * high, :] = total[:, width:].astype(out.dtype)


def pair_sum_kernel(mine, other, *outs):
    planes = lax.axis_size("ctx") // GROUP
    z = lax.axis_index("ctx") // GROUP
    high = outs[0].shape[0]
    for dz, ref in enumerate(outs):
        at = pl.ds(pl.multiple_of(lax.rem(z + dz, planes) * high, high), high)
        ref[...] = (mine[at, :] + other[at, :].astype(jnp.float32)).astype(ref.dtype)


def sum_kernel(*refs):
    ins, (near, far, hold) = refs[:-3], refs[-3:]
    total = ins[0][...].astype(jnp.float32)
    for ref in ins[1:]:
        total = total + ref[...].astype(jnp.float32)
    hold[...] = total.T
    share = near.shape[0]
    core = lax.rem(lax.axis_index("ctx"), 2)
    near[...] = hold[pl.ds(pl.multiple_of(core * share, share), share), :].astype(jnp.bfloat16)
    far[...] = hold[pl.ds(pl.multiple_of((1 - core) * share, share), share), :].astype(jnp.bfloat16)


def join_kernel(own, other, out):
    core = lax.rem(place(), 2)
    width = own.shape[1]
    out[:, pl.ds(pl.multiple_of(core * width, width), width)] = own[...]
    out[:, pl.ds(pl.multiple_of((1 - core) * width, width), width)] = other[...]


def finish_kernel(own, other, gq, gk):
    first = upper() ^ lax.axis_index("dp")
    for pair, ref in ((first, own), (1 - first, other)):
        for core in range(2):
            cols = head_cols(2 * pair + core)
            gq[:, cols] = ref[:, 2 * core * HD : (2 * core + 1) * HD]
            gk[:, cols] = ref[:, (2 * core + 1) * HD : (2 * core + 2) * HD]


def merge_kernel(i0, i1, i2, i3, first, second):
    mine = head()
    for k, ref in enumerate((i0, i1, i2, i3)):
        cols = head_cols(mine ^ k)
        first[:, cols] = ref[:, :HD]
        second[:, cols] = ref[:, HD:]


def direct_reduce(dqk, gathered, share):
    count = lax.axis_size("ctx")
    planes = count // GROUP
    width = gathered[0].shape[1]
    block = width // (2 * planes)
    shape = (2 * HD * planes, block)
    args = (dqk, *gathered)
    (give,) = call(functools.partial(half_terms_kernel, False), [like(*shape)], args, busy=1)
    (keep,) = call(
        functools.partial(half_terms_kernel, True), [like(*shape, jnp.float32)], args, busy=1
    )
    across = [(y * count + i, (1 - y) * count + (i ^ 2)) for y in range(2) for i in range(count)]
    got = lax.ppermute(give, ("dp", "ctx"), across)
    sends = call(
        pair_sum_kernel,
        [like(2 * HD, block, jnp.float32)] + [like(2 * HD, block)] * (planes - 1),
        (keep, got),
    )
    arrived = [sends[0]] + [around(sends[dz], dz, dz) for dz in range(1, planes)]
    near, far = call(
        sum_kernel,
        [like(share, 2 * HD)] * 2,
        arrived,
        scratch=[pltpu.VMEM((block, 2 * HD), jnp.float32)],
    )
    (both,) = call(join_kernel, [like(share, 4 * HD)], (near, partner(far, 1)), busy=0.1)
    other = lax.ppermute(both, "dp", [(0, 1), (1, 0)])
    return got, call(finish_kernel, [like(share, GROUP * HD)] * 2, (both, other))


def general_reduce(dqk, gathered, share):
    count = lax.axis_size("ctx")
    planes = count // GROUP
    width = gathered[0].shape[1]
    (whole,) = call(
        terms_kernel, [like(2 * HD, width, jnp.float32)], (dqk, *gathered), busy=2
    )
    whole = lax.psum(whole.T, "dp")
    same_head = [[g * GROUP + j for g in range(planes)] for j in range(GROUP)]
    plane = [[g * GROUP + j for j in range(GROUP)] for g in range(planes)]
    part = lax.psum_scatter(
        whole, "ctx", scatter_dimension=0, axis_index_groups=same_head, tiled=True
    ).astype(jnp.bfloat16)
    part = lax.all_to_all(
        part.reshape(GROUP, share, 2 * HD), "ctx", 0, 0, axis_index_groups=plane, tiled=True
    )
    part = jnp.moveaxis(part.reshape(GROUP, share, 2, HD), 0, 2)
    grads = part[:, 0].reshape(share, GROUP * HD), part[:, 1].reshape(share, GROUP * HD)
    return dqk, grads


def body(events, w_query, w_key, values, grad_out, lengths, stream_shift, block_keep):
    rows, width = events.shape[1:]
    features = w_query.shape[1]
    count = lax.axis_size("ctx")
    local = events[0]
    all_rows = GROUP * rows
    pair = like(rows, 2 * HD)
    full = like(all_rows, HD)

    e1 = partner(local, 1)
    e2 = partner(local, 2)
    vo0, vo1, far, weights = call(
        fetch_kernel,
        [pair] * 2 + [like(rows, 4 * HD), like(width, 4 * HD)],
        [
            pltpu.with_memory_space_constraint(a, pltpu.HBM)
            for a in (values[0], grad_out[0], w_key, w_query)
        ],
        specs=[HBM] * 4,
        busy=0.1,
        scratch=[pltpu.SemaphoreType.DMA((12,))],
    )
    vo1 = partner(vo1, 1)
    info = (lengths, stream_shift, block_keep)
    wide, tall = like(HD, all_rows, jnp.float32), like(all_rows, HD, jnp.float32)
    sums = [wide, wide, tall, tall]
    wide, tall = like(HD, 2 * rows, jnp.float32), like(2 * rows, HD, jnp.float32)
    kq0, kq1 = call(project_kernel, [pair] * 2, (local, e1, weights), busy=0.1)
    big, small = call(
        functools.partial(edge_kernel, True, 0),
        [like(2 * rows, 2 * HD), pair],
        (kq0, kq1, vo0, vo1),
        busy=0.1,
    )
    own = around(big, -1, 1), around(small, 1, -1)
    early = call(
        early_kernel,
        [wide, wide, tall, tall],
        (*info, after(kq0, small), kq1, vo0, vo1),
        specs=[SMEM] * 3 + [VMEM] * 4,
        busy=0.1,
        scratch=[pltpu.VMEM((2 * rows, 2 * HD), jnp.bfloat16)] * 2,
    )
    vo2 = partner(after(far, *early), 2)
    kq2, give = call(project_both_kernel, [pair] * 2, (after(e2, own[1], *early), weights), busy=0.1)
    kq3 = partner(give, 1)
    big_kq, _ = call(
        functools.partial(edge_kernel, False, 0),
        [like(2 * rows + 64, HD), like(rows, HD)],
        (kq2, kq3),
        busy=0.1,
    )
    (half,) = call(second_half_kernel, [pair], (after(vo2, own[0], big_kq),), busy=0.1)
    vo3 = partner(half, 1)
    big_vo, small = call(
        functools.partial(edge_kernel, False, 1),
        [like(2 * rows, HD), pair],
        (kq2, kq3, vo2, vo3),
        busy=0.1,
    )
    big_kq = around(big_kq, 1, -1)
    kq3 = after(kq3, big_kq)
    other = big_kq, around(big_vo, 1, -1), around(small, -1, 1)
    k, q, v, o, *held = call(
        inner_kernel,
        [full] * 4 + sums,
        (*info, kq0, kq1, kq2, kq3, vo0, vo1, vo2, vo3, *own, *early),
        specs=[SMEM] * 3 + [VMEM] * 14,
        busy=15,
    )
    *_, p0, p1, p2, p3, dqk = call(
        outer_kernel,
        sums + [pair] * GROUP + [like(2 * HD, all_rows)],
        (*info, k, q, v, o, *other, *held),
        specs=[SMEM] * 3 + [VMEM] * 11,
        aliases={10: 0, 11: 1, 12: 2, 13: 3},
        busy=6,
    )
    e3 = partner(after(e2, *held), 1)
    share = width // count
    reduce = direct_reduce if paired() else general_reduce
    reached, (grad_wq, grad_wk) = reduce(dqk, (local, e1, e2, e3), share)
    parts = [partner(after(p, reached), k) for k, p in ((1, p1), (2, p2), (3, p3))]
    attended, grad_values = call(merge_kernel, [like(rows, features)] * 2, (p0, *parts))
    return (attended[None], grad_values[None], grad_wq, grad_wk)


def solution(mesh):
    placed = (
        P("dp", "ctx", None),
        P(),
        P(),
        P("dp", "ctx", None),
        P("dp", "ctx", None),
        P("dp", None),
        P("dp"),
        P("dp", None),
    )
    return jax.shard_map(
        body,
        mesh=mesh,
        in_specs=placed,
        out_specs=(P("dp", "ctx", None), P("dp", "ctx", None), P("ctx", None), P("ctx", None)),
        check_vma=False,
    )
```

```python
import functools

import jax
import jax.numpy as jnp
from jax import lax
from jax.experimental import pallas as pl
from jax.experimental.pallas import tpu as pltpu
from jax.sharding import PartitionSpec as P

HD = 128
BLOCK = 128
MAXLEN = 768
GROUP = 4
FAR = 1 << 30
PEAK = 1.15e9
ALPHA = 1.0 / HD**0.5
SCALE = 1.0 / MAXLEN**0.5
VMEM = pl.BlockSpec(memory_space=pltpu.VMEM)
HBM = pl.BlockSpec(memory_space=pltpu.HBM)
SMEM = pl.BlockSpec(memory_space=pltpu.SMEM)


def call(kernel, outs, args, specs=None, busy=0.5, scratch=(), aliases=None):
    return pl.pallas_call(
        kernel,
        out_shape=tuple(outs),
        in_specs=specs or [VMEM] * len(args),
        out_specs=tuple([VMEM] * len(outs)),
        scratch_shapes=scratch,
        input_output_aliases=aliases or {},
        compiler_params=pltpu.CompilerParams(vmem_limit_bytes=24 * 1024 * 1024),
        cost_estimate=pl.CostEstimate(
            flops=int(busy * PEAK), bytes_accessed=0, transcendentals=0
        ),
    )(*args)


def like(rows, cols, dtype=jnp.bfloat16):
    return jax.ShapeDtypeStruct((rows, cols), dtype)


def partner(value, steps):
    count = lax.axis_size("ctx")
    return lax.ppermute(value, "ctx", [(i, i ^ steps) for i in range(count)])


def around(value, low, high):
    count = lax.axis_size("ctx")
    pairs = []
    for i in range(count):
        planes = low if i % GROUP < GROUP // 2 else high
        pairs.append((i, (i + planes * GROUP) % count))
    return lax.ppermute(value, "ctx", pairs)


def place():
    return lax.rem(lax.axis_index("ctx"), GROUP)


def paired():
    return lax.axis_size("dp") == 2 and lax.axis_size("ctx") == 16


def head():
    return place() ^ (2 * lax.axis_index("dp")) if paired() else place()


def head_cols(h):
    return pl.ds(pl.multiple_of(h * HD, HD), HD)


def nn(a, b):
    return jnp.dot(a, b, preferred_element_type=jnp.float32)


def fetch_kernel(a_ref, b_ref, wk_ref, wq_ref, *refs):
    *outs, weights, sems = refs
    mine = head()
    copies = []
    for k in range(2):
        for side, ref in enumerate((wk_ref, wq_ref)):
            to = slice((2 * k + side) * HD, (2 * k + side + 1) * HD)
            copies.append((ref.at[:, head_cols(mine ^ k)], weights.at[:, to]))
    rows = a_ref.shape[0]
    for k, out in enumerate(outs):
        if out.shape[0] > rows:
            out[rows:, :] = jnp.zeros((out.shape[0] - rows, out.shape[1]), out.dtype)
        for side, ref in enumerate((a_ref, b_ref)):
            to = slice(side * HD, (side + 1) * HD)
            copies.append((ref.at[:, head_cols(mine ^ k)], out.at[:rows, to]))
    started = [pltpu.make_async_copy(*pair, sems.at[i]) for i, pair in enumerate(copies)]
    for copy in started:
        copy.start()
    for copy in started:
        copy.wait()


def project_kernel(near, far, weights, near_kq, far_kq):
    own = weights[:, : 2 * HD]
    near_kq[...] = nn(near[...], own).astype(jnp.bfloat16)
    far_kq[...] = nn(far[...], own).astype(jnp.bfloat16)


def project_both_kernel(rows_ref, weights, own_kq, other_kq):
    both = nn(rows_ref[...], weights[...]).astype(jnp.bfloat16)
    own_kq[...] = both[:, : 2 * HD]
    other_kq[...] = both[:, 2 * HD :]


def upper():
    return lax.div(place(), 2)


def edge_kernel(own, skip, *refs):
    *sources, big, small = refs
    rows = small.shape[0]
    if big.shape[0] > 2 * rows:
        big[2 * rows :, :] = jnp.zeros((big.shape[0] - 2 * rows, big.shape[1]), big.dtype)
    core = lax.rem(place(), 2)
    keys_big = upper() == (1 if own else 0)
    for pair in range(len(sources) // 2):
        to = slice(pair * HD, (pair + 1) * HD)
        to_big = slice((pair - skip) * HD, (pair - skip + 1) * HD)
        for i, at_core in ((0, core), (1, 1 - core)):
            ref = sources[2 * pair + i]
            ref = ref.at[:rows, :]
            at = pl.ds(pl.multiple_of(at_core * rows, rows), rows)

            @pl.when(keys_big)
            def _():
                if pair >= skip:
                    big[at, to_big] = ref[:, :HD]

                @pl.when(at_core == 0)
                def _():
                    small[:, to] = ref[:, HD:]

            @pl.when(jnp.logical_not(keys_big))
            def _():
                if pair >= skip:
                    big[at, to_big] = ref[:, HD:]

                @pl.when(at_core == 1)
                def _():
                    small[:, to] = ref[:, :HD]


def offset_of(row, shift, total):
    return lax.rem(row - shift + 2 * total, total)


def key_place(row, rows, shift, keep_ref, total):
    base = offset_of(row, shift, total)
    nblk = keep_ref.shape[1]
    raw = base + lax.broadcasted_iota(jnp.int32, (rows, HD), 0)
    b0 = base // BLOCK
    kept = jnp.full((rows, HD), keep_ref[0, b0], jnp.int32)
    for more in range(1, rows // BLOCK + 1):
        flag = keep_ref[0, lax.rem(b0 + more, nblk)]
        kept = jnp.where(raw >= (b0 + more) * BLOCK, flag, kept)
    where = jnp.where(raw >= total, raw - total, raw)
    return jnp.where(kept > 0, where, FAR)


def query_place(row, rows, shift, len_ref, total):
    base = offset_of(row, shift, total)
    raw = base + lax.broadcasted_iota(jnp.int32, (1, rows), 1)
    where = jnp.where(raw >= total, raw - total, raw)
    begin = jnp.zeros((1, rows), jnp.int32)
    end = jnp.int32(0)
    for u in range(len_ref.shape[1]):
        length = len_ref[0, u]
        end = end + length
        begin = begin + jnp.where(where >= end, length, 0)
    return where, begin


def after(value, *earlier):
    return lax.optimization_barrier((value, *earlier))[0]


def tile_terms(k, v, q_t, o_t, kpos, qpos, qbegin):
    y = nn(k, q_t) * (0.5 * ALPHA)
    t = jnp.tanh(y)
    u = 1.0 + t
    kpos = jnp.concatenate([kpos] * (q_t.shape[1] // HD), axis=1)
    valid = (kpos >= qbegin) & (kpos <= qpos)
    att = jnp.where(valid, y * u, 0.0).astype(jnp.bfloat16)
    slope = u * (1.0 + y * (1.0 - t))
    ds = jnp.where(valid, nn(v, o_t) * slope, 0.0).astype(jnp.bfloat16)
    return att, ds


def cross_pairs(
    own, len_ref, shift_ref, keep_ref, k_ref, q_ref, v_ref, o_ref, big, small,
    out_t, dq_t, dk, dv,
):
    rows = small[0].shape[0]
    span = GROUP - 1
    total = rows * lax.axis_size("ctx")
    shift = shift_ref[0]
    base = plane_base(rows)

    def shard(j):
        return slice(j * rows, (j + 1) * rows)

    def load(refs, j):
        if len(refs) == 1:
            return refs[0][shard(j), :HD], refs[0][shard(j), HD:]
        return refs[0][shard(j), :], refs[1][shard(j), :]

    def before(ref, first, reached):
        q_ts = [q_ref[shard(j), :].T for j in range(max(reached) + 1)]
        o_ts = [o_ref[shard(j), :].T for j in range(max(reached) + 1)]
        for p in reached:
            k, v = load(ref, p - first)
            k_t, v_t = k.T, v.T
            kpos = key_place(base + (p - span) * rows, rows, shift, keep_ref, total)
            for qt in range(p + 1):
                place_q = query_place(base + qt * rows, rows, shift, len_ref, total)
                att, ds = tile_terms(k, v, q_ts[qt], o_ts[qt], kpos, *place_q)
                out_t[:, shard(qt)] += nn(v_t, att)
                dq_t[:, shard(qt)] += nn(k_t, ds)

    def behind(ref, first, reached):
        for n in reached:
            q, o = load(ref, n - first)
            q_t, o_t = q.T, o.T
            place_q = query_place(base + (GROUP + n) * rows, rows, shift, len_ref, total)
            for kt in range(n + 1, GROUP):
                kpos = key_place(base + kt * rows, rows, shift, keep_ref, total)
                att, ds = tile_terms(
                    k_ref[shard(kt), :], v_ref[shard(kt), :], q_t, o_t, kpos, *place_q
                )
                dv[shard(kt), :] += nn(att, o)
                dk[shard(kt), :] += nn(ds, q)

    keys_big = upper() == (1 if own else 0)

    @pl.when(keys_big)
    def _():
        before(big, 1, range(1, span))
        behind(small, span - 1, [span - 1])

    @pl.when(jnp.logical_not(keys_big))
    def _():
        before(small, 0, [0])
        behind(big, 0, range(span - 1))


def square(own_row, shift, total, len_ref, keep_ref, pairs, out_t, dq_t, dk, dv, at):
    rows = pairs[0][0].shape[0]
    q_ts = [q.T for _, q, _, _ in pairs]
    o_ts = [o.T for _, _, _, o in pairs]
    places = [query_place(own_row + i * rows, rows, shift, len_ref, total) for i in (0, 1)]
    for kt, (k, _, v, _) in enumerate(pairs):
        k_t, v_t = k.T, v.T
        kpos = key_place(own_row + kt * rows, rows, shift, keep_ref, total)
        dk_sum, dv_sum = 0.0, 0.0
        for qt in range(kt, 2):
            att, ds = tile_terms(k, v, q_ts[qt], o_ts[qt], kpos, *places[qt])
            if kt == 0:
                out_t[:, at[qt]] = nn(v_t, att)
                dq_t[:, at[qt]] = nn(k_t, ds)
            else:
                out_t[:, at[qt]] += nn(v_t, att)
                dq_t[:, at[qt]] += nn(k_t, ds)
            dv_sum = dv_sum + nn(att, pairs[qt][3])
            dk_sum = dk_sum + nn(ds, pairs[qt][1])
        dk[at[kt], :] = dk_sum
        dv[at[kt], :] = dv_sum


def plane_base(rows):
    return (lax.axis_index("ctx") // GROUP) * (GROUP * rows)


def early_kernel(
    len_ref, shift_ref, keep_ref, a0, a1, b0, b1, out_t, dq_t, dk, dv, kq_ref, vo_ref
):
    rows = a0.shape[0]
    core = lax.rem(place(), 2)
    total = rows * lax.axis_size("ctx")
    for at_core, kq, vo in ((core, a0, b0), (1 - core, a1, b1)):
        at = pl.ds(pl.multiple_of(at_core * rows, rows), rows)
        kq_ref[at, :] = kq[...]
        vo_ref[at, :] = vo[...]
    shards = [slice(0, rows), slice(rows, 2 * rows)]
    pairs = [(kq_ref[i, :HD], kq_ref[i, HD:], vo_ref[i, :HD], vo_ref[i, HD:]) for i in shards]
    own_row = plane_base(rows) + upper() * 2 * rows
    square(
        own_row, shift_ref[0], total, len_ref, keep_ref, pairs, out_t, dq_t, dk, dv, shards
    )


def inner_kernel(
    len_ref, shift_ref, keep_ref, a0, a1, a2, a3, b0, b1, b2, b3,
    early_out, early_dq, early_dk, early_dv,
    k_ref, q_ref, v_ref, o_ref, out_t, dq_t, dk, dv,
):
    rows = a0.shape[0]
    total = rows * lax.axis_size("ctx")
    shift = shift_ref[0]
    base = plane_base(rows)
    me = place()
    b2, b3 = b2.at[:rows, :], b3.at[:rows, :]
    for i, (kq, vo) in enumerate(((a0, b0), (a1, b1), (a2, b2), (a3, b3))):
        at = pl.ds(pl.multiple_of((me ^ i) * rows, rows), rows)
        k_ref[at, :] = kq[:, :HD]
        q_ref[at, :] = kq[:, HD:]
        v_ref[at, :] = vo[:, :HD]
        o_ref[at, :] = vo[:, HD:]
    own = pl.ds(pl.multiple_of(upper() * 2 * rows, 2 * rows), 2 * rows)
    out_t[:, own] = early_out[...]
    dq_t[:, own] = early_dq[...]
    dk[own, :] = early_dk[...]
    dv[own, :] = early_dv[...]
    first = (1 - upper()) * 2 * rows
    others = [pl.ds(pl.multiple_of(first + i * rows, rows), rows) for i in (0, 1)]
    pairs = [(k_ref[at, :], q_ref[at, :], v_ref[at, :], o_ref[at, :]) for at in others]
    square(
        base + first, shift, total, len_ref, keep_ref, pairs, out_t, dq_t, dk, dv, others
    )
    shards = [slice(j * rows, (j + 1) * rows) for j in range(GROUP)]
    half = range(GROUP // 2, GROUP)
    places = {j: query_place(base + j * rows, rows, shift, len_ref, total) for j in half}
    q_ts = {j: q_ref[shards[j], :].T for j in half}
    o_ts = {j: o_ref[shards[j], :].T for j in half}
    for kt in range(GROUP // 2):
        at = shards[kt]
        k, v = k_ref[at, :], v_ref[at, :]
        k_t, v_t = k.T, v.T
        kpos = key_place(base + kt * rows, rows, shift, keep_ref, total)
        dk_sum, dv_sum = 0.0, 0.0
        for qt in half:
            qs = shards[qt]
            att, ds = tile_terms(k, v, q_ts[qt], o_ts[qt], kpos, *places[qt])
            out_t[:, qs] += nn(v_t, att)
            dq_t[:, qs] += nn(k_t, ds)
            dv_sum = dv_sum + nn(att, o_ref[qs, :])
            dk_sum = dk_sum + nn(ds, q_ref[qs, :])
        dk[at, :] += dk_sum
        dv[at, :] += dv_sum


def own_halo_kernel(
    len_ref, shift_ref, keep_ref, k_ref, q_ref, v_ref, o_ref, big, small, *refs
):
    cross_pairs(
        True, len_ref, shift_ref, keep_ref, k_ref, q_ref, v_ref, o_ref, (big,), (small,),
        *refs[4:],
    )


def outer_kernel(
    len_ref, shift_ref, keep_ref, k_ref, q_ref, v_ref, o_ref, big_kq, big_vo, small,
    *refs,
):
    out_t, dq_t, dk, dv, s0, s1, s2, s3, dqk = refs[4:]
    cross_pairs(
        False, len_ref, shift_ref, keep_ref, k_ref, q_ref, v_ref, o_ref,
        (big_kq, big_vo), (small,), out_t, dq_t, dk, dv,
    )
    rows = small.shape[0]
    me = place()
    factor = 0.5 * SCALE * ALPHA
    dqk[:HD, :] = (dq_t[...] * factor).astype(jnp.bfloat16)
    for j in range(GROUP):
        dqk[HD:, slice(j * rows, (j + 1) * rows)] = (dk[slice(j * rows, (j + 1) * rows), :] * factor).T.astype(jnp.bfloat16)
    for i, ref in enumerate((s0, s1, s2, s3)):
        at = pl.ds(pl.multiple_of((me ^ i) * rows, rows), rows)
        ref[:, :HD] = (out_t[:, at] * SCALE).T.astype(jnp.bfloat16)
        ref[:, HD:] = (dv[at, :] * SCALE).astype(jnp.bfloat16)


def terms_of(dqk, e0, e1, e2, e3):
    rows = e0.shape[0]
    me = place()
    total = None
    for k, ref in enumerate((e0, e1, e2, e3)):
        at = pl.ds(pl.multiple_of((me ^ k) * rows, rows), rows)
        part = nn(dqk[:, at], ref[...])
        total = part if total is None else total + part
    return total


def terms_kernel(dqk, e0, e1, e2, e3, whole):
    whole[...] = terms_of(dqk, e0, e1, e2, e3)


def half_terms_kernel(same, dqk, e0, e1, e2, e3, out):
    rows = e0.shape[0]
    me = place()
    half = upper() if same else 1 - upper()
    width = out.shape[1]
    high = dqk.shape[0]
    count = out.shape[0] // high
    for z in range(0, count, 2):
        cols = [pl.ds(pl.multiple_of((2 * (z + i) + half) * width, width), width) for i in (0, 1)]
        total = 0.0
        for k, ref in enumerate((e0, e1, e2, e3)):
            at = pl.ds(pl.multiple_of((me ^ k) * rows, rows), rows)
            piece = jnp.concatenate([ref[:, cols[0]], ref[:, cols[1]]], axis=1)
            total = total + nn(dqk[:, at], piece)
        out[z * high : (z + 1) * high, :] = total[:, :width].astype(out.dtype)
        out[(z + 1) * high : (z + 2) * high, :] = total[:, width:].astype(out.dtype)


def pair_sum_kernel(mine, other, *outs):
    planes = lax.axis_size("ctx") // GROUP
    z = lax.axis_index("ctx") // GROUP
    high = outs[0].shape[0]
    for dz, ref in enumerate(outs):
        at = pl.ds(pl.multiple_of(lax.rem(z + dz, planes) * high, high), high)
        ref[...] = (mine[at, :] + other[at, :].astype(jnp.float32)).astype(ref.dtype)


def sum_kernel(*refs):
    ins, (near, far, hold) = refs[:-3], refs[-3:]
    total = ins[0][...].astype(jnp.float32)
    for ref in ins[1:]:
        total = total + ref[...].astype(jnp.float32)
    hold[...] = total.T
    share = near.shape[0]
    core = lax.rem(lax.axis_index("ctx"), 2)
    near[...] = hold[pl.ds(pl.multiple_of(core * share, share), share), :].astype(jnp.bfloat16)
    far[...] = hold[pl.ds(pl.multiple_of((1 - core) * share, share), share), :].astype(jnp.bfloat16)


def join_kernel(own, other, out):
    core = lax.rem(place(), 2)
    width = own.shape[1]
    out[:, pl.ds(pl.multiple_of(core * width, width), width)] = own[...]
    out[:, pl.ds(pl.multiple_of((1 - core) * width, width), width)] = other[...]


def finish_kernel(own, other, gq, gk):
    first = upper() ^ lax.axis_index("dp")
    for pair, ref in ((first, own), (1 - first, other)):
        for core in range(2):
            cols = head_cols(2 * pair + core)
            gq[:, cols] = ref[:, 2 * core * HD : (2 * core + 1) * HD]
            gk[:, cols] = ref[:, (2 * core + 1) * HD : (2 * core + 2) * HD]


def merge_kernel(i0, i1, i2, i3, first, second):
    mine = head()
    for k, ref in enumerate((i0, i1, i2, i3)):
        cols = head_cols(mine ^ k)
        first[:, cols] = ref[:, :HD]
        second[:, cols] = ref[:, HD:]


def direct_reduce(dqk, gathered, share):
    count = lax.axis_size("ctx")
    planes = count // GROUP
    width = gathered[0].shape[1]
    block = width // (2 * planes)
    shape = (2 * HD * planes, block)
    args = (dqk, *gathered)
    (give,) = call(functools.partial(half_terms_kernel, False), [like(*shape)], args, busy=1)
    (keep,) = call(
        functools.partial(half_terms_kernel, True), [like(*shape, jnp.float32)], args, busy=1
    )
    across = [(y * count + i, (1 - y) * count + (i ^ 2)) for y in range(2) for i in range(count)]
    got = lax.ppermute(give, ("dp", "ctx"), across)
    sends = call(
        pair_sum_kernel,
        [like(2 * HD, block, jnp.float32)] + [like(2 * HD, block)] * (planes - 1),
        (keep, got),
    )
    arrived = [sends[0]] + [around(sends[dz], dz, dz) for dz in range(1, planes)]
    near, far = call(
        sum_kernel,
        [like(share, 2 * HD)] * 2,
        arrived,
        scratch=[pltpu.VMEM((block, 2 * HD), jnp.float32)],
    )
    (both,) = call(join_kernel, [like(share, 4 * HD)], (near, partner(far, 1)), busy=0.1)
    other = lax.ppermute(both, "dp", [(0, 1), (1, 0)])
    return got, call(finish_kernel, [like(share, GROUP * HD)] * 2, (both, other))


def general_reduce(dqk, gathered, share):
    count = lax.axis_size("ctx")
    planes = count // GROUP
    width = gathered[0].shape[1]
    (whole,) = call(
        terms_kernel, [like(2 * HD, width, jnp.float32)], (dqk, *gathered), busy=2
    )
    whole = lax.psum(whole.T, "dp")
    same_head = [[g * GROUP + j for g in range(planes)] for j in range(GROUP)]
    plane = [[g * GROUP + j for j in range(GROUP)] for g in range(planes)]
    part = lax.psum_scatter(
        whole, "ctx", scatter_dimension=0, axis_index_groups=same_head, tiled=True
    ).astype(jnp.bfloat16)
    part = lax.all_to_all(
        part.reshape(GROUP, share, 2 * HD), "ctx", 0, 0, axis_index_groups=plane, tiled=True
    )
    part = jnp.moveaxis(part.reshape(GROUP, share, 2, HD), 0, 2)
    grads = part[:, 0].reshape(share, GROUP * HD), part[:, 1].reshape(share, GROUP * HD)
    return dqk, grads


def body(events, w_query, w_key, values, grad_out, lengths, stream_shift, block_keep):
    rows, width = events.shape[1:]
    features = w_query.shape[1]
    count = lax.axis_size("ctx")
    local = events[0]
    all_rows = GROUP * rows
    pair = like(rows, 2 * HD)
    full = like(all_rows, HD)

    e1 = partner(local, 1)
    e2 = partner(local, 2)
    vo0, vo1, vo2, vo3, weights = call(
        fetch_kernel,
        [pair] * 2 + [like(rows + 32, 2 * HD)] * 2 + [like(width, 4 * HD)],
        [
            pltpu.with_memory_space_constraint(a, pltpu.HBM)
            for a in (values[0], grad_out[0], w_key, w_query)
        ],
        specs=[HBM] * 4,
        busy=0.1,
        scratch=[pltpu.SemaphoreType.DMA((12,))],
    )
    vo1 = partner(vo1, 1)
    info = (lengths, stream_shift, block_keep)
    wide, tall = like(HD, all_rows, jnp.float32), like(all_rows, HD, jnp.float32)
    sums = [wide, wide, tall, tall]
    wide, tall = like(HD, 2 * rows, jnp.float32), like(2 * rows, HD, jnp.float32)
    kq0, kq1 = call(project_kernel, [pair] * 2, (local, e1, weights), busy=0.1)
    big, small = call(
        functools.partial(edge_kernel, True, 0),
        [like(2 * rows, 2 * HD), pair],
        (kq0, kq1, vo0, vo1),
        busy=0.1,
    )
    own = around(big, -1, 1), around(small, 1, -1)
    early = call(
        early_kernel,
        [wide, wide, tall, tall],
        (*info, after(kq0, small), kq1, vo0, vo1),
        specs=[SMEM] * 3 + [VMEM] * 4,
        busy=0.1,
        scratch=[pltpu.VMEM((2 * rows, 2 * HD), jnp.bfloat16)] * 2,
    )
    vo2, vo3 = partner(after(vo2, *early), 2), partner(after(vo3, *early), 3)
    kq2, give = call(project_both_kernel, [pair] * 2, (after(e2, own[1], *early), weights), busy=0.1)
    kq3 = partner(give, 1)
    big_kq, _ = call(
        functools.partial(edge_kernel, False, 0),
        [like(2 * rows + 64, HD), like(rows, HD)],
        (kq2, kq3),
        busy=0.1,
    )
    big_vo, small = call(
        functools.partial(edge_kernel, False, 1),
        [like(2 * rows, HD), pair],
        (kq2, kq3, after(vo2, own[0], big_kq), vo3),
        busy=2,
    )
    big_kq = around(big_kq, 1, -1)
    kq3 = after(kq3, big_vo)
    own0 = after(own[0], big_kq)
    other = big_kq, around(big_vo, 1, -1), around(small, -1, 1)
    k, q, v, o, *held = call(
        inner_kernel,
        [full] * 4 + sums,
        (*info, kq0, kq1, kq2, kq3, vo0, vo1, vo2, vo3, *early),
        specs=[SMEM] * 3 + [VMEM] * 12,
        busy=3,
    )
    held = call(
        own_halo_kernel,
        sums,
        (*info, k, q, v, o, own0, own[1], *held),
        specs=[SMEM] * 3 + [VMEM] * 10,
        aliases={9: 0, 10: 1, 11: 2, 12: 3},
        busy=5,
    )
    *_, p0, p1, p2, p3, dqk = call(
        outer_kernel,
        sums + [pair] * GROUP + [like(2 * HD, all_rows)],
        (*info, k, q, v, o, *other, *held),
        specs=[SMEM] * 3 + [VMEM] * 11,
        aliases={10: 0, 11: 1, 12: 2, 13: 3},
        busy=6,
    )
    e3 = partner(after(e2, *held), 1)
    share = width // count
    reduce = direct_reduce if paired() else general_reduce
    reached, (grad_wq, grad_wk) = reduce(dqk, (local, e1, e2, e3), share)
    parts = [partner(after(p, reached), k) for k, p in ((1, p1), (2, p2), (3, p3))]
    attended, grad_values = call(merge_kernel, [like(rows, features)] * 2, (p0, *parts))
    return (attended[None], grad_values[None], grad_wq, grad_wk)


def solution(mesh):
    placed = (
        P("dp", "ctx", None),
        P(),
        P(),
        P("dp", "ctx", None),
        P("dp", "ctx", None),
        P("dp", None),
        P("dp"),
        P("dp", None),
    )
    return jax.shard_map(
        body,
        mesh=mesh,
        in_specs=placed,
        out_specs=(P("dp", "ctx", None), P("dp", "ctx", None), P("ctx", None), P("ctx", None)),
        check_vma=False,
    )
```

```python
import functools

import jax
import jax.numpy as jnp
from jax import lax
from jax.experimental import pallas as pl
from jax.experimental.pallas import tpu as pltpu
from jax.sharding import PartitionSpec as P

HD = 128
BLOCK = 128
MAXLEN = 768
GROUP = 4
FAR = 1 << 30
PEAK = 1.15e9
ALPHA = 1.0 / HD**0.5
SCALE = 1.0 / MAXLEN**0.5
VMEM = pl.BlockSpec(memory_space=pltpu.VMEM)
HBM = pl.BlockSpec(memory_space=pltpu.HBM)
SMEM = pl.BlockSpec(memory_space=pltpu.SMEM)


def call(kernel, outs, args, specs=None, busy=0.5, scratch=(), aliases=None):
    return pl.pallas_call(
        kernel,
        out_shape=tuple(outs),
        in_specs=specs or [VMEM] * len(args),
        out_specs=tuple([VMEM] * len(outs)),
        scratch_shapes=scratch,
        input_output_aliases=aliases or {},
        compiler_params=pltpu.CompilerParams(vmem_limit_bytes=24 * 1024 * 1024),
        cost_estimate=pl.CostEstimate(
            flops=int(busy * PEAK), bytes_accessed=0, transcendentals=0
        ),
    )(*args)


def like(rows, cols, dtype=jnp.bfloat16):
    return jax.ShapeDtypeStruct((rows, cols), dtype)


def partner(value, steps):
    count = lax.axis_size("ctx")
    return lax.ppermute(value, "ctx", [(i, i ^ steps) for i in range(count)])


def around(value, low, high):
    count = lax.axis_size("ctx")
    pairs = []
    for i in range(count):
        planes = low if i % GROUP < GROUP // 2 else high
        pairs.append((i, (i + planes * GROUP) % count))
    return lax.ppermute(value, "ctx", pairs)


def place():
    return lax.rem(lax.axis_index("ctx"), GROUP)


def paired():
    return lax.axis_size("dp") == 2 and lax.axis_size("ctx") == 16


def head():
    return place() ^ (2 * lax.axis_index("dp")) if paired() else place()


def head_cols(h):
    return pl.ds(pl.multiple_of(h * HD, HD), HD)


def nn(a, b):
    return jnp.dot(a, b, preferred_element_type=jnp.float32)


def fetch_kernel(a_ref, b_ref, wk_ref, wq_ref, *refs):
    *outs, weights, sems = refs
    mine = head()
    copies = []
    for k in range(2):
        for side, ref in enumerate((wk_ref, wq_ref)):
            to = slice((2 * k + side) * HD, (2 * k + side + 1) * HD)
            copies.append((ref.at[:, head_cols(mine ^ k)], weights.at[:, to]))
    for k, out in enumerate(outs):
        for side, ref in enumerate((a_ref, b_ref)):
            to = slice(side * HD, (side + 1) * HD)
            copies.append((ref.at[:, head_cols(mine ^ k)], out.at[:, to]))
    started = [pltpu.make_async_copy(*pair, sems.at[i]) for i, pair in enumerate(copies)]
    for copy in started:
        copy.start()
    for copy in started:
        copy.wait()


def project_kernel(near, far, weights, near_kq, far_kq):
    own = weights[:, : 2 * HD]
    near_kq[...] = nn(near[...], own).astype(jnp.bfloat16)
    far_kq[...] = nn(far[...], own).astype(jnp.bfloat16)


class Sides:
    def __init__(self, left, right):
        self.left, self.right = left, right

    def __getitem__(self, where):
        rows, cols = where
        return (self.right if cols.start == HD else self.left)[rows, :]


def project_both_kernel(rows_ref, weights, own_kq, other_k, other_q):
    both = nn(rows_ref[...], weights[...]).astype(jnp.bfloat16)
    own_kq[...] = both[:, : 2 * HD]
    other_k[...] = both[:, 2 * HD : 3 * HD]
    other_q[...] = both[:, 3 * HD :]


def upper():
    return lax.div(place(), 2)


def edge_kernel(own, skip, *refs):
    *sources, big, small = refs
    if len(sources) % 2:
        sources[1:3] = [Sides(*sources[1:3])]
    rows = small.shape[0]
    if big.shape[0] > 2 * rows:
        big[2 * rows :, :] = jnp.zeros((big.shape[0] - 2 * rows, big.shape[1]), big.dtype)
    core = lax.rem(place(), 2)
    keys_big = upper() == (1 if own else 0)
    for pair in range(len(sources) // 2):
        to = slice(pair * HD, (pair + 1) * HD)
        to_big = slice((pair - skip) * HD, (pair - skip + 1) * HD)
        for i, at_core in ((0, core), (1, 1 - core)):
            ref = sources[2 * pair + i]
            at = pl.ds(pl.multiple_of(at_core * rows, rows), rows)

            @pl.when(keys_big)
            def _():
                if pair >= skip:
                    big[at, to_big] = ref[:, :HD]

                @pl.when(at_core == 0)
                def _():
                    small[:, to] = ref[:, HD:]

            @pl.when(jnp.logical_not(keys_big))
            def _():
                if pair >= skip:
                    big[at, to_big] = ref[:, HD:]

                @pl.when(at_core == 1)
                def _():
                    small[:, to] = ref[:, :HD]


def offset_of(row, shift, total):
    return lax.rem(row - shift + 2 * total, total)


def key_place(row, rows, shift, keep_ref, total):
    base = offset_of(row, shift, total)
    nblk = keep_ref.shape[1]
    raw = base + lax.broadcasted_iota(jnp.int32, (rows, HD), 0)
    b0 = base // BLOCK
    kept = jnp.full((rows, HD), keep_ref[0, b0], jnp.int32)
    for more in range(1, rows // BLOCK + 1):
        flag = keep_ref[0, lax.rem(b0 + more, nblk)]
        kept = jnp.where(raw >= (b0 + more) * BLOCK, flag, kept)
    where = jnp.where(raw >= total, raw - total, raw)
    return jnp.where(kept > 0, where, FAR)


def query_place(row, rows, shift, len_ref, total):
    base = offset_of(row, shift, total)
    raw = base + lax.broadcasted_iota(jnp.int32, (1, rows), 1)
    where = jnp.where(raw >= total, raw - total, raw)
    begin = jnp.zeros((1, rows), jnp.int32)
    end = jnp.int32(0)
    for u in range(len_ref.shape[1]):
        length = len_ref[0, u]
        end = end + length
        begin = begin + jnp.where(where >= end, length, 0)
    return where, begin


def after(value, *earlier):
    return lax.optimization_barrier((value, *earlier))[0]


def tile_terms(k, v, q_t, o_t, kpos, qpos, qbegin):
    y = nn(k, q_t) * (0.5 * ALPHA)
    t = jnp.tanh(y)
    u = 1.0 + t
    kpos = jnp.concatenate([kpos] * (q_t.shape[1] // HD), axis=1)
    valid = (kpos >= qbegin) & (kpos <= qpos)
    att = jnp.where(valid, y * u, 0.0).astype(jnp.bfloat16)
    slope = u * (1.0 + y * (1.0 - t))
    ds = jnp.where(valid, nn(v, o_t) * slope, 0.0).astype(jnp.bfloat16)
    return att, ds


def cross_pairs(
    own, len_ref, shift_ref, keep_ref, k_ref, q_ref, v_ref, o_ref, big, small,
    out_t, dq_t, dk, dv,
):
    rows = small[0].shape[0]
    span = GROUP - 1
    total = rows * lax.axis_size("ctx")
    shift = shift_ref[0]
    base = plane_base(rows)

    def shard(j):
        return slice(j * rows, (j + 1) * rows)

    def load(refs, j):
        if len(refs) == 1:
            return refs[0][shard(j), :HD], refs[0][shard(j), HD:]
        return refs[0][shard(j), :], refs[1][shard(j), :]

    def before(ref, first, reached):
        q_ts = [q_ref[shard(j), :].T for j in range(max(reached) + 1)]
        o_ts = [o_ref[shard(j), :].T for j in range(max(reached) + 1)]
        for p in reached:
            k, v = load(ref, p - first)
            k_t, v_t = k.T, v.T
            kpos = key_place(base + (p - span) * rows, rows, shift, keep_ref, total)
            for qt in range(p + 1):
                place_q = query_place(base + qt * rows, rows, shift, len_ref, total)
                att, ds = tile_terms(k, v, q_ts[qt], o_ts[qt], kpos, *place_q)
                out_t[:, shard(qt)] += nn(v_t, att)
                dq_t[:, shard(qt)] += nn(k_t, ds)

    def behind(ref, first, reached):
        for n in reached:
            q, o = load(ref, n - first)
            q_t, o_t = q.T, o.T
            place_q = query_place(base + (GROUP + n) * rows, rows, shift, len_ref, total)
            for kt in range(n + 1, GROUP):
                kpos = key_place(base + kt * rows, rows, shift, keep_ref, total)
                att, ds = tile_terms(
                    k_ref[shard(kt), :], v_ref[shard(kt), :], q_t, o_t, kpos, *place_q
                )
                dv[shard(kt), :] += nn(att, o)
                dk[shard(kt), :] += nn(ds, q)

    keys_big = upper() == (1 if own else 0)

    @pl.when(keys_big)
    def _():
        before(big, 1, range(1, span))
        behind(small, span - 1, [span - 1])

    @pl.when(jnp.logical_not(keys_big))
    def _():
        before(small, 0, [0])
        behind(big, 0, range(span - 1))


def square(own_row, shift, total, len_ref, keep_ref, pairs, out_t, dq_t, dk, dv, at):
    rows = pairs[0][0].shape[0]
    q_ts = [q.T for _, q, _, _ in pairs]
    o_ts = [o.T for _, _, _, o in pairs]
    places = [query_place(own_row + i * rows, rows, shift, len_ref, total) for i in (0, 1)]
    for kt, (k, _, v, _) in enumerate(pairs):
        k_t, v_t = k.T, v.T
        kpos = key_place(own_row + kt * rows, rows, shift, keep_ref, total)
        dk_sum, dv_sum = 0.0, 0.0
        for qt in range(kt, 2):
            att, ds = tile_terms(k, v, q_ts[qt], o_ts[qt], kpos, *places[qt])
            if kt == 0:
                out_t[:, at[qt]] = nn(v_t, att)
                dq_t[:, at[qt]] = nn(k_t, ds)
            else:
                out_t[:, at[qt]] += nn(v_t, att)
                dq_t[:, at[qt]] += nn(k_t, ds)
            dv_sum = dv_sum + nn(att, pairs[qt][3])
            dk_sum = dk_sum + nn(ds, pairs[qt][1])
        dk[at[kt], :] = dk_sum
        dv[at[kt], :] = dv_sum


def plane_base(rows):
    return (lax.axis_index("ctx") // GROUP) * (GROUP * rows)


def early_kernel(
    len_ref, shift_ref, keep_ref, a0, a1, b0, b1, out_t, dq_t, dk, dv, kq_ref, vo_ref
):
    rows = a0.shape[0]
    core = lax.rem(place(), 2)
    total = rows * lax.axis_size("ctx")
    for at_core, kq, vo in ((core, a0, b0), (1 - core, a1, b1)):
        at = pl.ds(pl.multiple_of(at_core * rows, rows), rows)
        kq_ref[at, :] = kq[...]
        vo_ref[at, :] = vo[...]
    shards = [slice(0, rows), slice(rows, 2 * rows)]
    pairs = [(kq_ref[i, :HD], kq_ref[i, HD:], vo_ref[i, :HD], vo_ref[i, HD:]) for i in shards]
    own_row = plane_base(rows) + upper() * 2 * rows
    square(
        own_row, shift_ref[0], total, len_ref, keep_ref, pairs, out_t, dq_t, dk, dv, shards
    )


def inner_kernel(
    len_ref, shift_ref, keep_ref, a0, a1, a2, a3_k, a3_q, b0, b1, b2, b3,
    early_out, early_dq, early_dk, early_dv,
    k_ref, q_ref, v_ref, o_ref, out_t, dq_t, dk, dv,
):
    rows = a0.shape[0]
    total = rows * lax.axis_size("ctx")
    shift = shift_ref[0]
    base = plane_base(rows)
    me = place()
    a3 = Sides(a3_k, a3_q)
    for i, (kq, vo) in enumerate(((a0, b0), (a1, b1), (a2, b2), (a3, b3))):
        at = pl.ds(pl.multiple_of((me ^ i) * rows, rows), rows)
        k_ref[at, :] = kq[:, :HD]
        q_ref[at, :] = kq[:, HD:]
        v_ref[at, :] = vo[:, :HD]
        o_ref[at, :] = vo[:, HD:]
    own = pl.ds(pl.multiple_of(upper() * 2 * rows, 2 * rows), 2 * rows)
    out_t[:, own] = early_out[...]
    dq_t[:, own] = early_dq[...]
    dk[own, :] = early_dk[...]
    dv[own, :] = early_dv[...]
    first = (1 - upper()) * 2 * rows
    others = [pl.ds(pl.multiple_of(first + i * rows, rows), rows) for i in (0, 1)]
    pairs = [(k_ref[at, :], q_ref[at, :], v_ref[at, :], o_ref[at, :]) for at in others]
    square(
        base + first, shift, total, len_ref, keep_ref, pairs, out_t, dq_t, dk, dv, others
    )
    shards = [slice(j * rows, (j + 1) * rows) for j in range(GROUP)]
    half = range(GROUP // 2, GROUP)
    places = {j: query_place(base + j * rows, rows, shift, len_ref, total) for j in half}
    q_ts = {j: q_ref[shards[j], :].T for j in half}
    o_ts = {j: o_ref[shards[j], :].T for j in half}
    for kt in range(GROUP // 2):
        at = shards[kt]
        k, v = k_ref[at, :], v_ref[at, :]
        k_t, v_t = k.T, v.T
        kpos = key_place(base + kt * rows, rows, shift, keep_ref, total)
        dk_sum, dv_sum = 0.0, 0.0
        for qt in half:
            qs = shards[qt]
            att, ds = tile_terms(k, v, q_ts[qt], o_ts[qt], kpos, *places[qt])
            out_t[:, qs] += nn(v_t, att)
            dq_t[:, qs] += nn(k_t, ds)
            dv_sum = dv_sum + nn(att, o_ref[qs, :])
            dk_sum = dk_sum + nn(ds, q_ref[qs, :])
        dk[at, :] += dk_sum
        dv[at, :] += dv_sum


def own_halo_kernel(
    len_ref, shift_ref, keep_ref, k_ref, q_ref, v_ref, o_ref, big, small, *refs
):
    cross_pairs(
        True, len_ref, shift_ref, keep_ref, k_ref, q_ref, v_ref, o_ref, (big,), (small,),
        *refs[4:],
    )


def outer_kernel(
    len_ref, shift_ref, keep_ref, k_ref, q_ref, v_ref, o_ref, big_kq, big_vo, small,
    *refs,
):
    out_t, dq_t, dk, dv, s0, s1, s2, s3, dqk = refs[4:]
    cross_pairs(
        False, len_ref, shift_ref, keep_ref, k_ref, q_ref, v_ref, o_ref,
        (big_kq, big_vo), (small,), out_t, dq_t, dk, dv,
    )
    rows = small.shape[0]
    me = place()
    factor = 0.5 * SCALE * ALPHA
    dqk[:HD, :] = (dq_t[...] * factor).astype(jnp.bfloat16)
    for j in range(GROUP):
        dqk[HD:, slice(j * rows, (j + 1) * rows)] = (dk[slice(j * rows, (j + 1) * rows), :] * factor).T.astype(jnp.bfloat16)
    for i, ref in enumerate((s0, s1, s2, s3)):
        at = pl.ds(pl.multiple_of((me ^ i) * rows, rows), rows)
        ref[:, :HD] = (out_t[:, at] * SCALE).T.astype(jnp.bfloat16)
        ref[:, HD:] = (dv[at, :] * SCALE).astype(jnp.bfloat16)


def terms_of(dqk, e0, e1, e2, e3):
    rows = e0.shape[0]
    me = place()
    total = None
    for k, ref in enumerate((e0, e1, e2, e3)):
        at = pl.ds(pl.multiple_of((me ^ k) * rows, rows), rows)
        part = nn(dqk[:, at], ref[...])
        total = part if total is None else total + part
    return total


def terms_kernel(dqk, e0, e1, e2, e3, whole):
    whole[...] = terms_of(dqk, e0, e1, e2, e3)


def half_terms_kernel(same, dqk, e0, e1, e2, e3, out):
    rows = e0.shape[0]
    me = place()
    half = upper() if same else 1 - upper()
    width = out.shape[1]
    high = dqk.shape[0]
    count = out.shape[0] // high
    for z in range(0, count, 2):
        cols = [pl.ds(pl.multiple_of((2 * (z + i) + half) * width, width), width) for i in (0, 1)]
        total = 0.0
        for k, ref in enumerate((e0, e1, e2, e3)):
            at = pl.ds(pl.multiple_of((me ^ k) * rows, rows), rows)
            piece = jnp.concatenate([ref[:, cols[0]], ref[:, cols[1]]], axis=1)
            total = total + nn(dqk[:, at], piece)
        out[z * high : (z + 1) * high, :] = total[:, :width].astype(out.dtype)
        out[(z + 1) * high : (z + 2) * high, :] = total[:, width:].astype(out.dtype)


def pair_sum_kernel(mine, other, *outs):
    planes = lax.axis_size("ctx") // GROUP
    z = lax.axis_index("ctx") // GROUP
    high = outs[0].shape[0]
    for dz, ref in enumerate(outs):
        at = pl.ds(pl.multiple_of(lax.rem(z + dz, planes) * high, high), high)
        ref[...] = (mine[at, :] + other[at, :].astype(jnp.float32)).astype(ref.dtype)


def sum_kernel(*refs):
    ins, (near, far, hold) = refs[:-3], refs[-3:]
    total = ins[0][...].astype(jnp.float32)
    for ref in ins[1:]:
        total = total + ref[...].astype(jnp.float32)
    hold[...] = total.T
    share = near.shape[0]
    core = lax.rem(lax.axis_index("ctx"), 2)
    near[...] = hold[pl.ds(pl.multiple_of(core * share, share), share), :].astype(jnp.bfloat16)
    far[...] = hold[pl.ds(pl.multiple_of((1 - core) * share, share), share), :].astype(jnp.bfloat16)


def join_kernel(own, other, out):
    core = lax.rem(place(), 2)
    width = own.shape[1]
    out[:, pl.ds(pl.multiple_of(core * width, width), width)] = own[...]
    out[:, pl.ds(pl.multiple_of((1 - core) * width, width), width)] = other[...]


def finish_kernel(own, other, gq, gk):
    first = upper() ^ lax.axis_index("dp")
    for pair, ref in ((first, own), (1 - first, other)):
        for core in range(2):
            cols = head_cols(2 * pair + core)
            gq[:, cols] = ref[:, 2 * core * HD : (2 * core + 1) * HD]
            gk[:, cols] = ref[:, (2 * core + 1) * HD : (2 * core + 2) * HD]


def merge_kernel(i0, i1, i2, i3, first, second):
    mine = head()
    for k, ref in enumerate((i0, i1, i2, i3)):
        cols = head_cols(mine ^ k)
        first[:, cols] = ref[:, :HD]
        second[:, cols] = ref[:, HD:]


def direct_reduce(dqk, gathered, share):
    count = lax.axis_size("ctx")
    planes = count // GROUP
    width = gathered[0].shape[1]
    block = width // (2 * planes)
    shape = (2 * HD * planes, block)
    args = (dqk, *gathered)
    (give,) = call(functools.partial(half_terms_kernel, False), [like(*shape)], args, busy=1)
    (keep,) = call(
        functools.partial(half_terms_kernel, True), [like(*shape, jnp.float32)], args, busy=1
    )
    across = [(y * count + i, (1 - y) * count + (i ^ 2)) for y in range(2) for i in range(count)]
    got = lax.ppermute(give, ("dp", "ctx"), across)
    sends = call(
        pair_sum_kernel,
        [like(2 * HD, block, jnp.float32)] + [like(2 * HD, block)] * (planes - 1),
        (keep, got),
    )
    arrived = [sends[0]] + [around(sends[dz], dz, dz) for dz in range(1, planes)]
    near, far = call(
        sum_kernel,
        [like(share, 2 * HD)] * 2,
        arrived,
        scratch=[pltpu.VMEM((block, 2 * HD), jnp.float32)],
    )
    (both,) = call(join_kernel, [like(share, 4 * HD)], (near, partner(far, 1)), busy=0.1)
    other = lax.ppermute(both, "dp", [(0, 1), (1, 0)])
    return got, call(finish_kernel, [like(share, GROUP * HD)] * 2, (both, other))


def general_reduce(dqk, gathered, share):
    count = lax.axis_size("ctx")
    planes = count // GROUP
    width = gathered[0].shape[1]
    (whole,) = call(
        terms_kernel, [like(2 * HD, width, jnp.float32)], (dqk, *gathered), busy=2
    )
    whole = lax.psum(whole.T, "dp")
    same_head = [[g * GROUP + j for g in range(planes)] for j in range(GROUP)]
    plane = [[g * GROUP + j for j in range(GROUP)] for g in range(planes)]
    part = lax.psum_scatter(
        whole, "ctx", scatter_dimension=0, axis_index_groups=same_head, tiled=True
    ).astype(jnp.bfloat16)
    part = lax.all_to_all(
        part.reshape(GROUP, share, 2 * HD), "ctx", 0, 0, axis_index_groups=plane, tiled=True
    )
    part = jnp.moveaxis(part.reshape(GROUP, share, 2, HD), 0, 2)
    grads = part[:, 0].reshape(share, GROUP * HD), part[:, 1].reshape(share, GROUP * HD)
    return dqk, grads


def body(events, w_query, w_key, values, grad_out, lengths, stream_shift, block_keep):
    rows, width = events.shape[1:]
    features = w_query.shape[1]
    count = lax.axis_size("ctx")
    local = events[0]
    all_rows = GROUP * rows
    pair = like(rows, 2 * HD)
    full = like(all_rows, HD)

    e1 = partner(local, 1)
    e2 = partner(local, 2)
    vo0, vo1, vo2, vo3, weights = call(
        fetch_kernel,
        [pair] * GROUP + [like(width, 4 * HD)],
        [
            pltpu.with_memory_space_constraint(a, pltpu.HBM)
            for a in (values[0], grad_out[0], w_key, w_query)
        ],
        specs=[HBM] * 4,
        busy=0.1,
        scratch=[pltpu.SemaphoreType.DMA((12,))],
    )
    vo1 = partner(vo1, 1)
    info = (lengths, stream_shift, block_keep)
    wide, tall = like(HD, all_rows, jnp.float32), like(all_rows, HD, jnp.float32)
    sums = [wide, wide, tall, tall]
    wide, tall = like(HD, 2 * rows, jnp.float32), like(2 * rows, HD, jnp.float32)
    kq0, kq1 = call(project_kernel, [pair] * 2, (local, e1, weights), busy=1)
    big, small = call(
        functools.partial(edge_kernel, True, 0),
        [like(2 * rows, 2 * HD), pair],
        (kq0, kq1, vo0, vo1),
        busy=0.1,
    )
    own = around(big, -1, 1), around(small, 1, -1)
    early = call(
        early_kernel,
        [wide, wide, tall, tall],
        (*info, after(kq0, small), kq1, vo0, vo1),
        specs=[SMEM] * 3 + [VMEM] * 4,
        busy=0.1,
        scratch=[pltpu.VMEM((2 * rows, 2 * HD), jnp.bfloat16)] * 2,
    )
    vo2, vo3 = partner(after(vo2, *early), 2), partner(after(vo3, *early), 3)
    half = like(rows, HD)
    kq2, *give = call(project_both_kernel, [pair, half, half], (after(e2, own[1], *early), weights), busy=1)
    k3, q3 = partner(give[0], 1), partner(give[1], 1)
    big_kq, _ = call(
        functools.partial(edge_kernel, False, 0),
        [like(2 * rows + 16, HD), like(rows, HD)],
        (kq2, k3, q3),
        busy=0.1,
    )
    big_vo, small = call(
        functools.partial(edge_kernel, False, 1),
        [like(2 * rows, HD), pair],
        (kq2, k3, q3, after(vo2, own[0], big_kq), vo3),
        busy=2,
    )
    big_kq = around(big_kq, 1, -1)
    k3 = after(k3, big_vo)
    own0 = after(own[0], big_kq)
    other = big_kq, around(big_vo, 1, -1), around(small, -1, 1)
    k, q, v, o, *held = call(
        inner_kernel,
        [full] * 4 + sums,
        (*info, kq0, kq1, kq2, k3, q3, vo0, vo1, vo2, vo3, *early),
        specs=[SMEM] * 3 + [VMEM] * 13,
        busy=3,
    )
    held = call(
        own_halo_kernel,
        sums,
        (*info, k, q, v, o, own0, own[1], *held),
        specs=[SMEM] * 3 + [VMEM] * 10,
        aliases={9: 0, 10: 1, 11: 2, 12: 3},
        busy=5,
    )
    *_, p0, p1, p2, p3, dqk = call(
        outer_kernel,
        sums + [pair] * GROUP + [like(2 * HD, all_rows)],
        (*info, k, q, v, o, *other, *held),
        specs=[SMEM] * 3 + [VMEM] * 11,
        aliases={10: 0, 11: 1, 12: 2, 13: 3},
        busy=6,
    )
    e3 = partner(after(e2, *held), 1)
    share = width // count
    reduce = direct_reduce if paired() else general_reduce
    reached, (grad_wq, grad_wk) = reduce(dqk, (local, e1, e2, e3), share)
    parts = [partner(after(p, reached), k) for k, p in ((1, p1), (2, p2), (3, p3))]
    attended, grad_values = call(merge_kernel, [like(rows, features)] * 2, (p0, *parts))
    return (attended[None], grad_values[None], grad_wq, grad_wk)


def solution(mesh):
    placed = (
        P("dp", "ctx", None),
        P(),
        P(),
        P("dp", "ctx", None),
        P("dp", "ctx", None),
        P("dp", None),
        P("dp"),
        P("dp", None),
    )
    return jax.shard_map(
        body,
        mesh=mesh,
        in_specs=placed,
        out_specs=(P("dp", "ctx", None), P("dp", "ctx", None), P("ctx", None), P("ctx", None)),
        check_vma=False,
    )
```

```python
import functools

import jax
import jax.numpy as jnp
from jax import lax
from jax.experimental import pallas as pl
from jax.experimental.pallas import tpu as pltpu
from jax.sharding import PartitionSpec as P

HD = 128
BLOCK = 128
MAXLEN = 768
GROUP = 4
FAR = 1 << 30
PEAK = 1.15e9
ALPHA = 1.0 / HD**0.5
SCALE = 1.0 / MAXLEN**0.5
VMEM = pl.BlockSpec(memory_space=pltpu.VMEM)
HBM = pl.BlockSpec(memory_space=pltpu.HBM)
SMEM = pl.BlockSpec(memory_space=pltpu.SMEM)


def call(kernel, outs, args, specs=None, busy=0.5, scratch=(), aliases=None):
    return pl.pallas_call(
        kernel,
        out_shape=tuple(outs),
        in_specs=specs or [VMEM] * len(args),
        out_specs=tuple([VMEM] * len(outs)),
        scratch_shapes=scratch,
        input_output_aliases=aliases or {},
        compiler_params=pltpu.CompilerParams(vmem_limit_bytes=24 * 1024 * 1024),
        cost_estimate=pl.CostEstimate(
            flops=int(busy * PEAK), bytes_accessed=0, transcendentals=0
        ),
    )(*args)


def like(rows, cols, dtype=jnp.bfloat16):
    return jax.ShapeDtypeStruct((rows, cols), dtype)


def partner(value, steps):
    count = lax.axis_size("ctx")
    return lax.ppermute(value, "ctx", [(i, i ^ steps) for i in range(count)])


def around(value, low, high):
    count = lax.axis_size("ctx")
    pairs = []
    for i in range(count):
        planes = low if i % GROUP < GROUP // 2 else high
        pairs.append((i, (i + planes * GROUP) % count))
    return lax.ppermute(value, "ctx", pairs)


def place():
    return lax.rem(lax.axis_index("ctx"), GROUP)


def paired():
    return lax.axis_size("dp") == 2 and lax.axis_size("ctx") == 16


def head():
    return place() ^ (2 * lax.axis_index("dp")) if paired() else place()


def head_cols(h):
    return pl.ds(pl.multiple_of(h * HD, HD), HD)


def nn(a, b):
    return jnp.dot(a, b, preferred_element_type=jnp.float32)


def fetch_kernel(a_ref, b_ref, wk_ref, wq_ref, *refs):
    *outs, weights, sems = refs
    mine = head()
    copies = []
    for k in range(2):
        for side, ref in enumerate((wk_ref, wq_ref)):
            to = slice((2 * k + side) * HD, (2 * k + side + 1) * HD)
            copies.append((ref.at[:, head_cols(mine ^ k)], weights.at[:, to]))
    for k, out in enumerate(outs):
        for side, ref in enumerate((a_ref, b_ref)):
            to = slice(side * HD, (side + 1) * HD)
            copies.append((ref.at[:, head_cols(mine ^ k)], out.at[:, to]))
    started = [pltpu.make_async_copy(*pair, sems.at[i]) for i, pair in enumerate(copies)]
    for copy in started:
        copy.start()
    for copy in started:
        copy.wait()


def project_kernel(near, far, weights, near_kq, far_kq):
    own = weights[:, : 2 * HD]
    near_kq[...] = nn(near[...], own).astype(jnp.bfloat16)
    far_kq[...] = nn(far[...], own).astype(jnp.bfloat16)


class Sides:
    def __init__(self, left, right):
        self.left, self.right = left, right

    def __getitem__(self, where):
        rows, cols = where
        return (self.right if cols.start == HD else self.left)[rows, :]


def project_both_kernel(rows_ref, weights, own_kq, other_k, other_q):
    both = nn(rows_ref[...], weights[...]).astype(jnp.bfloat16)
    own_kq[...] = both[:, : 2 * HD]
    other_k[...] = both[:, 2 * HD : 3 * HD]
    other_q[...] = both[:, 3 * HD :]


def upper():
    return lax.div(place(), 2)


def edge_kernel(own, skip, *refs):
    *sources, big, small = refs
    if len(sources) % 2:
        sources[1:3] = [Sides(*sources[1:3])]
    rows = small.shape[0]
    if big.shape[0] > 2 * rows:
        big[2 * rows :, :] = jnp.zeros((big.shape[0] - 2 * rows, big.shape[1]), big.dtype)
    core = lax.rem(place(), 2)
    keys_big = upper() == (1 if own else 0)
    for pair in range(len(sources) // 2):
        to = slice(pair * HD, (pair + 1) * HD)
        to_big = slice((pair - skip) * HD, (pair - skip + 1) * HD)
        for i, at_core in ((0, core), (1, 1 - core)):
            ref = sources[2 * pair + i]
            at = pl.ds(pl.multiple_of(at_core * rows, rows), rows)

            @pl.when(keys_big)
            def _():
                if pair >= skip:
                    big[at, to_big] = ref[:, :HD]

                @pl.when(at_core == 0)
                def _():
                    small[:, to] = ref[:, HD:]

            @pl.when(jnp.logical_not(keys_big))
            def _():
                if pair >= skip:
                    big[at, to_big] = ref[:, HD:]

                @pl.when(at_core == 1)
                def _():
                    small[:, to] = ref[:, :HD]


def offset_of(row, shift, total):
    return lax.rem(row - shift + 2 * total, total)


def key_place(row, rows, shift, keep_ref, total):
    base = offset_of(row, shift, total)
    nblk = keep_ref.shape[1]
    raw = base + lax.broadcasted_iota(jnp.int32, (rows, HD), 0)
    b0 = base // BLOCK
    kept = jnp.full((rows, HD), keep_ref[0, b0], jnp.int32)
    for more in range(1, rows // BLOCK + 1):
        flag = keep_ref[0, lax.rem(b0 + more, nblk)]
        kept = jnp.where(raw >= (b0 + more) * BLOCK, flag, kept)
    where = jnp.where(raw >= total, raw - total, raw)
    return jnp.where(kept > 0, where, FAR)


def query_place(row, rows, shift, len_ref, total):
    base = offset_of(row, shift, total)
    raw = base + lax.broadcasted_iota(jnp.int32, (1, rows), 1)
    where = jnp.where(raw >= total, raw - total, raw)
    begin = jnp.zeros((1, rows), jnp.int32)
    end = jnp.int32(0)
    for u in range(len_ref.shape[1]):
        length = len_ref[0, u]
        end = end + length
        begin = begin + jnp.where(where >= end, length, 0)
    return where, begin


def after(value, *earlier):
    return lax.optimization_barrier((value, *earlier))[0]


def tile_terms(k, v, q_t, o_t, kpos, qpos, qbegin):
    y = nn(k, q_t) * (0.5 * ALPHA)
    t = jnp.tanh(y)
    u = 1.0 + t
    kpos = jnp.concatenate([kpos] * (q_t.shape[1] // HD), axis=1)
    valid = (kpos >= qbegin) & (kpos <= qpos)
    att = jnp.where(valid, y * u, 0.0).astype(jnp.bfloat16)
    slope = u * (1.0 + y * (1.0 - t))
    ds = jnp.where(valid, nn(v, o_t) * slope, 0.0).astype(jnp.bfloat16)
    return att, ds


def cross_pairs(
    own, len_ref, shift_ref, keep_ref, k_ref, q_ref, v_ref, o_ref, big, small,
    out_t, dq_t, dk, dv,
):
    rows = k_ref.shape[0] // GROUP
    span = GROUP - 1
    total = rows * lax.axis_size("ctx")
    shift = shift_ref[0]
    base = plane_base(rows)

    def shard(j):
        return slice(j * rows, (j + 1) * rows)

    def load(refs, j):
        if len(refs) == 1:
            return refs[0][shard(j), :HD], refs[0][shard(j), HD:]
        return refs[0][shard(j), :], refs[1][shard(j), :]

    def before(ref, first, reached):
        q_ts = [q_ref[shard(j), :].T for j in range(max(reached) + 1)]
        o_ts = [o_ref[shard(j), :].T for j in range(max(reached) + 1)]
        for p in reached:
            k, v = load(ref, p - first)
            k_t, v_t = k.T, v.T
            kpos = key_place(base + (p - span) * rows, rows, shift, keep_ref, total)
            for qt in range(p + 1):
                place_q = query_place(base + qt * rows, rows, shift, len_ref, total)
                att, ds = tile_terms(k, v, q_ts[qt], o_ts[qt], kpos, *place_q)
                out_t[:, shard(qt)] += nn(v_t, att)
                dq_t[:, shard(qt)] += nn(k_t, ds)

    def behind(ref, first, reached):
        for n in reached:
            q, o = load(ref, n - first)
            q_t, o_t = q.T, o.T
            place_q = query_place(base + (GROUP + n) * rows, rows, shift, len_ref, total)
            for kt in range(n + 1, GROUP):
                kpos = key_place(base + kt * rows, rows, shift, keep_ref, total)
                att, ds = tile_terms(
                    k_ref[shard(kt), :], v_ref[shard(kt), :], q_t, o_t, kpos, *place_q
                )
                dv[shard(kt), :] += nn(att, o)
                dk[shard(kt), :] += nn(ds, q)

    keys_big = upper() == (1 if own else 0)

    @pl.when(keys_big)
    def _():
        if big:
            before(big, 1, range(1, span))
        if small:
            behind(small, span - 1, [span - 1])

    @pl.when(jnp.logical_not(keys_big))
    def _():
        if small:
            before(small, 0, [0])
        if big:
            behind(big, 0, range(span - 1))


def square(own_row, shift, total, len_ref, keep_ref, pairs, out_t, dq_t, dk, dv, at):
    rows = pairs[0][0].shape[0]
    q_ts = [q.T for _, q, _, _ in pairs]
    o_ts = [o.T for _, _, _, o in pairs]
    places = [query_place(own_row + i * rows, rows, shift, len_ref, total) for i in (0, 1)]
    for kt, (k, _, v, _) in enumerate(pairs):
        k_t, v_t = k.T, v.T
        kpos = key_place(own_row + kt * rows, rows, shift, keep_ref, total)
        dk_sum, dv_sum = 0.0, 0.0
        for qt in range(kt, 2):
            att, ds = tile_terms(k, v, q_ts[qt], o_ts[qt], kpos, *places[qt])
            if kt == 0:
                out_t[:, at[qt]] = nn(v_t, att)
                dq_t[:, at[qt]] = nn(k_t, ds)
            else:
                out_t[:, at[qt]] += nn(v_t, att)
                dq_t[:, at[qt]] += nn(k_t, ds)
            dv_sum = dv_sum + nn(att, pairs[qt][3])
            dk_sum = dk_sum + nn(ds, pairs[qt][1])
        dk[at[kt], :] = dk_sum
        dv[at[kt], :] = dv_sum


def plane_base(rows):
    return (lax.axis_index("ctx") // GROUP) * (GROUP * rows)


def early_kernel(
    len_ref, shift_ref, keep_ref, a0, a1, b0, b1, out_t, dq_t, dk, dv, kq_ref, vo_ref
):
    rows = a0.shape[0]
    core = lax.rem(place(), 2)
    total = rows * lax.axis_size("ctx")
    for at_core, kq, vo in ((core, a0, b0), (1 - core, a1, b1)):
        at = pl.ds(pl.multiple_of(at_core * rows, rows), rows)
        kq_ref[at, :] = kq[...]
        vo_ref[at, :] = vo[...]
    shards = [slice(0, rows), slice(rows, 2 * rows)]
    pairs = [(kq_ref[i, :HD], kq_ref[i, HD:], vo_ref[i, :HD], vo_ref[i, HD:]) for i in shards]
    own_row = plane_base(rows) + upper() * 2 * rows
    square(
        own_row, shift_ref[0], total, len_ref, keep_ref, pairs, out_t, dq_t, dk, dv, shards
    )


def inner_kernel(
    len_ref, shift_ref, keep_ref, a0, a1, a2, a3_k, a3_q, b0, b1, b2, b3,
    early_out, early_dq, early_dk, early_dv,
    k_ref, q_ref, v_ref, o_ref, out_t, dq_t, dk, dv,
):
    rows = a0.shape[0]
    total = rows * lax.axis_size("ctx")
    shift = shift_ref[0]
    base = plane_base(rows)
    me = place()
    a3 = Sides(a3_k, a3_q)
    for i, (kq, vo) in enumerate(((a0, b0), (a1, b1), (a2, b2), (a3, b3))):
        at = pl.ds(pl.multiple_of((me ^ i) * rows, rows), rows)
        k_ref[at, :] = kq[:, :HD]
        q_ref[at, :] = kq[:, HD:]
        v_ref[at, :] = vo[:, :HD]
        o_ref[at, :] = vo[:, HD:]
    own = pl.ds(pl.multiple_of(upper() * 2 * rows, 2 * rows), 2 * rows)
    out_t[:, own] = early_out[...]
    dq_t[:, own] = early_dq[...]
    dk[own, :] = early_dk[...]
    dv[own, :] = early_dv[...]
    first = (1 - upper()) * 2 * rows
    others = [pl.ds(pl.multiple_of(first + i * rows, rows), rows) for i in (0, 1)]
    pairs = [(k_ref[at, :], q_ref[at, :], v_ref[at, :], o_ref[at, :]) for at in others]
    square(
        base + first, shift, total, len_ref, keep_ref, pairs, out_t, dq_t, dk, dv, others
    )
    shards = [slice(j * rows, (j + 1) * rows) for j in range(GROUP)]
    half = range(GROUP // 2, GROUP)
    places = {j: query_place(base + j * rows, rows, shift, len_ref, total) for j in half}
    q_ts = {j: q_ref[shards[j], :].T for j in half}
    o_ts = {j: o_ref[shards[j], :].T for j in half}
    for kt in range(GROUP // 2):
        at = shards[kt]
        k, v = k_ref[at, :], v_ref[at, :]
        k_t, v_t = k.T, v.T
        kpos = key_place(base + kt * rows, rows, shift, keep_ref, total)
        dk_sum, dv_sum = 0.0, 0.0
        for qt in half:
            qs = shards[qt]
            att, ds = tile_terms(k, v, q_ts[qt], o_ts[qt], kpos, *places[qt])
            out_t[:, qs] += nn(v_t, att)
            dq_t[:, qs] += nn(k_t, ds)
            dv_sum = dv_sum + nn(att, o_ref[qs, :])
            dk_sum = dk_sum + nn(ds, q_ref[qs, :])
        dk[at, :] += dk_sum
        dv[at, :] += dv_sum


def own_halo_kernel(
    len_ref, shift_ref, keep_ref, k_ref, q_ref, v_ref, o_ref, big, small, *refs
):
    cross_pairs(
        True, len_ref, shift_ref, keep_ref, k_ref, q_ref, v_ref, o_ref, (big,), (small,),
        *refs[4:],
    )


def big_halo_kernel(
    len_ref, shift_ref, keep_ref, k_ref, q_ref, v_ref, o_ref, big_kq, big_vo, *refs
):
    rows = k_ref.shape[0] // GROUP
    cross_pairs(
        False, len_ref, shift_ref, keep_ref, k_ref, q_ref, v_ref, o_ref,
        (big_kq.at[: 2 * rows, :], big_vo), (), *refs[4:],
    )


def outer_kernel(
    len_ref, shift_ref, keep_ref, k_ref, q_ref, v_ref, o_ref, small, *refs
):
    out_t, dq_t, dk, dv, s0, s1, s2, s3, dqk = refs[4:]
    cross_pairs(
        False, len_ref, shift_ref, keep_ref, k_ref, q_ref, v_ref, o_ref, (), (small,),
        out_t, dq_t, dk, dv,
    )
    rows = small.shape[0]
    me = place()
    factor = 0.5 * SCALE * ALPHA
    dqk[:HD, :] = (dq_t[...] * factor).astype(jnp.bfloat16)
    for j in range(GROUP):
        dqk[HD:, slice(j * rows, (j + 1) * rows)] = (dk[slice(j * rows, (j + 1) * rows), :] * factor).T.astype(jnp.bfloat16)
    for i, ref in enumerate((s0, s1, s2, s3)):
        at = pl.ds(pl.multiple_of((me ^ i) * rows, rows), rows)
        ref[:, :HD] = (out_t[:, at] * SCALE).T.astype(jnp.bfloat16)
        ref[:, HD:] = (dv[at, :] * SCALE).astype(jnp.bfloat16)


def terms_of(dqk, e0, e1, e2, e3):
    rows = e0.shape[0]
    me = place()
    total = None
    for k, ref in enumerate((e0, e1, e2, e3)):
        at = pl.ds(pl.multiple_of((me ^ k) * rows, rows), rows)
        part = nn(dqk[:, at], ref[...])
        total = part if total is None else total + part
    return total


def terms_kernel(dqk, e0, e1, e2, e3, whole):
    whole[...] = terms_of(dqk, e0, e1, e2, e3)


def half_terms_kernel(same, dqk, e0, e1, e2, e3, out):
    rows = e0.shape[0]
    me = place()
    half = upper() if same else 1 - upper()
    width = out.shape[1]
    high = dqk.shape[0]
    count = out.shape[0] // high
    for z in range(0, count, 2):
        cols = [pl.ds(pl.multiple_of((2 * (z + i) + half) * width, width), width) for i in (0, 1)]
        total = 0.0
        for k, ref in enumerate((e0, e1, e2, e3)):
            at = pl.ds(pl.multiple_of((me ^ k) * rows, rows), rows)
            piece = jnp.concatenate([ref[:, cols[0]], ref[:, cols[1]]], axis=1)
            total = total + nn(dqk[:, at], piece)
        out[z * high : (z + 1) * high, :] = total[:, :width].astype(out.dtype)
        out[(z + 1) * high : (z + 2) * high, :] = total[:, width:].astype(out.dtype)


def pair_sum_kernel(mine, other, *outs):
    planes = lax.axis_size("ctx") // GROUP
    z = lax.axis_index("ctx") // GROUP
    high = outs[0].shape[0]
    for dz, ref in enumerate(outs):
        at = pl.ds(pl.multiple_of(lax.rem(z + dz, planes) * high, high), high)
        ref[...] = (mine[at, :] + other[at, :].astype(jnp.float32)).astype(ref.dtype)


def sum_kernel(*refs):
    ins, (near, far, hold) = refs[:-3], refs[-3:]
    total = ins[0][...].astype(jnp.float32)
    for ref in ins[1:]:
        total = total + ref[...].astype(jnp.float32)
    hold[...] = total.T
    share = near.shape[0]
    core = lax.rem(lax.axis_index("ctx"), 2)
    near[...] = hold[pl.ds(pl.multiple_of(core * share, share), share), :].astype(jnp.bfloat16)
    far[...] = hold[pl.ds(pl.multiple_of((1 - core) * share, share), share), :].astype(jnp.bfloat16)


def join_kernel(own, other, out):
    core = lax.rem(place(), 2)
    width = own.shape[1]
    out[:, pl.ds(pl.multiple_of(core * width, width), width)] = own[...]
    out[:, pl.ds(pl.multiple_of((1 - core) * width, width), width)] = other[...]


def finish_kernel(own, other, gq, gk):
    first = upper() ^ lax.axis_index("dp")
    for pair, ref in ((first, own), (1 - first, other)):
        for core in range(2):
            cols = head_cols(2 * pair + core)
            gq[:, cols] = ref[:, 2 * core * HD : (2 * core + 1) * HD]
            gk[:, cols] = ref[:, (2 * core + 1) * HD : (2 * core + 2) * HD]


def merge_kernel(i0, i1, i2, i3, first, second):
    mine = head()
    for k, ref in enumerate((i0, i1, i2, i3)):
        cols = head_cols(mine ^ k)
        first[:, cols] = ref[:, :HD]
        second[:, cols] = ref[:, HD:]


def direct_reduce(dqk, gathered, share):
    count = lax.axis_size("ctx")
    planes = count // GROUP
    width = gathered[0].shape[1]
    block = width // (2 * planes)
    shape = (2 * HD * planes, block)
    args = (dqk, *gathered)
    (give,) = call(functools.partial(half_terms_kernel, False), [like(*shape)], args, busy=1)
    (keep,) = call(
        functools.partial(half_terms_kernel, True), [like(*shape, jnp.float32)], args, busy=1
    )
    across = [(y * count + i, (1 - y) * count + (i ^ 2)) for y in range(2) for i in range(count)]
    got = lax.ppermute(give, ("dp", "ctx"), across)
    sends = call(
        pair_sum_kernel,
        [like(2 * HD, block, jnp.float32)] + [like(2 * HD, block)] * (planes - 1),
        (keep, got),
    )
    arrived = [sends[0]] + [around(sends[dz], dz, dz) for dz in range(1, planes)]
    near, far = call(
        sum_kernel,
        [like(share, 2 * HD)] * 2,
        arrived,
        scratch=[pltpu.VMEM((block, 2 * HD), jnp.float32)],
    )
    (both,) = call(join_kernel, [like(share, 4 * HD)], (near, partner(far, 1)), busy=0.1)
    other = lax.ppermute(both, "dp", [(0, 1), (1, 0)])
    return got, call(finish_kernel, [like(share, GROUP * HD)] * 2, (both, other))


def general_reduce(dqk, gathered, share):
    count = lax.axis_size("ctx")
    planes = count // GROUP
    width = gathered[0].shape[1]
    (whole,) = call(
        terms_kernel, [like(2 * HD, width, jnp.float32)], (dqk, *gathered), busy=2
    )
    whole = lax.psum(whole.T, "dp")
    same_head = [[g * GROUP + j for g in range(planes)] for j in range(GROUP)]
    plane = [[g * GROUP + j for j in range(GROUP)] for g in range(planes)]
    part = lax.psum_scatter(
        whole, "ctx", scatter_dimension=0, axis_index_groups=same_head, tiled=True
    ).astype(jnp.bfloat16)
    part = lax.all_to_all(
        part.reshape(GROUP, share, 2 * HD), "ctx", 0, 0, axis_index_groups=plane, tiled=True
    )
    part = jnp.moveaxis(part.reshape(GROUP, share, 2, HD), 0, 2)
    grads = part[:, 0].reshape(share, GROUP * HD), part[:, 1].reshape(share, GROUP * HD)
    return dqk, grads


def body(events, w_query, w_key, values, grad_out, lengths, stream_shift, block_keep):
    rows, width = events.shape[1:]
    features = w_query.shape[1]
    count = lax.axis_size("ctx")
    local = events[0]
    all_rows = GROUP * rows
    pair = like(rows, 2 * HD)
    full = like(all_rows, HD)

    e1 = partner(local, 1)
    e2 = partner(local, 2)
    vo0, vo1, vo2, vo3, weights = call(
        fetch_kernel,
        [pair] * GROUP + [like(width, 4 * HD)],
        [
            pltpu.with_memory_space_constraint(a, pltpu.HBM)
            for a in (values[0], grad_out[0], w_key, w_query)
        ],
        specs=[HBM] * 4,
        busy=0.1,
        scratch=[pltpu.SemaphoreType.DMA((12,))],
    )
    vo1 = partner(vo1, 1)
    info = (lengths, stream_shift, block_keep)
    wide, tall = like(HD, all_rows, jnp.float32), like(all_rows, HD, jnp.float32)
    sums = [wide, wide, tall, tall]
    wide, tall = like(HD, 2 * rows, jnp.float32), like(2 * rows, HD, jnp.float32)
    kq0, kq1 = call(project_kernel, [pair] * 2, (local, e1, weights), busy=1)
    big, small = call(
        functools.partial(edge_kernel, True, 0),
        [like(2 * rows, 2 * HD), pair],
        (kq0, kq1, vo0, vo1),
        busy=0.1,
    )
    own = around(big, -1, 1), around(small, 1, -1)
    early = call(
        early_kernel,
        [wide, wide, tall, tall],
        (*info, after(kq0, small), kq1, vo0, vo1),
        specs=[SMEM] * 3 + [VMEM] * 4,
        busy=0.1,
        scratch=[pltpu.VMEM((2 * rows, 2 * HD), jnp.bfloat16)] * 2,
    )
    vo2, vo3 = partner(after(vo2, *early), 2), partner(after(vo3, *early), 3)
    half = like(rows, HD)
    kq2, *give = call(project_both_kernel, [pair, half, half], (after(e2, own[1], *early), weights), busy=1)
    k3, q3 = partner(give[0], 1), partner(give[1], 1)
    big_kq, _ = call(
        functools.partial(edge_kernel, False, 0),
        [like(2 * rows + 16, HD), like(rows, HD)],
        (kq2, k3, q3),
        busy=0.1,
    )
    big_vo, small = call(
        functools.partial(edge_kernel, False, 1),
        [like(2 * rows, HD), pair],
        (kq2, k3, q3, after(vo2, own[0], big_kq), vo3),
        busy=2,
    )
    big_kq = around(big_kq, 1, -1)
    k3 = after(k3, big_vo)
    own0 = after(own[0], big_kq)
    other = big_kq, around(big_vo, 1, -1), around(small, -1, 1)
    k, q, v, o, *held = call(
        inner_kernel,
        [full] * 4 + sums,
        (*info, kq0, kq1, kq2, k3, q3, vo0, vo1, vo2, vo3, *early),
        specs=[SMEM] * 3 + [VMEM] * 13,
        busy=3,
    )
    held = call(
        own_halo_kernel,
        sums,
        (*info, k, q, v, o, own0, own[1], *held),
        specs=[SMEM] * 3 + [VMEM] * 10,
        aliases={9: 0, 10: 1, 11: 2, 12: 3},
        busy=5,
    )
    held = call(
        big_halo_kernel,
        sums,
        (*info, k, q, v, o, *other[:2], *held),
        specs=[SMEM] * 3 + [VMEM] * 10,
        aliases={9: 0, 10: 1, 11: 2, 12: 3},
        busy=4,
    )
    *_, p0, p1, p2, p3, dqk = call(
        outer_kernel,
        sums + [pair] * GROUP + [like(2 * HD, all_rows)],
        (*info, k, q, v, o, other[2], *held),
        specs=[SMEM] * 3 + [VMEM] * 9,
        aliases={8: 0, 9: 1, 10: 2, 11: 3},
        busy=2,
    )
    e3 = partner(after(e2, kq2), 1)
    share = width // count
    reduce = direct_reduce if paired() else general_reduce
    reached, (grad_wq, grad_wk) = reduce(dqk, (local, e1, e2, e3), share)
    parts = [partner(after(p, reached), k) for k, p in ((1, p1), (2, p2), (3, p3))]
    attended, grad_values = call(merge_kernel, [like(rows, features)] * 2, (p0, *parts))
    return (attended[None], grad_values[None], grad_wq, grad_wk)


def solution(mesh):
    placed = (
        P("dp", "ctx", None),
        P(),
        P(),
        P("dp", "ctx", None),
        P("dp", "ctx", None),
        P("dp", None),
        P("dp"),
        P("dp", None),
    )
    return jax.shard_map(
        body,
        mesh=mesh,
        in_specs=placed,
        out_specs=(P("dp", "ctx", None), P("dp", "ctx", None), P("ctx", None), P("ctx", None)),
        check_vma=False,
    )
```

```python
import functools

import jax
import jax.numpy as jnp
from jax import lax
from jax.experimental import pallas as pl
from jax.experimental.pallas import tpu as pltpu
from jax.sharding import PartitionSpec as P

HD = 128
BLOCK = 128
MAXLEN = 768
GROUP = 4
FAR = 1 << 30
PEAK = 1.15e9
ALPHA = 1.0 / HD**0.5
SCALE = 1.0 / MAXLEN**0.5
VMEM = pl.BlockSpec(memory_space=pltpu.VMEM)
HBM = pl.BlockSpec(memory_space=pltpu.HBM)
SMEM = pl.BlockSpec(memory_space=pltpu.SMEM)


def call(kernel, outs, args, specs=None, busy=0.5, scratch=(), aliases=None):
    return pl.pallas_call(
        kernel,
        out_shape=tuple(outs),
        in_specs=specs or [VMEM] * len(args),
        out_specs=tuple([VMEM] * len(outs)),
        scratch_shapes=scratch,
        input_output_aliases=aliases or {},
        compiler_params=pltpu.CompilerParams(vmem_limit_bytes=24 * 1024 * 1024),
        cost_estimate=pl.CostEstimate(
            flops=int(busy * PEAK), bytes_accessed=0, transcendentals=0
        ),
    )(*args)


def like(rows, cols, dtype=jnp.bfloat16):
    return jax.ShapeDtypeStruct((rows, cols), dtype)


def partner(value, steps):
    count = lax.axis_size("ctx")
    return lax.ppermute(value, "ctx", [(i, i ^ steps) for i in range(count)])


def around(value, low, high):
    count = lax.axis_size("ctx")
    pairs = []
    for i in range(count):
        planes = low if i % GROUP < GROUP // 2 else high
        pairs.append((i, (i + planes * GROUP) % count))
    return lax.ppermute(value, "ctx", pairs)


def place():
    return lax.rem(lax.axis_index("ctx"), GROUP)


def paired():
    return lax.axis_size("dp") == 2 and lax.axis_size("ctx") == 16


def head():
    return place() ^ (2 * lax.axis_index("dp")) if paired() else place()


def head_cols(h):
    return pl.ds(pl.multiple_of(h * HD, HD), HD)


def nn(a, b):
    return jnp.dot(a, b, preferred_element_type=jnp.float32)


def fetch_kernel(a_ref, b_ref, wk_ref, wq_ref, *refs):
    *outs, weights, sems = refs
    mine = head()
    copies = []
    for k in range(2):
        for side, ref in enumerate((wk_ref, wq_ref)):
            to = slice((2 * k + side) * HD, (2 * k + side + 1) * HD)
            copies.append((ref.at[:, head_cols(mine ^ k)], weights.at[:, to]))
    for k, out in enumerate(outs):
        for side, ref in enumerate((a_ref, b_ref)):
            to = slice(side * HD, (side + 1) * HD)
            copies.append((ref.at[:, head_cols(mine ^ k)], out.at[:, to]))
    started = [pltpu.make_async_copy(*pair, sems.at[i]) for i, pair in enumerate(copies)]
    for copy in started:
        copy.start()
    for copy in started:
        copy.wait()


def project_kernel(near, far, weights, near_kq, far_kq):
    own = weights[:, : 2 * HD]
    near_kq[...] = nn(near[...], own).astype(jnp.bfloat16)
    far_kq[...] = nn(far[...], own).astype(jnp.bfloat16)


class Sides:
    def __init__(self, left, right):
        self.left, self.right = left, right

    def __getitem__(self, where):
        rows, cols = where
        return (self.right if cols.start == HD else self.left)[rows, :]


def project_both_kernel(rows_ref, weights, own_kq, other_k, other_q):
    both = nn(rows_ref[...], weights[...]).astype(jnp.bfloat16)
    own_kq[...] = both[:, : 2 * HD]
    other_k[...] = both[:, 2 * HD : 3 * HD]
    other_q[...] = both[:, 3 * HD :]


def upper():
    return lax.div(place(), 2)


def edge_kernel(own, skip, *refs):
    *sources, big, small = refs
    if len(sources) % 2:
        sources[1:3] = [Sides(*sources[1:3])]
    rows = small.shape[0]
    if big.shape[0] > 2 * rows:
        big[2 * rows :, :] = jnp.zeros((big.shape[0] - 2 * rows, big.shape[1]), big.dtype)
    core = lax.rem(place(), 2)
    keys_big = upper() == (1 if own else 0)
    for pair in range(len(sources) // 2):
        to = slice(pair * HD, (pair + 1) * HD)
        to_big = slice((pair - skip) * HD, (pair - skip + 1) * HD)
        for i, at_core in ((0, core), (1, 1 - core)):
            ref = sources[2 * pair + i]
            at = pl.ds(pl.multiple_of(at_core * rows, rows), rows)

            @pl.when(keys_big)
            def _():
                if pair >= skip:
                    big[at, to_big] = ref[:, :HD]

                @pl.when(at_core == 0)
                def _():
                    small[:, to] = ref[:, HD:]

            @pl.when(jnp.logical_not(keys_big))
            def _():
                if pair >= skip:
                    big[at, to_big] = ref[:, HD:]

                @pl.when(at_core == 1)
                def _():
                    small[:, to] = ref[:, :HD]


def offset_of(row, shift, total):
    return lax.rem(row - shift + 2 * total, total)


def key_place(row, rows, shift, keep_ref, total):
    base = offset_of(row, shift, total)
    nblk = keep_ref.shape[1]
    raw = base + lax.broadcasted_iota(jnp.int32, (rows, HD), 0)
    b0 = base // BLOCK
    kept = jnp.full((rows, HD), keep_ref[0, b0], jnp.int32)
    for more in range(1, rows // BLOCK + 1):
        flag = keep_ref[0, lax.rem(b0 + more, nblk)]
        kept = jnp.where(raw >= (b0 + more) * BLOCK, flag, kept)
    where = jnp.where(raw >= total, raw - total, raw)
    return jnp.where(kept > 0, where, FAR)


def query_place(row, rows, shift, len_ref, total):
    base = offset_of(row, shift, total)
    raw = base + lax.broadcasted_iota(jnp.int32, (1, rows), 1)
    where = jnp.where(raw >= total, raw - total, raw)
    begin = jnp.zeros((1, rows), jnp.int32)
    end = jnp.int32(0)
    for u in range(len_ref.shape[1]):
        length = len_ref[0, u]
        end = end + length
        begin = begin + jnp.where(where >= end, length, 0)
    return where, begin


def after(value, *earlier):
    return lax.optimization_barrier((value, *earlier))[0]


def tile_terms(k, v, q_t, o_t, kpos, qpos, qbegin):
    y = nn(k, q_t) * (0.5 * ALPHA)
    t = jnp.tanh(y)
    u = 1.0 + t
    kpos = jnp.concatenate([kpos] * (q_t.shape[1] // HD), axis=1)
    valid = (kpos >= qbegin) & (kpos <= qpos)
    att = jnp.where(valid, y * u, 0.0).astype(jnp.bfloat16)
    slope = u * (1.0 + y * (1.0 - t))
    ds = jnp.where(valid, nn(v, o_t) * slope, 0.0).astype(jnp.bfloat16)
    return att, ds


def cross_pairs(
    own, len_ref, shift_ref, keep_ref, k_ref, q_ref, v_ref, o_ref, big, small,
    out_t, dq_t, dk, dv,
):
    rows = k_ref.shape[0] // GROUP
    span = GROUP - 1
    total = rows * lax.axis_size("ctx")
    shift = shift_ref[0]
    base = plane_base(rows)

    def shard(j):
        return slice(j * rows, (j + 1) * rows)

    def load(refs, j):
        if len(refs) == 1:
            return refs[0][shard(j), :HD], refs[0][shard(j), HD:]
        return refs[0][shard(j), :], refs[1][shard(j), :]

    def before(ref, first, reached):
        q_ts = [q_ref[shard(j), :].T for j in range(max(reached) + 1)]
        o_ts = [o_ref[shard(j), :].T for j in range(max(reached) + 1)]
        for p in reached:
            k, v = load(ref, p - first)
            k_t, v_t = k.T, v.T
            kpos = key_place(base + (p - span) * rows, rows, shift, keep_ref, total)
            for qt in range(p + 1):
                place_q = query_place(base + qt * rows, rows, shift, len_ref, total)
                att, ds = tile_terms(k, v, q_ts[qt], o_ts[qt], kpos, *place_q)
                out_t[:, shard(qt)] += nn(v_t, att)
                dq_t[:, shard(qt)] += nn(k_t, ds)

    def behind(ref, first, reached):
        for n in reached:
            q, o = load(ref, n - first)
            q_t, o_t = q.T, o.T
            place_q = query_place(base + (GROUP + n) * rows, rows, shift, len_ref, total)
            for kt in range(n + 1, GROUP):
                kpos = key_place(base + kt * rows, rows, shift, keep_ref, total)
                att, ds = tile_terms(
                    k_ref[shard(kt), :], v_ref[shard(kt), :], q_t, o_t, kpos, *place_q
                )
                dv[shard(kt), :] += nn(att, o)
                dk[shard(kt), :] += nn(ds, q)

    keys_big = upper() == (1 if own else 0)

    @pl.when(keys_big)
    def _():
        if big:
            before(big, 1, range(1, span))
        if small:
            behind(small, span - 1, [span - 1])

    @pl.when(jnp.logical_not(keys_big))
    def _():
        if small:
            before(small, 0, [0])
        if big:
            behind(big, 0, range(span - 1))


def square(own_row, shift, total, len_ref, keep_ref, pairs, out_t, dq_t, dk, dv, at):
    rows = pairs[0][0].shape[0]
    q_ts = [q.T for _, q, _, _ in pairs]
    o_ts = [o.T for _, _, _, o in pairs]
    places = [query_place(own_row + i * rows, rows, shift, len_ref, total) for i in (0, 1)]
    for kt, (k, _, v, _) in enumerate(pairs):
        k_t, v_t = k.T, v.T
        kpos = key_place(own_row + kt * rows, rows, shift, keep_ref, total)
        dk_sum, dv_sum = 0.0, 0.0
        for qt in range(kt, 2):
            att, ds = tile_terms(k, v, q_ts[qt], o_ts[qt], kpos, *places[qt])
            if kt == 0:
                out_t[:, at[qt]] = nn(v_t, att)
                dq_t[:, at[qt]] = nn(k_t, ds)
            else:
                out_t[:, at[qt]] += nn(v_t, att)
                dq_t[:, at[qt]] += nn(k_t, ds)
            dv_sum = dv_sum + nn(att, pairs[qt][3])
            dk_sum = dk_sum + nn(ds, pairs[qt][1])
        dk[at[kt], :] = dk_sum
        dv[at[kt], :] = dv_sum


def plane_base(rows):
    return (lax.axis_index("ctx") // GROUP) * (GROUP * rows)


def early_kernel(
    len_ref, shift_ref, keep_ref, a0, a1, b0, b1, out_t, dq_t, dk, dv, kq_ref, vo_ref
):
    rows = a0.shape[0]
    core = lax.rem(place(), 2)
    total = rows * lax.axis_size("ctx")
    for at_core, kq, vo in ((core, a0, b0), (1 - core, a1, b1)):
        at = pl.ds(pl.multiple_of(at_core * rows, rows), rows)
        kq_ref[at, :] = kq[...]
        vo_ref[at, :] = vo[...]
    shards = [slice(0, rows), slice(rows, 2 * rows)]
    pairs = [(kq_ref[i, :HD], kq_ref[i, HD:], vo_ref[i, :HD], vo_ref[i, HD:]) for i in shards]
    own_row = plane_base(rows) + upper() * 2 * rows
    square(
        own_row, shift_ref[0], total, len_ref, keep_ref, pairs, out_t, dq_t, dk, dv, shards
    )


def inner_kernel(
    len_ref, shift_ref, keep_ref, a0, a1, a2, a3_k, a3_q, b0, b1, b2, b3,
    early_out, early_dq, early_dk, early_dv,
    k_ref, q_ref, v_ref, o_ref, out_t, dq_t, dk, dv,
):
    rows = a0.shape[0]
    total = rows * lax.axis_size("ctx")
    shift = shift_ref[0]
    base = plane_base(rows)
    me = place()
    a3 = Sides(a3_k, a3_q)
    for i, (kq, vo) in enumerate(((a0, b0), (a1, b1), (a2, b2), (a3, b3))):
        at = pl.ds(pl.multiple_of((me ^ i) * rows, rows), rows)
        k_ref[at, :] = kq[:, :HD]
        q_ref[at, :] = kq[:, HD:]
        v_ref[at, :] = vo[:, :HD]
        o_ref[at, :] = vo[:, HD:]
    own = pl.ds(pl.multiple_of(upper() * 2 * rows, 2 * rows), 2 * rows)
    out_t[:, own] = early_out[...]
    dq_t[:, own] = early_dq[...]
    dk[own, :] = early_dk[...]
    dv[own, :] = early_dv[...]
    first = (1 - upper()) * 2 * rows
    others = [pl.ds(pl.multiple_of(first + i * rows, rows), rows) for i in (0, 1)]
    pairs = [(k_ref[at, :], q_ref[at, :], v_ref[at, :], o_ref[at, :]) for at in others]
    square(
        base + first, shift, total, len_ref, keep_ref, pairs, out_t, dq_t, dk, dv, others
    )
    shards = [slice(j * rows, (j + 1) * rows) for j in range(GROUP)]
    half = range(GROUP // 2, GROUP)
    places = {j: query_place(base + j * rows, rows, shift, len_ref, total) for j in half}
    q_ts = {j: q_ref[shards[j], :].T for j in half}
    o_ts = {j: o_ref[shards[j], :].T for j in half}
    for kt in range(GROUP // 2):
        at = shards[kt]
        k, v = k_ref[at, :], v_ref[at, :]
        k_t, v_t = k.T, v.T
        kpos = key_place(base + kt * rows, rows, shift, keep_ref, total)
        dk_sum, dv_sum = 0.0, 0.0
        for qt in half:
            qs = shards[qt]
            att, ds = tile_terms(k, v, q_ts[qt], o_ts[qt], kpos, *places[qt])
            out_t[:, qs] += nn(v_t, att)
            dq_t[:, qs] += nn(k_t, ds)
            dv_sum = dv_sum + nn(att, o_ref[qs, :])
            dk_sum = dk_sum + nn(ds, q_ref[qs, :])
        dk[at, :] += dk_sum
        dv[at, :] += dv_sum


def own_halo_kernel(
    len_ref, shift_ref, keep_ref, k_ref, q_ref, v_ref, o_ref, big, small, *refs
):
    cross_pairs(
        True, len_ref, shift_ref, keep_ref, k_ref, q_ref, v_ref, o_ref, (big,), (small,),
        *refs[4:],
    )


def big_halo_kernel(
    len_ref, shift_ref, keep_ref, k_ref, q_ref, v_ref, o_ref, big_kq, big_vo, *refs
):
    rows = k_ref.shape[0] // GROUP
    cross_pairs(
        False, len_ref, shift_ref, keep_ref, k_ref, q_ref, v_ref, o_ref,
        (big_kq.at[: 2 * rows, :], big_vo), (), *refs[4:],
    )


def outer_kernel(
    len_ref, shift_ref, keep_ref, k_ref, q_ref, v_ref, o_ref, small, *refs
):
    out_t, dq_t, dk, dv, s0, s1, s2, s3, dqk = refs[4:]
    cross_pairs(
        False, len_ref, shift_ref, keep_ref, k_ref, q_ref, v_ref, o_ref, (), (small,),
        out_t, dq_t, dk, dv,
    )
    rows = small.shape[0]
    me = place()
    factor = 0.5 * SCALE * ALPHA
    dqk[:HD, :] = (dq_t[...] * factor).astype(jnp.bfloat16)
    for j in range(GROUP):
        dqk[HD:, slice(j * rows, (j + 1) * rows)] = (dk[slice(j * rows, (j + 1) * rows), :] * factor).T.astype(jnp.bfloat16)
    for i, ref in enumerate((s0, s1, s2, s3)):
        at = pl.ds(pl.multiple_of((me ^ i) * rows, rows), rows)
        ref[:, :HD] = (out_t[:, at] * SCALE).T.astype(jnp.bfloat16)
        ref[:, HD:] = (dv[at, :] * SCALE).astype(jnp.bfloat16)


def terms_of(dqk, e0, e1, e2, e3):
    rows = e0.shape[0]
    me = place()
    total = None
    for k, ref in enumerate((e0, e1, e2, e3)):
        at = pl.ds(pl.multiple_of((me ^ k) * rows, rows), rows)
        part = nn(dqk[:, at], ref[...])
        total = part if total is None else total + part
    return total


def terms_kernel(dqk, e0, e1, e2, e3, whole):
    whole[...] = terms_of(dqk, e0, e1, e2, e3)


def half_terms_kernel(same, dqk, e0, e1, e2, e3, out):
    rows = e0.shape[0]
    me = place()
    half = upper() if same else 1 - upper()
    width = out.shape[1]
    high = dqk.shape[0]
    count = out.shape[0] // high
    for z in range(0, count, 2):
        cols = [pl.ds(pl.multiple_of((2 * (z + i) + half) * width, width), width) for i in (0, 1)]
        total = 0.0
        for k, ref in enumerate((e0, e1, e2, e3)):
            at = pl.ds(pl.multiple_of((me ^ k) * rows, rows), rows)
            piece = jnp.concatenate([ref[:, cols[0]], ref[:, cols[1]]], axis=1)
            total = total + nn(dqk[:, at], piece)
        out[z * high : (z + 1) * high, :] = total[:, :width].astype(out.dtype)
        out[(z + 1) * high : (z + 2) * high, :] = total[:, width:].astype(out.dtype)


def pair_sum_kernel(mine, other, *outs):
    planes = lax.axis_size("ctx") // GROUP
    z = lax.axis_index("ctx") // GROUP
    high = outs[0].shape[0]
    for dz, ref in enumerate(outs):
        at = pl.ds(pl.multiple_of(lax.rem(z + dz, planes) * high, high), high)
        ref[...] = (mine[at, :] + other[at, :].astype(jnp.float32)).astype(ref.dtype)


def sum_kernel(*refs):
    ins, (near, far, hold) = refs[:-3], refs[-3:]
    total = ins[0][...].astype(jnp.float32)
    for ref in ins[1:]:
        total = total + ref[...].astype(jnp.float32)
    hold[...] = total.T
    share = near.shape[0]
    core = lax.rem(lax.axis_index("ctx"), 2)
    near[...] = hold[pl.ds(pl.multiple_of(core * share, share), share), :].astype(jnp.bfloat16)
    far[...] = hold[pl.ds(pl.multiple_of((1 - core) * share, share), share), :].astype(jnp.bfloat16)


def join_kernel(own, other, out):
    core = lax.rem(place(), 2)
    width = own.shape[1]
    out[:, pl.ds(pl.multiple_of(core * width, width), width)] = own[...]
    out[:, pl.ds(pl.multiple_of((1 - core) * width, width), width)] = other[...]


def finish_kernel(own, other, gq, gk):
    first = upper() ^ lax.axis_index("dp")
    for pair, ref in ((first, own), (1 - first, other)):
        for core in range(2):
            cols = head_cols(2 * pair + core)
            gq[:, cols] = ref[:, 2 * core * HD : (2 * core + 1) * HD]
            gk[:, cols] = ref[:, (2 * core + 1) * HD : (2 * core + 2) * HD]


def merge_kernel(i0, i1, i2, i3, first, second):
    mine = head()
    for k, ref in enumerate((i0, i1, i2, i3)):
        cols = head_cols(mine ^ k)
        first[:, cols] = ref[:, :HD]
        second[:, cols] = ref[:, HD:]


def direct_reduce(dqk, gathered, share):
    count = lax.axis_size("ctx")
    planes = count // GROUP
    width = gathered[0].shape[1]
    block = width // (2 * planes)
    shape = (2 * HD * planes, block)
    args = (dqk, *gathered)
    (give,) = call(functools.partial(half_terms_kernel, False), [like(*shape)], args, busy=1)
    (keep,) = call(
        functools.partial(half_terms_kernel, True), [like(*shape, jnp.float32)], args, busy=1
    )
    across = [(y * count + i, (1 - y) * count + (i ^ 2)) for y in range(2) for i in range(count)]
    got = lax.ppermute(give, ("dp", "ctx"), across)
    sends = call(
        pair_sum_kernel,
        [like(2 * HD, block, jnp.float32)] + [like(2 * HD, block)] * (planes - 1),
        (keep, got),
    )
    arrived = [sends[0]] + [around(sends[dz], dz, dz) for dz in range(1, planes)]
    near, far = call(
        sum_kernel,
        [like(share, 2 * HD)] * 2,
        arrived,
        scratch=[pltpu.VMEM((block, 2 * HD), jnp.float32)],
    )
    (both,) = call(join_kernel, [like(share, 4 * HD)], (near, partner(far, 1)), busy=0.1)
    other = lax.ppermute(both, "dp", [(0, 1), (1, 0)])
    return got, call(finish_kernel, [like(share, GROUP * HD)] * 2, (both, other))


def general_reduce(dqk, gathered, share):
    count = lax.axis_size("ctx")
    planes = count // GROUP
    width = gathered[0].shape[1]
    (whole,) = call(
        terms_kernel, [like(2 * HD, width, jnp.float32)], (dqk, *gathered), busy=2
    )
    whole = lax.psum(whole.T, "dp")
    same_head = [[g * GROUP + j for g in range(planes)] for j in range(GROUP)]
    plane = [[g * GROUP + j for j in range(GROUP)] for g in range(planes)]
    part = lax.psum_scatter(
        whole, "ctx", scatter_dimension=0, axis_index_groups=same_head, tiled=True
    ).astype(jnp.bfloat16)
    part = lax.all_to_all(
        part.reshape(GROUP, share, 2 * HD), "ctx", 0, 0, axis_index_groups=plane, tiled=True
    )
    part = jnp.moveaxis(part.reshape(GROUP, share, 2, HD), 0, 2)
    grads = part[:, 0].reshape(share, GROUP * HD), part[:, 1].reshape(share, GROUP * HD)
    return dqk, grads


def body(events, w_query, w_key, values, grad_out, lengths, stream_shift, block_keep):
    rows, width = events.shape[1:]
    features = w_query.shape[1]
    count = lax.axis_size("ctx")
    local = events[0]
    all_rows = GROUP * rows
    pair = like(rows, 2 * HD)
    full = like(all_rows, HD)

    e1 = partner(local, 1)
    e2 = partner(local, 2)
    vo0, vo1, vo2, vo3, weights = call(
        fetch_kernel,
        [pair] * GROUP + [like(width, 4 * HD)],
        [
            pltpu.with_memory_space_constraint(a, pltpu.HBM)
            for a in (values[0], grad_out[0], w_key, w_query)
        ],
        specs=[HBM] * 4,
        busy=0.1,
        scratch=[pltpu.SemaphoreType.DMA((12,))],
    )
    vo1 = partner(vo1, 1)
    info = (lengths, stream_shift, block_keep)
    wide, tall = like(HD, all_rows, jnp.float32), like(all_rows, HD, jnp.float32)
    sums = [wide, wide, tall, tall]
    wide, tall = like(HD, 2 * rows, jnp.float32), like(2 * rows, HD, jnp.float32)
    kq0, kq1 = call(project_kernel, [pair] * 2, (local, e1, weights), busy=1)
    big, small = call(
        functools.partial(edge_kernel, True, 0),
        [like(2 * rows, 2 * HD), pair],
        (kq0, kq1, vo0, vo1),
        busy=0.1,
    )
    own = around(big, -1, 1), around(small, 1, -1)
    early = call(
        early_kernel,
        [wide, wide, tall, tall],
        (*info, after(kq0, small), kq1, vo0, vo1),
        specs=[SMEM] * 3 + [VMEM] * 4,
        busy=0.1,
        scratch=[pltpu.VMEM((2 * rows, 2 * HD), jnp.bfloat16)] * 2,
    )
    vo2, vo3 = partner(after(vo2, *early), 2), partner(after(vo3, *early), 3)
    half = like(rows, HD)
    kq2, *give = call(project_both_kernel, [pair, half, half], (after(e2, own[1], *early), weights), busy=1)
    k3, q3 = partner(give[0], 1), partner(give[1], 1)
    big_kq, _ = call(
        functools.partial(edge_kernel, False, 0),
        [like(2 * rows, HD), like(rows, HD)],
        (kq2, k3, q3),
        busy=0.1,
    )
    big_vo, small = call(
        functools.partial(edge_kernel, False, 1),
        [like(2 * rows, HD), pair],
        (kq2, k3, q3, after(vo2, own[0], big_kq), vo3),
        busy=2,
    )
    big_kq = around(big_kq, 1, -1)
    k3 = after(k3, big_vo)
    own0 = after(own[0], big_kq)
    other = big_kq, around(big_vo, 1, -1), around(small, -1, 1)
    k, q, v, o, *held = call(
        inner_kernel,
        [full] * 4 + sums,
        (*info, kq0, kq1, kq2, k3, q3, vo0, vo1, vo2, vo3, *early),
        specs=[SMEM] * 3 + [VMEM] * 13,
        busy=3,
    )
    held = call(
        own_halo_kernel,
        sums,
        (*info, k, q, v, o, own0, own[1], *held),
        specs=[SMEM] * 3 + [VMEM] * 10,
        aliases={9: 0, 10: 1, 11: 2, 12: 3},
        busy=5,
    )
    held = call(
        big_halo_kernel,
        sums,
        (*info, k, q, v, o, *other[:2], *held),
        specs=[SMEM] * 3 + [VMEM] * 10,
        aliases={9: 0, 10: 1, 11: 2, 12: 3},
        busy=4,
    )
    *_, p0, p1, p2, p3, dqk = call(
        outer_kernel,
        sums + [pair] * GROUP + [like(2 * HD, all_rows)],
        (*info, k, q, v, o, other[2], *held),
        specs=[SMEM] * 3 + [VMEM] * 9,
        aliases={8: 0, 9: 1, 10: 2, 11: 3},
        busy=2,
    )
    e3 = partner(after(e2, kq2), 1)
    share = width // count
    reduce = direct_reduce if paired() else general_reduce
    reached, (grad_wq, grad_wk) = reduce(dqk, (local, e1, e2, e3), share)
    parts = [partner(after(p, reached), k) for k, p in ((1, p1), (2, p2), (3, p3))]
    attended, grad_values = call(merge_kernel, [like(rows, features)] * 2, (p0, *parts))
    return (attended[None], grad_values[None], grad_wq, grad_wk)


def solution(mesh):
    placed = (
        P("dp", "ctx", None),
        P(),
        P(),
        P("dp", "ctx", None),
        P("dp", "ctx", None),
        P("dp", None),
        P("dp"),
        P("dp", None),
    )
    return jax.shard_map(
        body,
        mesh=mesh,
        in_specs=placed,
        out_specs=(P("dp", "ctx", None), P("dp", "ctx", None), P("ctx", None), P("ctx", None)),
        check_vma=False,
    )
```
